128 devices in a mesh: dp: 32 (over x_lo, y, z), tensor: 4 (over x_hi, core).
Axes of the slice: x: 4 (x_hi: 2, x_lo: 2; x = x_hi * 2 + x_lo), y: 4, z: 4, core: 2. Of those that a mesh axis runs over, the one named last changes fastest.
Arguments:
- layer_input: bfloat16 [16384, 2048], P(('dp', 'tensor')), may hold values from -6 to 6
- cotangent: bfloat16 [16384, 2048], P(('dp', 'tensor')), may hold values from -6 to 6
- lengths: int32 [32], P('dp'), may hold values from 385 to 512
- expert_ids: int32 [16384, 8], P('dp'), may hold values from 0 to 9, all different within a row; in each aligned block of 512 rows (0 to 511, 512 to 1023, ...) at most 448 rows name the same one
- gains: bfloat16 [4, 2048], P(None, ('dp', 'tensor')), may hold values from 0.5 to 1.5
- w_qkv: bfloat16 [3, 2048, 2048], P(None, 'dp', 'tensor'), may hold values from -0.125 to 0.125
- w_out: bfloat16 [2048, 2048], P('tensor', 'dp'), may hold values from -1.75 to 1.75
- w_router: bfloat16 [2048, 10], P(('dp', 'tensor')), may hold values from -0.0625 to 0.0625
- w_gate_up: bfloat16 [10, 2, 2048, 1024], P(None, None, 'dp', 'tensor'), may hold values from -0.125 to 0.125
- w_down: bfloat16 [10, 1024, 2048], P(None, 'tensor', 'dp'), may hold values from -0.75 to 0.75
Outputs:
- output: bfloat16 [16384, 2048], P(('dp', 'tensor'))
- input_grad: float32 [16384, 2048], P(('dp', 'tensor'))
- gains_grad: float32 [4, 2048], P(None, ('dp', 'tensor'))
- qkv_grad: float32 [3, 2048, 2048], P(None, 'dp', 'tensor')
- out_grad: float32 [2048, 2048], P('tensor', 'dp')
- router_grad: float32 [2048, 10], P(('dp', 'tensor'))
- gate_up_grad: float32 [10, 2, 2048, 1024], P(None, None, 'dp', 'tensor')
- down_grad: float32 [10, 1024, 2048], P(None, 'tensor', 'dp')
The draws below stay inside these ranges and needn't reach their ends.
Inputs may be any that keep to these rules, and one draw needn't show every extreme that they name: `expert_ids`: within the 512 rows of one sequence no expert is named by more than 448 rows, a bound that some block reaches.
All inputs are finite; a program needn't handle non-finite values.
Results may differ from the reference program's by a relative error of at most 0.03.
Values may be sent and summed in bfloat16 or wider, within the bound.
A program may use at most 320 MiB of HBM per device.

```python
import math
import jax
import jax.numpy as jnp
import numpy as np
from jax import lax

D = 2048
HEADS = 16
HD = 128
FF = 1024
TOPK = 8
E = 10
SEQ = 512
SLOTS = 32
TOKENS = 16384
CAP = 448


def with_ends(drawn, key, smallest, high):
    spot = [jax.random.randint(jax.random.fold_in(key, axis), (), 0, length) for axis, length in enumerate(drawn.shape)]
    widest = drawn.shape.index(max(drawn.shape))
    next_to = spot[:widest] + [(spot[widest] + 1) % drawn.shape[widest]] + spot[widest + 1:]
    return drawn.at[tuple(spot)].set(smallest).at[tuple(next_to)].set(high)


def shard_levels(own_key, shape, cuts, least, high):
    loudness, own = 1.0, jax.random.fold_in(own_key, 6)
    for axis_at, blocks in cuts:
        steps = jnp.exp(jax.random.uniform(jax.random.fold_in(own, axis_at), (blocks,), jnp.float32, least / len(cuts), high / len(cuts)))
        loudness = loudness * jnp.repeat(steps, shape[axis_at] // blocks).reshape([-1 if axis == axis_at else 1 for axis in range(len(shape))])
    return loudness


def deal_out(key, own, number, rows, amount, top, reach, slope):
    ranking = jax.random.permutation(key, amount)
    crowded, usual = load_shares(amount, rows * top, reach, slope, True), load_shares(amount, rows * top, reach, slope, False)
    places = jnp.arange(amount)

    def named(sizes, offset_by):
        used = int((sizes > 0).sum())
        fixed = max(1, used // 4)
        passed = fixed + (places - fixed + offset_by * (used - fixed)) % max(1, amount - fixed)
        return jnp.zeros((amount,), jnp.int32).at[ranking[jnp.where(places < fixed, places, passed)]].set(jnp.asarray(sizes, jnp.int32))

    sizes = jnp.where(number % 4 == 0, named(crowded, number // 4), named(usual, number - number // 4 - 1))
    mixed = jax.random.permutation(jax.random.fold_in(own, 3), amount)
    giver, receiver = mixed[0:amount // 2 * 2:2], mixed[1:amount // 2 * 2:2]
    room = jnp.minimum(sizes[giver] - 1, reach - sizes[receiver]) // 2
    room = jnp.where((giver == ranking[0]) | (receiver == ranking[0]) | (sizes[receiver] == 0), 0, jnp.maximum(room, 0))
    passed = jax.random.randint(jax.random.fold_in(own, 4), (amount // 2,), 0, 1 << 20) % (room + 1)
    sizes = sizes.at[giver].add(-passed).at[receiver].add(passed)
    members = jnp.searchsorted(jnp.cumsum(sizes), jnp.arange(rows * top), side="right").astype(jnp.int32)
    grid = members.reshape(top, rows).T
    grid = grid[jax.random.permutation(jax.random.fold_in(own, 1), rows)]
    offset_by = jax.random.randint(jax.random.fold_in(own, 2), (rows, 1), 0, top)
    return jnp.take_along_axis(grid, (jnp.arange(top)[None, :] + offset_by) % top, axis=1)


def load_shares(count, total, limit, skew, full):
    portions = [(1 << 20) // math.isqrt(rank ** skew) + 1 for rank in range(1, count + 1)]
    largest = limit if full else min(limit, max(-(-total // count), total * portions[0] // sum(portions)))
    least = 1 if total - largest >= count - 1 else 0
    counts, spare = [largest] + [least] * (count - 1), total - largest - least * (count - 1)
    while spare > 0:
        movable = [i for i in range(1, count) if counts[i] < largest] or [i for i in range(1, count) if counts[i] < limit]
        pool, left = sum([portions[i] for i in movable]), spare
        for i in movable:
            extra = min(limit - counts[i], max(1, left * portions[i] // pool), spare)
            counts[i] = counts[i] + extra
            spare = spare - extra
    return np.array(counts)


def bell_draw(stream_key, dims, scale, limit, cuts=(), held_as=jnp.bfloat16):
    entries = scale * jax.random.normal(stream_key, dims, jnp.float32)
    if cuts:
        entries = entries * shard_levels(stream_key, dims, cuts, -0.22, 0.18)
    return jnp.clip(entries, -limit, limit).astype(held_as)


def setup_inputs(seed: int = 0) -> dict:
    seeds = jax.random.split(jax.random.key(seed), 11)
    layer_input = bell_draw(seeds[0], (TOKENS, D), 1.0, 6.0, ((0, 128),))
    cotangent = bell_draw(seeds[1], (TOKENS, D), 1.0, 6.0, ((0, 128),))
    lengths = with_ends(jax.random.randint(seeds[2], (SLOTS,), SEQ - SEQ // 4 + 1, SEQ + 1), jax.random.fold_in(seeds[2], 1), SEQ - SEQ // 4 + 1, SEQ).astype(jnp.int32)
    expert_ids_keys = jax.random.split(jax.random.fold_in(seeds[3], 1), TOKENS // SEQ)
    expert_ids_turns = jax.random.permutation(jax.random.fold_in(seeds[3], 3), TOKENS // SEQ)
    expert_ids = jax.vmap(lambda own, number: deal_out(jax.random.fold_in(seeds[3], 2), own, number, SEQ, E, TOPK, CAP, 1))(expert_ids_keys, expert_ids_turns).reshape((TOKENS, TOPK))
    gains = jnp.clip(1.0 + 0.1 * jax.random.normal(seeds[4], (4, D), jnp.float32), 0.5, 1.5).astype(jnp.bfloat16)
    w_qkv = bell_draw(seeds[5], (3, D, D), D ** -0.5, 0.125, ((1, 32), (2, 4)))
    w_out = bell_draw(seeds[6], (D, D), (D * 3 // SEQ) ** -0.5, 1.75, ((0, 4), (1, 32)))
    w_router = bell_draw(seeds[7], (D, E), (4 * D) ** -0.5, 0.0625, ((0, 128),))
    w_gate_up = bell_draw(seeds[8], (E, 2, D, FF), D ** -0.5, 0.125, ((2, 32), (3, 4)))
    w_down = bell_draw(seeds[9], (E, FF, D), (FF // 16) ** -0.5, 0.75, ((1, 4), (2, 32)))
    return {"layer_input": layer_input, "cotangent": cotangent, "lengths": lengths, "expert_ids": expert_ids, "gains": gains, "w_qkv": w_qkv, "w_out": w_out, "w_router": w_router, "w_gate_up": w_gate_up, "w_down": w_down}


@jax.custom_vjp
def low(v):
    return lax.optimization_barrier(v.astype(jnp.bfloat16)).astype(jnp.float32)

@jax.custom_vjp
def low_back(v):
    return v

def low_keep(v):
    return (low(v), None)

def low_pass(kept, grad):
    return (grad,)

def back_keep(v):
    return (v, None)

def back_low(kept, grad):
    return (low(grad),)
low.defvjp(low_keep, low_pass)
low_back.defvjp(back_keep, back_low)
epsilon = 1e-06
theta = 10000.0
precise = lax.Precision.HIGHEST

def rms_scale(value, gain):
    return value * lax.rsqrt(lax.optimization_barrier(jnp.mean(value * value, axis=-1, keepdims=True)) + epsilon) * gain

def rotary(length_all, head_dim):
    half_dim = head_dim // 2
    freqs = theta ** (-(jnp.arange(half_dim, dtype=jnp.float32) * 2.0 / head_dim))
    angles = jnp.arange(length_all, dtype=jnp.float32)[:, None] * freqs[None, :]
    return (jnp.cos(angles), jnp.sin(angles))

def head_post(projected, gain, cos_table, sin_table, factor):
    row_count = projected.shape[0]
    head_count = gain.shape[0] // HD
    shaped = projected.reshape(row_count, head_count, HD)
    normed = rms_scale(shaped, gain.reshape(head_count, HD))
    first = normed[..., :HD // 2]
    second = normed[..., HD // 2:]
    cos_part = cos_table[:, None, :]
    sin_part = sin_table[:, None, :]
    turned = jnp.concatenate([first * cos_part - second * sin_part, second * cos_part + first * sin_part], axis=-1)
    return (turned * factor).reshape(row_count, head_count * HD)

def route_tables(expert_ids, length, capacity):
    seq_len = expert_ids.shape[0]
    flat_ids = expert_ids.reshape(-1)
    route_index = jnp.arange(seq_len * TOPK, dtype=jnp.int32)
    token_index = route_index // TOPK
    live_route = token_index < length
    matches = ((flat_ids[:, None] == jnp.arange(E, dtype=jnp.int32)[None, :]) & live_route[:, None]).astype(jnp.int32)
    before = jnp.cumsum(matches, axis=0) - matches
    place = lax.optimization_barrier(jnp.sum(before * matches, axis=1))
    target = jnp.where(live_route, flat_ids * capacity + place, E * capacity)
    slot_token = jnp.zeros((E * capacity,), jnp.int32).at[target].set(token_index, mode='drop')
    slot_route = jnp.full((E * capacity,), seq_len * TOPK, jnp.int32).at[target].set(route_index, mode='drop')
    return (slot_token.reshape(E, capacity), slot_route.reshape(E, capacity))

def layer(input_rows, gains, w_qkv, w_out, w_router, w_gate_up, w_down, length, expert_ids):
    seq_len = input_rows.shape[0]
    live = (jnp.arange(seq_len, dtype=jnp.int32) < length).astype(jnp.float32)
    cos_table, sin_table = rotary(seq_len, HD)
    normed_in = low(rms_scale(input_rows, gains[0]))
    project = jnp.einsum('sd,cdf->csf', normed_in, w_qkv, precision=precise)
    queries = low(head_post(low_back(project[0]), gains[2], cos_table, sin_table, HD ** (-0.5)))
    keys = low(head_post(low_back(project[1]), gains[3], cos_table, sin_table, 1.0))
    values = low(low_back(project[2]))
    query_heads = queries.reshape(seq_len, HEADS, HD)
    key_heads = keys.reshape(seq_len, HEADS, HD)
    value_heads = values.reshape(seq_len, HEADS, HD)
    scores = low_back(jnp.einsum('qhd,khd->hqk', query_heads, key_heads, precision=precise))
    highest = lax.optimization_barrier(jnp.max(scores, axis=-1, keepdims=True))
    weights = jnp.exp(scores - highest) * live[None, None, :]
    probs = weights / lax.optimization_barrier(jnp.sum(weights, axis=-1, keepdims=True))
    attended = low_back(low(jnp.einsum('hqk,khd->qhd', low(probs), value_heads, precision=precise))).reshape(seq_len, D)
    branch = low_back(jnp.dot(attended, w_out, precision=precise))
    state = input_rows + branch
    normed_mid = low(rms_scale(state, gains[1]))
    logits = jnp.dot(normed_mid, w_router, precision=precise)
    chosen = jnp.take_along_axis(logits, expert_ids, axis=1)
    gates = jax.nn.softmax(chosen, axis=-1) * live[:, None]
    slot_token, slot_route = route_tables(expert_ids, length, CAP)
    gate_pad = jnp.concatenate([gates.reshape(-1), jnp.zeros((1,), jnp.float32)])
    slot_gate = gate_pad[slot_route]

    def expert_block(pieces):
        gate_up, down, tokens = pieces
        rows_in = normed_mid[tokens]
        pre = jnp.einsum('cd,gdf->gcf', rows_in, gate_up, precision=precise)
        gate_part = low_back(pre[0])
        up_part = low_back(pre[1])
        inner = low(jax.nn.silu(gate_part) * up_part)
        return low_back(jnp.dot(inner, down, precision=precise))
    produced = lax.map(jax.checkpoint(expert_block), (w_gate_up, w_down, slot_token))
    mixed = jnp.zeros_like(input_rows).at[slot_token.reshape(-1)].add((slot_gate[..., None] * produced).reshape(-1, D))
    return state + mixed

def reference(layer_input, cotangent, lengths, expert_ids, gains, w_qkv, w_out, w_router, w_gate_up, w_down):
    params = tuple((param.astype(jnp.float32) for param in (gains, w_qkv, w_out, w_router, w_gate_up, w_down)))
    input_slots = layer_input.astype(jnp.float32).reshape(SLOTS, SEQ, D)
    cot_slots = cotangent.astype(jnp.float32).reshape(SLOTS, SEQ, D)
    id_slots = expert_ids.reshape(SLOTS, SEQ, TOPK)

    def per_slot(totals, pieces):
        input_rows, cot_rows, length, slot_ids = pieces

        def forward(rows_in, gain_in, qkv_in, out_in, router_in, gate_up_in, down_in):
            return layer(rows_in, gain_in, qkv_in, out_in, router_in, gate_up_in, down_in, length, slot_ids)
        result, pullback = jax.vjp(forward, input_rows, *params)
        grads = pullback(cot_rows)
        totals = tuple((total + grad_part for total, grad_part in zip(totals, grads[1:])))
        return (totals, (result.astype(jnp.bfloat16), grads[0]))
    zeros_init = tuple((jnp.zeros_like(param) for param in params))
    totals, (outputs, input_grads) = lax.scan(per_slot, zeros_init, (input_slots, cot_slots, lengths, id_slots))
    return (outputs.reshape(TOKENS, D), input_grads.reshape(TOKENS, D), totals[0], totals[1], totals[2], totals[3], totals[4], totals[5])
```

```python
import itertools

import jax
import jax.numpy as jnp
from jax import lax
from jax.sharding import Mesh
from jax.sharding import PartitionSpec as P

HD = 128
TOPK = 8
E = 10
D = 2048
SEQ = 512
BLK = 128
HALF_E = 5
FFS = 256
AXES = ("xl", "y", "z", "xh", "c")
SIZES = (2, 4, 4, 2, 2)
DP = ("xl", "y", "z")
DP_TENSOR = ("xl", "y", "z", "xh", "c")
epsilon = 1e-06
theta = 10000.0
precise = lax.Precision.HIGHEST
F32 = jnp.float32
BF16 = jnp.bfloat16


def shift(v, dx=0, dy=0, dz=0, dc=0):
    perm = []
    for xl, y, z, xh, c in itertools.product(*map(range, SIZES)):
        x = (xh * 2 + xl + dx) % 4
        to = (x % 2, (y + dy) % 4, (z + dz) % 4, x // 2, (c + dc) % 2)
        flat = lambda k: (((k[0] * 4 + k[1]) * 4 + k[2]) * 2 + k[3]) * 2 + k[4]
        perm.append((flat((xl, y, z, xh, c)), flat(to)))
    return lax.ppermute(v, AXES, perm)


def partner(v):
    perm = []
    for xl, y, z, xh, c in itertools.product(*map(range, SIZES)):
        flat = lambda k: (((k[0] * 4 + k[1]) * 4 + k[2]) * 2 + k[3]) * 2 + k[4]
        perm.append((flat((xl, y, z, xh, c)), flat((1 - xl, y, z, xh, c))))
    return lax.ppermute(v, AXES, perm)


def tied(value, *others):
    return lax.optimization_barrier((value, *others))[0]


def at(v, index, dim):
    return lax.dynamic_index_in_dim(v, index, dim, keepdims=False)


def ring_gather(v, axis, index, dim):
    shape = v.shape[:dim] + (4,) + v.shape[dim:]
    out = jnp.zeros(shape, v.dtype)
    out = lax.dynamic_update_index_in_dim(out, v, index, dim)
    for k in (1, 3, 2):
        got = shift(v, **{"d" + axis: k})
        out = lax.dynamic_update_index_in_dim(out, got, (index + 4 - k) % 4, dim)
    return out


def weight_gather(own, other, pos):
    own_a = ring_gather(own, "y", pos["y"], 0)
    other_a = ring_gather(other, "z", pos["z"], 0)
    return own_a, other_a


def weight_gather_end(own_a, other_a, pos):
    own_b = ring_gather(own_a, "z", pos["z"], 1)
    other_b = ring_gather(other_a, "y", pos["y"], 0)
    out = jnp.zeros((2,) + own_b.shape, own_b.dtype)
    out = lax.dynamic_update_index_in_dim(out, own_b, pos["xl"], 0)
    out = lax.dynamic_update_index_in_dim(out, other_b, 1 - pos["xl"], 0)
    return out.reshape(D, own_b.shape[-1])


def ring_scatter(v, axis, index, dim):
    total = at(v, index, dim).astype(F32)
    for k in (1, 3, 2):
        got = shift(at(v, (index + k) % 4, dim), **{"d" + axis: k})
        total = total + got.astype(F32)
    return total


def weight_scatter(grad, pos):
    parts = grad.reshape(2, 4, 4, 64, grad.shape[-1])
    own = at(parts, pos["xl"], 0)
    other = at(parts, 1 - pos["xl"], 0)
    own_a = ring_scatter(own, "z", pos["z"], 1).astype(BF16)
    other_a = ring_scatter(other, "y", pos["y"], 0).astype(BF16)
    own_b = ring_scatter(own_a, "y", pos["y"], 0)
    other_b = ring_scatter(other_a, "z", pos["z"], 0)
    return own_b, partner(other_b.astype(BF16)).astype(F32)


def token_gather(v, pos):
    mine = jnp.zeros((2, 2, 2) + v.shape, v.dtype)
    half = jnp.zeros((2, 2) + v.shape, v.dtype)
    zero = (0,) * v.ndim

    def put(buffer, block, dx):
        x = (pos["x"] + 4 - dx) % 4
        return lax.dynamic_update_slice(buffer, block[None, None], (x % 2, x // 2) + zero)

    half = put(half, v, 0)
    for k in (1, 3, 2):
        half = put(half, shift(v, dx=k), k)
    there = shift(half, dc=1)
    mine = lax.dynamic_update_index_in_dim(mine, half, pos["c"], 2)
    mine = lax.dynamic_update_index_in_dim(mine, there, 1 - pos["c"], 2)
    return mine.reshape(8 * v.shape[0], v.shape[1])


def token_scatter(v, pos, wire):
    parts = v.reshape(2, 2, 2, BLK, v.shape[1])
    got = shift(at(parts, 1 - pos["c"], 2).astype(wire), dc=1)
    half = (at(parts, pos["c"], 2).astype(F32) + got.astype(F32)).astype(wire)

    def pick(dx):
        x = (pos["x"] + dx) % 4
        return lax.dynamic_slice(half, (x % 2, x // 2, 0, 0), (1, 1, BLK, v.shape[1]))[0, 0]

    total = pick(0).astype(F32)
    for k in (1, 3, 2):
        total = total + shift(pick(k), dx=k).astype(F32)
    return total


def rms_scale(value, gain):
    return value * lax.rsqrt(jnp.mean(value * value, axis=-1, keepdims=True) + epsilon) * gain


def rotary(length_all, head_dim):
    half_dim = head_dim // 2
    freqs = theta ** (-(jnp.arange(half_dim, dtype=F32) * 2.0 / head_dim))
    angles = jnp.arange(length_all, dtype=F32)[:, None] * freqs[None, :]
    return (jnp.cos(angles), jnp.sin(angles))


def head_post(projected, gain, cos_table, sin_table, factor):
    normed = rms_scale(projected, gain)
    first = normed[..., : HD // 2]
    second = normed[..., HD // 2 :]
    cos_part = cos_table[None, :, None, :]
    sin_part = sin_table[None, :, None, :]
    turned = jnp.concatenate(
        [first * cos_part - second * sin_part, second * cos_part + first * sin_part], axis=-1
    )
    return turned * factor


def local(
    layer_input, cotangent, lengths, expert_ids, gains, w_qkv, w_out, w_router, w_gate_up, w_down
):
    pos = {a: lax.axis_index(a) for a in AXES}
    pos["x"] = pos["xh"] * 2 + pos["xl"]
    xl = pos["xl"]
    t = pos["xh"] * 2 + pos["c"]

    small = jnp.concatenate([gains.T, w_router], axis=1)
    small = jnp.pad(small, ((0, 0), (0, 128 - small.shape[1])))
    tiny = jnp.zeros((2, 2, 16, 128), BF16)
    tiny = lax.dynamic_update_slice(tiny, small[None, None], (pos["xh"], pos["c"], 0, 0))
    for dx, dc in ((0, 1), (2, 0), (2, 1)):
        got = shift(small, dx=dx, dc=dc)
        h = (pos["xh"] + dx // 2) % 2
        c = (pos["c"] + dc) % 2
        tiny = lax.dynamic_update_slice(tiny, got[None, None], (h, c, 0, 0))
    small = tiny.reshape(64, 128)
    out_rows = w_out.reshape(2, 256, 64).transpose(0, 2, 1)
    qkv_rows = w_qkv.reshape(3, 64, 2, 256).transpose(2, 1, 0, 3).reshape(2, 64, 768)
    att = jnp.concatenate([qkv_rows, out_rows], axis=2)
    att_own = jnp.concatenate([at(att, xl, 0), small], axis=1)
    att_give = jnp.concatenate([at(att, 1 - xl, 0), small], axis=1)
    att_other = partner(att_give)
    in_all = token_gather(layer_input, pos)
    att_a = weight_gather(att_own, att_other, pos)

    exp_rows = jnp.concatenate(
        [
            w_gate_up.reshape(2, HALF_E, 2, 64, FFS).transpose(0, 3, 1, 2, 4).reshape(2, 64, 2560),
            w_down.reshape(2, HALF_E, FFS, 64).transpose(0, 3, 1, 2).reshape(2, 64, 1280),
        ],
        axis=2,
    )
    exp_rows = tied(exp_rows, *att_a)
    att_full = weight_gather_end(*att_a, pos)
    exp_other = partner(at(exp_rows, 1 - xl, 0))
    exp_a = weight_gather(at(exp_rows, xl, 0), exp_other, pos)
    exp_a = lax.optimization_barrier((*exp_a, att_full))[:2]
    exp_full = weight_gather_end(*exp_a, pos)
    ids_other = partner(expert_ids)
    length_other = partner(jnp.broadcast_to(lengths, (8, 128)))[0, 0]
    cot_all = token_gather(tied(cotangent, in_all), pos)

    first = xl == 0
    length_both = jnp.stack(
        [jnp.where(first, lengths[0], length_other), jnp.where(first, length_other, lengths[0])]
    )
    ids_both = jnp.concatenate(
        [jnp.where(first, expert_ids, ids_other), jnp.where(first, ids_other, expert_ids)]
    )
    live = (jnp.arange(SEQ, dtype=jnp.int32)[None, :] < length_both[:, None]).astype(F32)

    w_qkv_all = att_full[:, :768]
    w_out_all = att_full[:, 768:1024]
    gain_f = att_full[:, 1024:1028].T.astype(F32)
    router = att_full[:, 1028:1038]
    head_start = t * 512 + xl * 256
    q_gain = lax.dynamic_slice_in_dim(gain_f[2], head_start, 256).reshape(2, HD)
    k_gain = lax.dynamic_slice_in_dim(gain_f[3], head_start, 256).reshape(2, HD)
    cos_table, sin_table = rotary(SEQ, HD)

    def post_query(projected, gain):
        return head_post(projected, gain, cos_table, sin_table, HD ** (-0.5))

    def post_key(projected, gain):
        return head_post(projected, gain, cos_table, sin_table, 1.0)

    in_float = in_all.astype(F32)
    in_scale = lax.rsqrt(jnp.mean(in_float * in_float, axis=-1, keepdims=True) + epsilon)
    normed_in = (in_float * in_scale * gain_f[0]).astype(BF16)
    project = jnp.dot(normed_in, w_qkv_all, preferred_element_type=F32)
    project = project.reshape(2, SEQ, 3, 2, HD)
    queries = post_query(project[:, :, 0], q_gain).astype(BF16)
    keys = post_key(project[:, :, 1], k_gain).astype(BF16)
    values = project[:, :, 2].astype(BF16)
    scores = jnp.einsum("sqhd,skhd->shqk", queries, keys, preferred_element_type=F32)
    highest = jnp.max(scores, axis=-1, keepdims=True)
    weights = jnp.exp(scores - highest) * live[:, None, None, :]
    probs = weights / jnp.sum(weights, axis=-1, keepdims=True)
    probs_low = probs.astype(BF16)
    attended = jnp.einsum("shqk,skhd->sqhd", probs_low, values, preferred_element_type=F32)
    attended = attended.astype(BF16).reshape(2 * SEQ, 256)
    branch = jnp.einsum("sf,df->sd", attended, w_out_all, preferred_element_type=F32)
    branch = token_scatter(branch, pos, BF16)
    input_float = layer_input.astype(F32)
    state = input_float + branch
    normed_mid = rms_scale(state, gain_f[1]).astype(BF16)
    mid_all = token_gather(normed_mid, pos)

    logits = jnp.dot(mid_all, router, preferred_element_type=F32)
    named = jnp.any(
        ids_both[:, :, None] == jnp.arange(E, dtype=jnp.int32)[None, None, :], axis=1
    )
    peak = jnp.max(jnp.where(named, logits, -jnp.inf), axis=-1, keepdims=True)
    soft = jnp.where(named, jnp.exp(jnp.where(named, logits - peak, 0.0)), 0.0)
    soft = soft / jnp.sum(soft, axis=-1, keepdims=True)
    live_rows = live.reshape(2 * SEQ, 1)
    gates = lax.dynamic_slice_in_dim(soft * live_rows, xl * HALF_E, HALF_E, axis=1)

    w_gu = exp_full[:, :2560]
    w_dn = exp_full[:, 2560:]
    hidden_grad = jnp.dot(cot_all, w_dn, preferred_element_type=F32).reshape(1024, HALF_E, FFS)
    pre = jnp.dot(mid_all, w_gu, preferred_element_type=F32).reshape(1024, HALF_E, 2, FFS)
    pre_gate = pre[:, :, 0]
    pre_up = pre[:, :, 1]
    sig = jax.nn.sigmoid(pre_gate)
    silu = pre_gate * sig
    inner = (silu * pre_up).astype(BF16).astype(F32)
    route_part = jnp.sum(inner * hidden_grad, axis=-1)
    gated_inner = (gates[:, :, None] * inner).astype(BF16).reshape(1024, HALF_E * FFS)
    inner_grad = gates[:, :, None] * hidden_grad
    gate_grad = inner_grad * pre_up * (sig + silu * (1.0 - sig))
    up_grad = inner_grad * silu
    pre_grad = jnp.stack([gate_grad, up_grad], axis=2).astype(BF16).reshape(1024, 2560)
    mid_part = jnp.einsum("sf,df->sd", pre_grad, w_gu, preferred_element_type=F32)

    route_wide = jnp.zeros((1024, E), F32)
    route_wide = lax.dynamic_update_slice(route_wide, route_part, (0, xl * HALF_E))
    route_grad = token_scatter(route_wide, pos, F32)
    own_start = xl * SEQ + t * BLK
    soft_own = lax.dynamic_slice_in_dim(soft, own_start, BLK)
    live_own = lax.dynamic_slice_in_dim(live_rows, own_start, BLK)
    soft_grad = route_grad * live_own
    logit_grad = soft_own * (soft_grad - jnp.sum(soft_own * soft_grad, axis=-1, keepdims=True))
    router_grad = jnp.dot(normed_mid.astype(F32).T, logit_grad, precision=precise)
    mid_from_router = jnp.dot(logit_grad, router.astype(F32).T, precision=precise)

    mid_grad = token_scatter(mid_part, pos, BF16) + mid_from_router
    mid_pull = jax.vjp(rms_scale, state, gain_f[1])[1]
    state_from_mid, mid_gain_grad = mid_pull(mid_grad)
    state_grad = cotangent.astype(F32) + state_from_mid
    branch_grad = token_gather(state_grad.astype(BF16), pos)

    mixed_part = jnp.einsum("sf,df->sd", gated_inner, w_dn, preferred_element_type=F32)
    mixed = token_scatter(mixed_part, pos, BF16)
    output = (state + mixed).astype(BF16)
    gu_grad = jnp.einsum("sd,sf->df", mid_all, pre_grad, preferred_element_type=F32).astype(BF16)
    dn_grad = jnp.einsum("sd,sf->df", cot_all, gated_inner, preferred_element_type=F32).astype(BF16)
    gu_sums = weight_scatter(gu_grad, pos)
    dn_sums = weight_scatter(dn_grad, pos)

    attended_grad = jnp.dot(branch_grad, w_out_all, preferred_element_type=F32).astype(BF16)
    out_grad = jnp.einsum("sd,sf->df", branch_grad, attended, preferred_element_type=F32)
    attended_grad = attended_grad.reshape(2, SEQ, 2, HD)
    prob_grad = jnp.einsum("sqhd,skhd->shqk", attended_grad, values, preferred_element_type=F32)
    inner_sum = jnp.sum(probs * prob_grad, axis=-1, keepdims=True)
    score_grad = (probs * (prob_grad - inner_sum)).astype(BF16)
    query_grad = jnp.einsum("shqk,skhd->sqhd", score_grad, keys, preferred_element_type=F32)
    key_grad = jnp.einsum("shqk,sqhd->skhd", score_grad, queries, preferred_element_type=F32)
    value_grad = jnp.einsum(
        "shqk,sqhd->skhd", probs_low, attended_grad, preferred_element_type=F32
    )
    query_proj, q_gain_grad = jax.vjp(post_query, project[:, :, 0], q_gain)[1](query_grad)
    key_proj, k_gain_grad = jax.vjp(post_key, project[:, :, 1], k_gain)[1](key_grad)
    proj_grad = jnp.stack([query_proj, key_proj, value_grad], axis=2).astype(BF16)
    proj_grad = proj_grad.reshape(1024, 768)
    in_part = jnp.einsum("sf,df->sd", proj_grad, w_qkv_all, preferred_element_type=F32)
    in_gain_grad = jnp.sum(in_part * (in_float * in_scale), axis=0)
    qkv_grad = jnp.einsum("sd,sf->df", normed_in, proj_grad, preferred_element_type=F32)
    in_grad = token_scatter(in_part, pos, BF16)
    in_pull = jax.vjp(lambda v: rms_scale(v, gain_f[0]), input_float)[1]
    input_grad = state_grad + in_pull(in_grad)[0]

    head_grads = lax.dynamic_update_slice(
        jnp.zeros((2, D), F32),
        jnp.stack([q_gain_grad.reshape(256), k_gain_grad.reshape(256)]),
        (0, head_start),
    )
    smalls = jnp.concatenate(
        [in_gain_grad[:, None], mid_gain_grad[:, None], head_grads.T, router_grad], axis=1
    )
    smalls = jnp.pad(smalls, ((0, 0), (0, 128 - smalls.shape[1])))
    att_grad = jnp.concatenate([qkv_grad, out_grad, smalls], axis=1).astype(BF16)
    att_own_sum, att_other_sum = weight_scatter(att_grad, pos)
    att_sums = jnp.zeros((2, 64, 1024), F32)
    att_sums = lax.dynamic_update_index_in_dim(att_sums, att_own_sum[:, :1024], xl, 0)
    att_sums = lax.dynamic_update_index_in_dim(att_sums, att_other_sum[:, :1024], 1 - xl, 0)
    qkv_out = att_sums[:, :, :768].reshape(2, 64, 3, 256).transpose(2, 1, 0, 3).reshape(3, 64, 512)
    out_out = att_sums[:, :, 768:].transpose(0, 2, 1).reshape(512, 64)
    small_sum = (att_own_sum + att_other_sum)[:, 1024:].reshape(2, 2, 16, 128)
    small_total = lax.dynamic_slice(small_sum, (pos["xh"], pos["c"], 0, 0), (1, 1, 16, 128))[0, 0]
    for dx, dc in ((0, 1), (2, 0), (2, 1)):
        h = (pos["xh"] + dx // 2) % 2
        c = (pos["c"] + dc) % 2
        give = lax.dynamic_slice(small_sum, (h, c, 0, 0), (1, 1, 16, 128))[0, 0]
        small_total = small_total + shift(give, dx=dx, dc=dc)
    gains_out = small_total[:, :4].T
    router_out = small_total[:, 4:14]

    def both(sums, width):
        joined = jnp.zeros((2, 64, width), F32)
        joined = lax.dynamic_update_index_in_dim(joined, sums[0], xl, 0)
        return lax.dynamic_update_index_in_dim(joined, sums[1], 1 - xl, 0)

    gate_up_out = both(gu_sums, 2560).reshape(2, 64, HALF_E, 2, FFS)
    gate_up_out = gate_up_out.transpose(0, 2, 3, 1, 4).reshape(E, 2, 64, FFS)
    down_out = both(dn_sums, 1280).reshape(2, 64, HALF_E, FFS)
    down_out = down_out.transpose(0, 2, 3, 1).reshape(E, FFS, 64)
    return (output, input_grad, gains_out, qkv_out, out_out, router_out, gate_up_out, down_out)


def solution(mesh):
    split = Mesh(mesh.devices.reshape(SIZES), AXES)
    placed = (
        P(DP_TENSOR, None),
        P(DP_TENSOR, None),
        P(DP),
        P(DP, None),
        P(None, DP_TENSOR),
        P(None, DP, ("xh", "c")),
        P(("xh", "c"), DP),
        P(DP_TENSOR, None),
        P(None, None, DP, ("xh", "c")),
        P(None, ("xh", "c"), DP),
    )
    return jax.shard_map(
        local,
        mesh=split,
        in_specs=placed,
        out_specs=(
            P(DP_TENSOR, None),
            P(DP_TENSOR, None),
            P(None, DP_TENSOR),
            P(None, DP, ("xh", "c")),
            P(("xh", "c"), DP),
            P(DP_TENSOR, None),
            P(None, None, DP, ("xh", "c")),
            P(None, ("xh", "c"), DP),
        ),
        check_vma=False,
    )
```

```python
import functools

import jax
import jax.numpy as jnp
import numpy as np
from jax import lax
from jax.experimental import pallas as pl
from jax.experimental.pallas import tpu as pltpu
from jax.sharding import Mesh
from jax.sharding import PartitionSpec as P

HD = 128
TOPK = 8
E = 10
D = 2048
SEQ = 512
ROWS = 1024
BLK = 128
HALF_E = 5
FFS = 256
GU = HALF_E * 2 * FFS
EW = HALF_E * 3 * FFS
AW = 1152
ROUTER_AT = 4
AXES = ("xl", "y", "z", "xh", "c")
SIZES = (2, 4, 4, 2, 2)
DP = ("xl", "y", "z")
EPS = 1e-06
THETA = 10000.0
F32 = jnp.float32
BF16 = jnp.bfloat16
MIB = 1 << 20
LOGICAL = pl.DeviceIdType.MESH
VMEM = pl.BlockSpec(memory_space=pltpu.VMEM)
ANY = pl.BlockSpec(memory_space=pl.ANY)


class Place:
    def __init__(self):
        self.xl, self.y, self.z, self.xh, self.c = (lax.axis_index(a) for a in AXES)
        self.x = self.xh * 2 + self.xl
        self.t = self.xh * 2 + self.c

    def at(self, dx=0, dy=0, dz=0, dc=0):
        x = lax.rem(self.x + (dx + 4), 4)
        return (
            lax.rem(x, 2),
            lax.rem(self.y + (dy + 4), 4),
            lax.rem(self.z + (dz + 4), 4),
            lax.div(x, 2),
            lax.rem(self.c + (dc + 2), 2),
        )

    def chip(self, dx):
        x = lax.rem(self.x + (dx + 4), 4)
        return lax.rem(x, 2), lax.div(x, 2)

    def partner(self):
        return (1 - self.xl, self.y, self.z, self.xh, self.c)


class Wires:
    def __init__(self, send, recv, near):
        self.send, self.recv, self.near = send, recv, near
        self.count, self.near_count = 0, 0

    def to(self, device, src, dst):
        k, self.count = self.count, self.count + 1
        copy = pltpu.make_async_remote_copy(
            src_ref=src,
            dst_ref=dst,
            send_sem=self.send.at[k],
            recv_sem=self.recv.at[k],
            device_id=device,
            device_id_type=LOGICAL,
        )
        copy.start()
        return copy

    def here(self, src, dst):
        k, self.near_count = self.near_count, self.near_count + 1
        copy = pltpu.make_async_copy(src, dst, self.near.at[k])
        copy.start()
        return copy


def wire_scratch(copies, local):
    return [
        pltpu.SemaphoreType.DMA((copies,)),
        pltpu.SemaphoreType.DMA((copies,)),
        pltpu.SemaphoreType.DMA((local,)),
    ]


def greet(devices):
    barrier = pltpu.get_barrier_semaphore()
    for device in devices:
        pl.semaphore_signal(barrier, inc=1, device_id=device, device_id_type=LOGICAL)
    pl.semaphore_wait(barrier, len(devices))


def params(collective_id=None, vmem=56):
    if collective_id is None:
        return pltpu.CompilerParams(vmem_limit_bytes=vmem * MIB)
    return pltpu.CompilerParams(
        collective_id=collective_id, has_side_effects=True, vmem_limit_bytes=vmem * MIB
    )


def each_rows(total, step, body):
    def run(i, carry):
        body(pl.ds(pl.multiple_of(i * step, step), step))
        return carry

    lax.fori_loop(0, total // step, run, 0)


class Spread:
    def __init__(self, wires, place, block, out):
        self.wires, self.place, self.out = wires, place, out
        mine = out.at[place.xl, place.xh, place.c]
        self.far = {k: wires.to(place.at(dx=k), block, mine) for k in (1, 3, 2)}
        self.rest = [wires.to(place.at(dc=1), block, mine)]
        self.local = wires.here(block, mine)

    def forward(self):
        for k in (1, 3, 2):
            self.far[k].wait_recv()
            xl, xh = self.place.chip(-k)
            got = self.out.at[xl, xh, self.place.c]
            self.rest.append(self.wires.to(self.place.at(dc=1), got, got))

    def finish(self):
        self.local.wait()
        for copy in self.rest:
            copy.wait()
        for copy in self.far.values():
            copy.wait_send()


class Collect:
    def __init__(self, wires, place, parts, got, own, half, arrived):
        self.wires, self.place = wires, place
        self.got, self.own, self.half, self.arrived = got, own, half, arrived
        self.swap, self.load = {}, {}
        for k in (1, 3, 2, 0):
            xl, xh = place.chip(k)
            self.swap[k] = wires.to(
                place.at(dc=1), parts.at[xl, xh, 1 - place.c], got.at[k]
            )
            self.load[k] = wires.here(parts.at[xl, xh, place.c], own.at[k])

    def pass_on(self):
        self.far = {}
        for k in (1, 3, 2):
            self.swap[k].wait_recv()
            self.load[k].wait()

            def add(rows, k=k):
                both = self.own[k, rows].astype(F32) + self.got[k, rows].astype(F32)
                self.half[k - 1, rows] = both.astype(self.half.dtype)

            each_rows(BLK, 16, add)
            self.far[k] = self.wires.to(
                self.place.at(dx=k), self.half.at[k - 1], self.arrived.at[k - 1]
            )

    def arrive(self):
        self.swap[0].wait_recv()
        self.load[0].wait()
        for k in (1, 3, 2):
            self.far[k].wait_recv()

    def total(self, rows):
        total = self.own[0, rows].astype(F32) + self.got[0, rows].astype(F32)
        for k in range(3):
            total = total + self.arrived[k, rows].astype(F32)
        return total

    def finish(self):
        for copy in self.swap.values():
            copy.wait_send()
        for copy in self.far.values():
            copy.wait_send()


def collect_scratch(width, dtype):
    return [
        pltpu.VMEM((4, BLK, width), dtype),
        pltpu.VMEM((4, BLK, width), dtype),
        pltpu.VMEM((3, BLK, width), dtype),
        pltpu.VMEM((3, BLK, width), dtype),
    ]


def cell_peers(place):
    return [place.at(dx=1), place.at(dx=2), place.at(dx=3), place.at(dc=1)]


def plane_peers(place):
    return [place.at(dy=k) for k in (1, 2, 3)] + [place.at(dz=k) for k in (1, 2, 3)]


def open_kernel(
    x_own,
    cot_own,
    att,
    small,
    exp,
    mask,
    live,
    in_all,
    cot_all,
    att_full,
    near_rows,
    far_rows,
    mask_both,
    live_both,
    send,
    recv,
    near,
):
    p = Place()
    w = Wires(send, recv, near)
    greet(cell_peers(p) + plane_peers(p) + [p.at(dx=2, dc=1)])
    xl, y, z, t = p.xl, p.y, p.z, p.t
    rows_t = pl.ds(pl.multiple_of(t * 16, 16), 16)
    mine = att_full.at[xl, y, z]
    small_mine = mine.at[rows_t, pl.ds(1024, 128)]
    smalls = [w.to(p.at(dx=a, dc=b), small, small_mine) for a, b in ((0, 1), (2, 0), (2, 1))]
    att_swap = w.to(p.partner(), att.at[1 - xl], mine.at[:, pl.ds(0, 1024)])
    local = [
        w.here(small, small_mine),
        w.here(att.at[xl], mine.at[:, pl.ds(0, 1024)]),
    ]
    tokens = Spread(w, p, x_own, in_all)
    exp_swap = w.to(p.partner(), exp.at[1 - xl], far_rows.at[z])
    masks = [
        w.to(p.partner(), mask, mask_both.at[xl]),
        w.to(p.partner(), live, live_both.at[xl]),
    ]
    later = [
        w.here(mask, mask_both.at[xl]),
        w.here(live, live_both.at[xl]),
        w.here(exp.at[xl], near_rows.at[y]),
    ]
    for copy in smalls:
        copy.wait_recv()
    for copy in local:
        copy.wait()
    strip = mine.at[:, pl.ds(1024, 128)]
    small_swap = w.to(p.partner(), strip, strip)
    att_near = [w.to(p.at(dy=k), mine, mine) for k in (1, 3, 2)]
    att_swap.wait_recv()
    small_swap.wait_recv()
    theirs = att_full.at[1 - xl, y, z]
    att_far = [w.to(p.at(dz=k), theirs, theirs) for k in (1, 3, 2)]
    exp_near = [w.to(p.at(dy=k), exp.at[xl], near_rows.at[y]) for k in (1, 3, 2)]
    exp_swap.wait_recv()
    exp_far = [w.to(p.at(dz=k), far_rows.at[z], far_rows.at[z]) for k in (1, 3, 2)]
    for copy in att_near + att_far:
        copy.wait_recv()
    whole = att_full.at[xl, :, z]
    att_end = [w.to(p.at(dz=k), whole, whole) for k in (1, 3, 2)]
    whole = att_full.at[1 - xl, y]
    att_end += [w.to(p.at(dy=k), whole, whole) for k in (1, 3, 2)]
    tokens.forward()
    cots = Spread(w, p, cot_own, cot_all)
    cots.forward()
    tokens.finish()
    cots.finish()
    for copy in masks + exp_near + exp_far + att_end + later:
        copy.wait()
    for copy in smalls + [att_swap, small_swap, exp_swap] + att_near + att_far:
        copy.wait_send()


def opening(x_own, cot_own, att, small, exp, mask, live):
    cell = jax.ShapeDtypeStruct((2, 2, 2, BLK, D), BF16)
    return pl.pallas_call(
        open_kernel,
        name="opening",
        out_shape=[
            cell,
            cell,
            jax.ShapeDtypeStruct((2, 4, 4, 64, AW), BF16),
            jax.ShapeDtypeStruct((4, 64, EW), BF16),
            jax.ShapeDtypeStruct((4, 64, EW), BF16),
            jax.ShapeDtypeStruct((2, SEQ, 128), BF16),
            jax.ShapeDtypeStruct((2, 16, SEQ), BF16),
        ],
        in_specs=[ANY] * 7,
        out_specs=[ANY] * 7,
        scratch_shapes=wire_scratch(48, 16),
        compiler_params=params(0),
    )(x_own, cot_own, att, small, exp, mask, live)


def middle_kernel(
    branch, near_rows, far_rows, x_own, gains, state, mid_all, exp_full,
    got, own, half, arrived, block, send, recv, near,
):
    p = Place()
    w = Wires(send, recv, near)
    xl, y, z = p.xl, p.y, p.z
    greet(cell_peers(p) + [p.at(dy=1), p.at(dy=3), p.at(dz=1), p.at(dz=3)])
    sums = Collect(w, p, branch, got, own, half, arrived)
    mine = exp_full.at[xl, :, z]
    theirs = exp_full.at[1 - xl, y]
    near_up = w.to(p.at(dz=1), near_rows, mine)
    near_down = w.to(p.at(dz=3), near_rows, mine)
    far_up = w.to(p.at(dy=1), far_rows, theirs)
    far_down = w.to(p.at(dy=3), far_rows, theirs)
    local = [w.here(near_rows, mine), w.here(far_rows, theirs)]
    sums.pass_on()
    sums.arrive()

    def norm(rows):
        now = x_own[rows].astype(F32) + sums.total(rows)
        state[rows] = now
        scale = lax.rsqrt(jnp.mean(now * now, axis=-1, keepdims=True) + EPS)
        block[rows] = (now * scale * gains[1:2]).astype(BF16)

    each_rows(BLK, 16, norm)
    tokens = Spread(w, p, block, mid_all)
    below = lax.rem(z + 3, 4)
    above = lax.rem(z + 1, 4)
    left = lax.rem(y + 3, 4)
    right = lax.rem(y + 1, 4)
    relays = []
    near_up.wait_recv()
    part = exp_full.at[xl, pl.ds(0, 2), below]
    relays.append(w.to(p.at(dz=1), part, part))
    far_up.wait_recv()
    part = exp_full.at[1 - xl, left, pl.ds(0, 2)]
    relays.append(w.to(p.at(dy=1), part, part))
    near_down.wait_recv()
    part = exp_full.at[xl, pl.ds(2, 2), above]
    relays.append(w.to(p.at(dz=3), part, part))
    far_down.wait_recv()
    part = exp_full.at[1 - xl, right, pl.ds(2, 2)]
    relays.append(w.to(p.at(dy=3), part, part))
    tokens.forward()
    tokens.finish()
    sums.finish()
    for copy in local + relays:
        copy.wait()
    for copy in (near_up, near_down, far_up, far_down):
        copy.wait_send()


def middle(branch, near_rows, far_rows, x_own, gains):
    return pl.pallas_call(
        middle_kernel,
        name="middle",
        out_shape=[
            jax.ShapeDtypeStruct((BLK, D), F32),
            jax.ShapeDtypeStruct((2, 2, 2, BLK, D), BF16),
            jax.ShapeDtypeStruct((2, 4, 4, 64, EW), BF16),
        ],
        in_specs=[ANY, ANY, ANY, VMEM, VMEM],
        out_specs=[VMEM, ANY, ANY],
        scratch_shapes=collect_scratch(D, BF16)
        + [pltpu.VMEM((BLK, D), BF16)]
        + wire_scratch(32, 16),
        compiler_params=params(1),
    )(branch, near_rows, far_rows, x_own, gains)


def split_dot(value, other, dims):
    high = value.astype(BF16)
    low = (value - high.astype(F32)).astype(BF16)
    dot = functools.partial(
        lax.dot_general, dimension_numbers=(dims, ((), ())), preferred_element_type=F32
    )
    return dot(high, other) + dot(low, other)


def norm_back(value, gain, grad):
    scale = lax.rsqrt(jnp.mean(value * value, axis=-1, keepdims=True) + EPS)
    shaped = grad * gain
    along = jnp.mean(shaped * value, axis=-1, keepdims=True)
    return scale * shaped - value * (scale * scale * scale * along), grad * value * scale


def turn_kernel(
    mid_part, route, gu, dn, state, cot_own, soft, small, gains,
    branch_grad, state_grad, gain_grad, logit_grad, near_rows, far_rows,
    got, own, half, arrived, rgot, rown, rhalf, rarrived, from_router, block,
    near_in, far_in, send, recv, near,
):
    p = Place()
    w = Wires(send, recv, near)
    xl, y, z = p.xl, p.y, p.z
    greet(cell_peers(p) + plane_peers(p))
    routes = Collect(w, p, route, rgot, rown, rhalf, rarrived)
    sums = Collect(w, p, mid_part, got, own, half, arrived)
    gu_cols, dn_cols = pl.ds(0, GU), pl.ds(GU, EW - GU)
    sent = []
    for k in (1, 3, 2):
        to_z, to_y = lax.rem(z + k, 4), lax.rem(y + k, 4)
        for source, cols in ((gu, gu_cols), (dn, dn_cols)):
            sent.append(
                w.to(p.at(dz=k), source.at[xl, :, to_z], near_in.at[k - 1, :, :, cols])
            )
            sent.append(
                w.to(p.at(dy=k), source.at[1 - xl, to_y], far_in.at[k - 1, :, :, cols])
            )
    local = []
    for source, cols in ((gu, gu_cols), (dn, dn_cols)):
        local.append(w.here(source.at[xl, :, z], near_rows.at[:, :, cols]))
        local.append(w.here(source.at[1 - xl, y], far_rows.at[:, :, cols]))
    routes.pass_on()
    sums.pass_on()
    routes.arrive()

    def router(rows):
        chance = soft[rows]
        grad = routes.total(rows)
        grad = chance * (grad - jnp.sum(chance * grad, axis=-1, keepdims=True))
        logit_grad[rows] = grad

    each_rows(BLK, 16, router)
    from_router[...] = split_dot(logit_grad[...], small[...], ((1,), (1,)))
    sums.arrive()
    gain_grad[...] = jnp.zeros_like(gain_grad)

    def back(rows):
        grad = sums.total(rows) + from_router[rows]
        change, gain_part = norm_back(state[rows], gains[1:2], grad)
        total = cot_own[rows].astype(F32) + change
        state_grad[rows] = total
        block[rows] = total.astype(BF16)
        gain_grad[0:1] += jnp.sum(gain_part, axis=0, keepdims=True)

    each_rows(BLK, 16, back)
    tokens = Spread(w, p, block, branch_grad)
    tokens.forward()
    for copy in local:
        copy.wait()
    for copy in sent:
        copy.wait_recv()
    for rows_ref, in_ref in ((near_rows, near_in), (far_rows, far_in)):
        for b in range(4):

            def add(rows, b=b, rows_ref=rows_ref, in_ref=in_ref):
                total = rows_ref[b, rows].astype(F32)
                for k in range(3):
                    total = total + in_ref[k, b, rows].astype(F32)
                rows_ref[b, rows] = total.astype(BF16)

            each_rows(64, 16, add)
    tokens.finish()
    sums.finish()
    routes.finish()
    for copy in sent:
        copy.wait_send()


def turn(mid_part, route, gu, dn, state, cot_own, soft, small, gains):
    part = jax.ShapeDtypeStruct((4, 64, EW), BF16)
    return pl.pallas_call(
        turn_kernel,
        name="turn",
        out_shape=[
            jax.ShapeDtypeStruct((2, 2, 2, BLK, D), BF16),
            jax.ShapeDtypeStruct((BLK, D), F32),
            jax.ShapeDtypeStruct((8, D), F32),
            jax.ShapeDtypeStruct((BLK, 128), F32),
            part,
            part,
        ],
        in_specs=[ANY] * 4 + [VMEM] * 5,
        out_specs=[ANY] + [VMEM] * 5,
        scratch_shapes=collect_scratch(D, BF16)
        + collect_scratch(128, F32)
        + [
            pltpu.VMEM((BLK, D), F32),
            pltpu.VMEM((BLK, D), BF16),
            pltpu.VMEM((3, 4, 64, EW), BF16),
            pltpu.VMEM((3, 4, 64, EW), BF16),
        ]
        + wire_scratch(48, 16),
        compiler_params=params(2),
    )(mid_part, route, gu, dn, state, cot_own, soft, small, gains)


def close_kernel(
    in_part, mixed, near_rows, far_rows, att_grad, state, state_grad, x_own, gains,
    input_grad, output, exp_sum, att_sum, small_sum,
    got, own, half, arrived, mgot, mown, mhalf, marrived,
    near_in, far_in, far_sum, att_near_in, att_far_in, att_near, att_far,
    att_near_end, att_far_end, att_far_sum, exp_got, att_got, small_all, small_in,
    send, recv, near,
):
    p = Place()
    w = Wires(send, recv, near)
    xl, y, z = p.xl, p.y, p.z
    greet(cell_peers(p) + plane_peers(p) + [p.at(dx=2, dc=1)])
    sums = Collect(w, p, in_part, got, own, half, arrived)
    sent = []
    atts = []
    exps = []
    for k in (1, 3, 2):
        to_z, to_y = lax.rem(z + k, 4), lax.rem(y + k, 4)
        atts.append(w.to(p.at(dz=k), att_grad.at[xl, :, to_z], att_near_in.at[k - 1]))
        atts.append(w.to(p.at(dy=k), att_grad.at[1 - xl, to_y], att_far_in.at[k - 1]))
    for k in (1, 3, 2):
        to_z, to_y = lax.rem(z + k, 4), lax.rem(y + k, 4)
        exps.append(w.to(p.at(dy=k), near_rows.at[to_y], near_in.at[k - 1]))
        exps.append(w.to(p.at(dz=k), far_rows.at[to_z], far_in.at[k - 1]))
    local = [
        w.here(att_grad.at[xl, :, z], att_near),
        w.here(att_grad.at[1 - xl, y], att_far),
        w.here(near_rows.at[y], near_in.at[3]),
        w.here(far_rows.at[z], far_in.at[3]),
    ]
    sums.pass_on()
    mixes = Collect(w, p, mixed, mgot, mown, mhalf, marrived)
    sums.arrive()

    def back(rows):
        change, _ = norm_back(x_own[rows].astype(F32), gains[0:1], sums.total(rows))
        input_grad[rows] = state_grad[rows] + change

    each_rows(BLK, 16, back)
    mixes.pass_on()
    for copy in local:
        copy.wait()
    for copy in atts:
        copy.wait_recv()
    for rows_ref, in_ref in ((att_near, att_near_in), (att_far, att_far_in)):
        for b in range(4):

            def add(rows, b=b, rows_ref=rows_ref, in_ref=in_ref):
                total = rows_ref[b, rows].astype(F32)
                for k in range(3):
                    total = total + in_ref[k, b, rows].astype(F32)
                rows_ref[b, rows] = total.astype(BF16)

            each_rows(64, 16, add)
    ends = []
    for k in (1, 3, 2):
        to_z, to_y = lax.rem(z + k, 4), lax.rem(y + k, 4)
        ends.append(w.to(p.at(dy=k), att_near.at[to_y], att_near_end.at[k - 1]))
        ends.append(w.to(p.at(dz=k), att_far.at[to_z], att_far_end.at[k - 1]))
    for copy in exps:
        copy.wait_recv()

    def exp_far(rows):
        total = far_in[3, rows].astype(F32)
        for k in range(3):
            total = total + far_in[k, rows].astype(F32)
        far_sum[rows] = total.astype(BF16)

    each_rows(64, 16, exp_far)
    exp_swap = w.to(p.partner(), far_sum, exp_got)

    def exp_near(rows):
        total = near_in[3, rows].astype(F32)
        for k in range(3):
            total = total + near_in[k, rows].astype(F32)
        exp_sum[0, rows] = total

    each_rows(64, 16, exp_near)
    mixes.arrive()

    def finish(rows):
        output[rows] = (state[rows] + mixes.total(rows)).astype(BF16)

    each_rows(BLK, 16, finish)
    for copy in ends:
        copy.wait_recv()

    def att_far_add(rows):
        total = att_far[z, rows].astype(F32)
        for k in range(3):
            total = total + att_far_end[k, rows].astype(F32)
        att_far_sum[rows] = total.astype(BF16)

    each_rows(64, 16, att_far_add)
    att_swap = w.to(p.partner(), att_far_sum, att_got)

    def att_near_add(rows):
        total = att_near[y, rows].astype(F32)
        for k in range(3):
            total = total + att_near_end[k, rows].astype(F32)
        att_sum[0, rows] = total

    each_rows(64, 16, att_near_add)
    exp_swap.wait_recv()
    exp_sum[1] = exp_got[...].astype(F32)
    att_swap.wait_recv()
    att_sum[1] = att_got[...].astype(F32)
    small_all[...] = att_sum[0, :, 1024:] + att_sum[1, :, 1024:]
    smalls = []
    for n, (a, b) in enumerate(((0, 1), (2, 0), (2, 1))):
        dest = lax.rem(p.xh + a // 2, 2) * 2 + lax.rem(p.c + b, 2)
        smalls.append(
            w.to(
                p.at(dx=a, dc=b),
                small_all.at[pl.ds(pl.multiple_of(dest * 16, 16), 16)],
                small_in.at[n],
            )
        )
    for copy in smalls:
        copy.wait_recv()
    total = small_all[pl.ds(pl.multiple_of(p.t * 16, 16), 16)]
    for n in range(3):
        total = total + small_in[n]
    small_sum[...] = total
    sums.finish()
    mixes.finish()
    for copy in atts + exps + ends + [exp_swap, att_swap] + smalls:
        copy.wait_send()


def closing(in_part, mixed, near_rows, far_rows, att_grad, state, state_grad, x_own, gains):
    return pl.pallas_call(
        close_kernel,
        name="closing",
        out_shape=[
            jax.ShapeDtypeStruct((BLK, D), F32),
            jax.ShapeDtypeStruct((BLK, D), BF16),
            jax.ShapeDtypeStruct((2, 64, EW), F32),
            jax.ShapeDtypeStruct((2, 64, AW), F32),
            jax.ShapeDtypeStruct((16, 128), F32),
        ],
        in_specs=[ANY] * 5 + [VMEM] * 4,
        out_specs=[VMEM] * 5,
        scratch_shapes=collect_scratch(D, BF16)
        + collect_scratch(D, BF16)
        + [
            pltpu.VMEM((4, 64, EW), BF16),
            pltpu.VMEM((4, 64, EW), BF16),
            pltpu.VMEM((64, EW), BF16),
            pltpu.VMEM((3, 4, 64, AW), BF16),
            pltpu.VMEM((3, 4, 64, AW), BF16),
            pltpu.VMEM((4, 64, AW), BF16),
            pltpu.VMEM((4, 64, AW), BF16),
            pltpu.VMEM((3, 64, AW), BF16),
            pltpu.VMEM((3, 64, AW), BF16),
            pltpu.VMEM((64, AW), BF16),
            pltpu.VMEM((64, EW), BF16),
            pltpu.VMEM((64, AW), BF16),
            pltpu.VMEM((64, 128), F32),
            pltpu.VMEM((3, 16, 128), F32),
        ]
        + wire_scratch(48, 16),
        compiler_params=params(3),
    )(in_part, mixed, near_rows, far_rows, att_grad, state, state_grad, x_own, gains)


def dot(a, b, dims=((1,), (0,))):
    return lax.dot_general(a, b, (dims, ((), ())), preferred_element_type=F32)


def turn_half(v):
    return pltpu.roll(v, HD // 2, 1)


def attend_kernel(
    x, w_att, gains, head_gains, cos, sin, live, normed, proj, qkv, attended, branch
):
    def norm(rows):
        v = x[rows].astype(F32)
        scale = lax.rsqrt(jnp.mean(v * v, axis=-1, keepdims=True) + EPS)
        normed[rows] = (v * scale * gains[0:1]).astype(BF16)

    each_rows(SEQ, 16, norm)
    for c in range(3):
        cols = pl.ds(c * 256, 256)
        proj[:, cols] = dot(normed[...], w_att[:, cols])
    for h in range(2):
        for c, factor in ((0, HD ** (-0.5)), (1, 1.0)):
            cols = pl.ds(c * 256 + h * HD, HD)
            v = proj[:, cols]
            scale = lax.rsqrt(jnp.mean(v * v, axis=-1, keepdims=True) + EPS)
            v = v * scale * head_gains[c : c + 1, h * HD : (h + 1) * HD]
            v = (v * cos[...] + turn_half(v) * sin[...]) * factor
            qkv[:, cols] = v.astype(BF16)
    qkv[:, 512:] = proj[:, 512:].astype(BF16)
    for h in range(2):
        q, k, v = (qkv[:, pl.ds(c * 256 + h * HD, HD)] for c in range(3))
        scores = dot(q, k, ((1,), (1,)))
        weights = jnp.exp(scores - jnp.max(scores, axis=-1, keepdims=True)) * live[0, 0:1]
        probs = (weights / jnp.sum(weights, axis=-1, keepdims=True)).astype(BF16)
        attended[:, pl.ds(h * HD, HD)] = dot(probs, v).astype(BF16)
    for n in range(4):
        rows = pl.ds(n * 512, 512)
        branch[:, rows] = dot(
            attended[...], w_att[rows, 768:1024], ((1,), (1,))
        ).astype(BF16)


def whole(shape):
    return pl.BlockSpec(shape, lambda s: (0,) * len(shape), pipeline_mode=pl.Buffered(1))


def by_seq(width):
    return pl.BlockSpec((SEQ, width), lambda s: (s, 0))


def attend(x, w_att, gains, head_gains, cos, sin, live):
    flops = 2 * ROWS * D * 1024 + 2 * 2 * 4 * SEQ * SEQ * HD
    return pl.pallas_call(
        attend_kernel,
        name="attend",
        grid=(2,),
        out_shape=[
            jax.ShapeDtypeStruct((ROWS, D), BF16),
            jax.ShapeDtypeStruct((ROWS, 768), F32),
            jax.ShapeDtypeStruct((ROWS, 768), BF16),
            jax.ShapeDtypeStruct((ROWS, 256), BF16),
            jax.ShapeDtypeStruct((ROWS, D), BF16),
        ],
        in_specs=[
            by_seq(D),
            whole((D, AW)),
            whole((8, D)),
            whole((8, 256)),
            whole((SEQ, HD)),
            whole((SEQ, HD)),
            pl.BlockSpec((1, 16, SEQ), lambda s: (s, 0, 0)),
        ],
        out_specs=[by_seq(D), by_seq(768), by_seq(768), by_seq(256), by_seq(D)],
        compiler_params=params(),
        cost_estimate=pl.CostEstimate(flops=flops, bytes_accessed=20 * MIB, transcendentals=0),
    )(x, w_att, gains, head_gains, cos, sin, live)


def attend_back_kernel(
    bg, x, w_att, gains, head_gains, cos, sin, live, proj, qkv,
    proj_grad, in_part, in_gain, head_gain, att_bg,
):
    first = pl.program_id(0) == 0

    @pl.when(first)
    def _():
        in_gain[...] = jnp.zeros_like(in_gain)
        head_gain[...] = jnp.zeros_like(head_gain)

    att_bg[...] = dot(bg[...], w_att[:, 768:1024]).astype(BF16)
    for h in range(2):
        head = pl.ds(h * HD, HD)
        q, k, v = (qkv[:, pl.ds(c * 256 + h * HD, HD)] for c in range(3))
        scores = dot(q, k, ((1,), (1,)))
        weights = jnp.exp(scores - jnp.max(scores, axis=-1, keepdims=True)) * live[0, 0:1]
        probs = weights / jnp.sum(weights, axis=-1, keepdims=True)
        prob_grad = dot(att_bg[:, head], v, ((1,), (1,)))
        inner = jnp.sum(probs * prob_grad, axis=-1, keepdims=True)
        score_grad = (probs * (prob_grad - inner)).astype(BF16)
        value_grad = dot(probs.astype(BF16), att_bg[:, head], ((0,), (0,)))
        proj_grad[:, pl.ds(512 + h * HD, HD)] = value_grad.astype(BF16)
        both = (
            (0, dot(score_grad, k) * HD ** (-0.5)),
            (1, dot(score_grad, q, ((0,), (0,)))),
        )
        for c, grad in both:
            cols = pl.ds(c * 256 + h * HD, HD)
            grad = grad * cos[...] - turn_half(grad) * sin[...]
            gain = head_gains[c : c + 1, h * HD : (h + 1) * HD]
            change, gain_part = norm_back(proj[:, cols], gain, grad)
            proj_grad[:, cols] = change.astype(BF16)
            head_gain[c : c + 1, h * HD : (h + 1) * HD] += jnp.sum(
                gain_part, axis=0, keepdims=True
            )
    for n in range(4):
        rows = pl.ds(n * 128, 128)
        part = dot(proj_grad[rows], w_att[:, :768], ((1,), (1,)))
        in_part[rows] = part.astype(BF16)
        v = x[rows].astype(F32)
        scale = lax.rsqrt(jnp.mean(v * v, axis=-1, keepdims=True) + EPS)
        in_gain[0:1] += jnp.sum(part * v * scale, axis=0, keepdims=True)


def attend_back(bg, x, w_att, gains, head_gains, cos, sin, live, proj, qkv):
    flops = 2 * ROWS * D * 1024 + 2 * 2 * 10 * SEQ * SEQ * HD
    return pl.pallas_call(
        attend_back_kernel,
        name="attend_back",
        grid=(2,),
        out_shape=[
            jax.ShapeDtypeStruct((ROWS, 768), BF16),
            jax.ShapeDtypeStruct((ROWS, D), BF16),
            jax.ShapeDtypeStruct((8, D), F32),
            jax.ShapeDtypeStruct((8, 256), F32),
        ],
        in_specs=[
            by_seq(D),
            by_seq(D),
            whole((D, AW)),
            whole((8, D)),
            whole((8, 256)),
            whole((SEQ, HD)),
            whole((SEQ, HD)),
            pl.BlockSpec((1, 16, SEQ), lambda s: (s, 0, 0)),
            by_seq(768),
            by_seq(768),
        ],
        out_specs=[by_seq(768), by_seq(D), whole((8, D)), whole((8, 256))],
        scratch_shapes=[pltpu.VMEM((SEQ, 256), BF16)],
        compiler_params=params(),
        cost_estimate=pl.CostEstimate(flops=flops, bytes_accessed=20 * MIB, transcendentals=0),
    )(bg, x, w_att, gains, head_gains, cos, sin, live, proj, qkv)


TILE = 256


def expert_kernel(
    mid, cot, w_exp, small, mask, pre_grad, gated, mid_part, mixed_part, soft, route, acc, acc2
):
    xl = lax.axis_index("xl")
    logits = dot(mid[...], small[...])
    on = mask[...] > 0
    peak = jnp.max(jnp.where(on, logits, -1e30), axis=-1, keepdims=True)
    chance = jnp.where(on, jnp.exp(jnp.where(on, logits - peak, 0.0)), 0.0)
    chance = chance / jnp.maximum(jnp.sum(chance, axis=-1, keepdims=True), 1.0)
    soft[...] = chance
    lane = lax.broadcasted_iota(jnp.int32, (TILE, 128), 1)
    routed = jnp.zeros((TILE, 128), F32)
    for e in range(HALF_E):
        here = lane == ROUTER_AT + xl * HALF_E + e
        gate = jnp.sum(jnp.where(here, chance, 0.0), axis=-1, keepdims=True)
        pre = dot(mid[...], w_exp[:, pl.ds(e * 512, 512)])
        hidden = dot(cot[...], w_exp[:, pl.ds(GU + e * 256, 256)])
        gate_pre, up_pre = pre[:, :FFS], pre[:, FFS:]
        sig = 1.0 / (1.0 + jnp.exp(-gate_pre))
        silu = gate_pre * sig
        inner = (silu * up_pre).astype(BF16).astype(F32)
        routed = jnp.where(here, jnp.sum(inner * hidden, axis=-1, keepdims=True), routed)
        gated[:, pl.ds(e * FFS, FFS)] = (gate * inner).astype(BF16)
        hidden = gate * hidden
        pre_grad[:, pl.ds(e * 512, FFS)] = (
            hidden * up_pre * (sig + silu * (1.0 - sig))
        ).astype(BF16)
        pre_grad[:, pl.ds(e * 512 + FFS, FFS)] = (hidden * silu).astype(BF16)
    route[...] = routed
    for n in range(4):
        rows = pl.ds(n * 512, 512)
        mid_part[:, rows] = dot(pre_grad[...], w_exp[rows, :GU], ((1,), (1,))).astype(BF16)
        mixed_part[:, rows] = dot(gated[...], w_exp[rows, GU:], ((1,), (1,))).astype(BF16)


def experts(mid, cot, w_exp, small, mask):
    def tile(width):
        return pl.BlockSpec((TILE, width), lambda s: (s, 0))

    return pl.pallas_call(
        expert_kernel,
        name="experts",
        grid=(ROWS // TILE,),
        out_shape=[
            jax.ShapeDtypeStruct((ROWS, GU), BF16),
            jax.ShapeDtypeStruct((ROWS, EW - GU), BF16),
            jax.ShapeDtypeStruct((ROWS, D), BF16),
            jax.ShapeDtypeStruct((ROWS, D), BF16),
            jax.ShapeDtypeStruct((ROWS, 128), F32),
            jax.ShapeDtypeStruct((ROWS, 128), F32),
        ],
        in_specs=[tile(D), tile(D), whole((D, EW)), whole((D, 128)), tile(128)],
        out_specs=[tile(GU), tile(EW - GU), tile(D), tile(D), tile(128), tile(128)],
        scratch_shapes=[pltpu.VMEM((8, 128), F32), pltpu.VMEM((8, 128), F32)],
        compiler_params=params(),
        cost_estimate=pl.CostEstimate(
            flops=2 * ROWS * D * 256 * 30, bytes_accessed=40 * MIB, transcendentals=0
        ),
    )(mid, cot, w_exp, small, mask)


def rotary_tables():
    half = HD // 2
    freqs = np.float32(THETA) ** (-(np.arange(half, dtype=np.float32) * np.float32(2.0 / HD)))
    angles = np.arange(SEQ, dtype=np.float32)[:, None] * freqs[None, :].astype(np.float32)
    cos, sin = np.cos(angles), np.sin(angles)
    return (
        np.concatenate([cos, cos], axis=1).astype(np.float32),
        np.concatenate([-sin, sin], axis=1).astype(np.float32),
    )


def local(
    layer_input, cotangent, lengths, expert_ids, gains, w_qkv, w_out, w_router, w_gate_up, w_down
):
    xl, xh, c = (lax.axis_index(a) for a in ("xl", "xh", "c"))
    t = xh * 2 + c

    small = jnp.concatenate([gains.T, w_router], axis=1)
    small = jnp.pad(small, ((0, 0), (0, 128 - small.shape[1])))
    out_rows = w_out.reshape(2, 256, 64).transpose(0, 2, 1)
    qkv_rows = w_qkv.reshape(3, 64, 2, 256).transpose(2, 1, 0, 3).reshape(2, 64, 768)
    att = jnp.concatenate([qkv_rows, out_rows], axis=2)
    exp = jnp.concatenate(
        [
            w_gate_up.reshape(2, HALF_E, 2, 64, FFS).transpose(0, 3, 1, 2, 4).reshape(2, 64, GU),
            w_down.reshape(2, HALF_E, FFS, 64).transpose(0, 3, 1, 2).reshape(2, 64, EW - GU),
        ],
        axis=2,
    )
    on = jnp.arange(SEQ, dtype=jnp.int32) < lengths[0]
    number = jnp.arange(128, dtype=jnp.int32) - ROUTER_AT
    named = jnp.zeros((SEQ, 128), bool)
    for k in range(TOPK):
        named = named | (expert_ids[:, k][:, None] == number[None, :])
    mask = (named & on[:, None]).astype(BF16)
    live = jnp.broadcast_to(on[None, :], (16, SEQ)).astype(BF16)

    in_all, cot_all, att_full, near_rows, far_rows, mask_both, live_both = opening(
        layer_input, cotangent, att, small, exp, mask, live
    )
    x_all = in_all.reshape(ROWS, D)
    cot_all = cot_all.reshape(ROWS, D)
    w_att = att_full.reshape(D, AW)
    w_small = w_att[:, 1024:]
    gain_rows = w_small[:, :8].astype(F32).T
    head_start = t * 512 + xl * 256
    head_gains = lax.dynamic_slice(gain_rows, (2, head_start), (2, 256))
    head_gains = jnp.pad(head_gains, ((0, 6), (0, 0)))
    live_both = live_both.astype(F32)
    cos, sin = (jnp.asarray(table) for table in rotary_tables())

    normed, proj, qkv, attended, branch = attend(
        x_all, w_att, gain_rows, head_gains, cos, sin, live_both
    )
    state, mid_all, exp_full = middle(
        branch.reshape(2, 2, 2, BLK, D), near_rows, far_rows, layer_input, gain_rows
    )
    mid = mid_all.reshape(ROWS, D)
    w_exp = exp_full.reshape(D, EW)
    pre_grad, gated, mid_part, mixed_part, soft, route = experts(
        mid, cot_all, w_exp, w_small, mask_both.reshape(ROWS, 128)
    )
    gu = jnp.einsum("sd,sf->df", mid, pre_grad, preferred_element_type=F32).astype(BF16)
    dn = jnp.einsum("sd,sf->df", cot_all, gated, preferred_element_type=F32).astype(BF16)
    own_start = xl * SEQ + t * BLK
    soft_own = lax.dynamic_slice_in_dim(soft, own_start, BLK)
    branch_grad, state_grad, mid_gain, logit_grad, near_sum, far_sum = turn(
        mid_part.reshape(2, 2, 2, BLK, D),
        route.reshape(2, 2, 2, BLK, 128),
        gu.reshape(2, 4, 4, 64, GU),
        dn.reshape(2, 4, 4, 64, EW - GU),
        state,
        cotangent,
        soft_own,
        w_small,
        gain_rows,
    )
    bg = branch_grad.reshape(ROWS, D)
    proj_grad, in_part, in_gain, head_gain = attend_back(
        bg, x_all, w_att, gain_rows, head_gains, cos, sin, live_both, proj, qkv
    )
    qkv_grad = jnp.einsum("sd,sf->df", normed, proj_grad, preferred_element_type=F32)
    out_grad = jnp.einsum("sd,sf->df", bg, attended, preferred_element_type=F32)
    mid_own = lax.dynamic_slice_in_dim(mid, own_start, BLK)
    router_grad = jnp.dot(
        mid_own.astype(F32).T, logit_grad, precision=lax.Precision.HIGHEST
    )[:, ROUTER_AT : ROUTER_AT + E]
    head_rows = lax.dynamic_update_slice(jnp.zeros((2, D), F32), head_gain[:2], (0, head_start))
    gain_part = jnp.concatenate([in_gain[:1], mid_gain[:1], head_rows]).T
    smalls = jnp.concatenate([gain_part, router_grad], axis=1)
    smalls = jnp.pad(smalls, ((0, 0), (0, 128 - smalls.shape[1])))
    att_grad = jnp.concatenate([qkv_grad, out_grad, smalls], axis=1).astype(BF16)
    input_grad, output, exp_sum, att_sum, small_sum = closing(
        in_part.reshape(2, 2, 2, BLK, D),
        mixed_part.reshape(2, 2, 2, BLK, D),
        near_sum,
        far_sum,
        att_grad.reshape(2, 4, 4, 64, AW),
        state,
        state_grad,
        layer_input,
        gain_rows,
    )

    def in_order(sums):
        return jnp.where(xl == 0, sums, sums[::-1])

    gate_up_out = in_order(exp_sum[:, :, :GU]).reshape(2, 64, HALF_E, 2, FFS)
    gate_up_out = gate_up_out.transpose(0, 2, 3, 1, 4).reshape(E, 2, 64, FFS)
    down_out = in_order(exp_sum[:, :, GU:]).reshape(2, 64, HALF_E, FFS)
    down_out = down_out.transpose(0, 2, 3, 1).reshape(E, FFS, 64)
    qkv_out = in_order(att_sum[:, :, :768]).reshape(2, 64, 3, 256)
    qkv_out = qkv_out.transpose(2, 1, 0, 3).reshape(3, 64, 512)
    out_out = in_order(att_sum[:, :, 768:1024]).transpose(0, 2, 1).reshape(512, 64)
    gains_out = small_sum[:, :4].T
    router_out = small_sum[:, ROUTER_AT : ROUTER_AT + E]
    return (output, input_grad, gains_out, qkv_out, out_out, router_out, gate_up_out, down_out)


def solution(mesh):
    split = Mesh(mesh.devices.reshape(SIZES), AXES)
    rows, tensor = P(AXES, None), ("xh", "c")
    return jax.shard_map(
        local,
        mesh=split,
        in_specs=(
            rows,
            rows,
            P(DP),
            P(DP, None),
            P(None, AXES),
            P(None, DP, tensor),
            P(tensor, DP),
            rows,
            P(None, None, DP, tensor),
            P(None, tensor, DP),
        ),
        out_specs=(
            rows,
            rows,
            P(None, AXES),
            P(None, DP, tensor),
            P(tensor, DP),
            rows,
            P(None, None, DP, tensor),
            P(None, tensor, DP),
        ),
        check_vma=False,
    )
```

```python
import functools

import jax
import jax.numpy as jnp
import numpy as np
from jax import lax
from jax.experimental import pallas as pl
from jax.experimental.pallas import tpu as pltpu
from jax.sharding import Mesh
from jax.sharding import PartitionSpec as P

HD = 128
TOPK = 8
E = 10
D = 2048
SEQ = 512
ROWS = 1024
BLK = 128
HALF_E = 5
FFS = 256
GU = HALF_E * 2 * FFS
EW = HALF_E * 3 * FFS
AW = 1152
ROUTER_AT = 4
AXES = ("xl", "y", "z", "xh", "c")
SIZES = (2, 4, 4, 2, 2)
DP = ("xl", "y", "z")
EPS = 1e-06
THETA = 10000.0
F32 = jnp.float32
BF16 = jnp.bfloat16
MIB = 1 << 20
LOGICAL = pl.DeviceIdType.MESH
VMEM = pl.BlockSpec(memory_space=pltpu.VMEM)
ANY = pl.BlockSpec(memory_space=pl.ANY)


class Place:
    def __init__(self):
        self.xl, self.y, self.z, self.xh, self.c = (lax.axis_index(a) for a in AXES)
        self.x = self.xh * 2 + self.xl
        self.t = self.xh * 2 + self.c

    def at(self, dx=0, dy=0, dz=0, dc=0):
        x = lax.rem(self.x + (dx + 4), 4)
        return (
            lax.rem(x, 2),
            lax.rem(self.y + (dy + 4), 4),
            lax.rem(self.z + (dz + 4), 4),
            lax.div(x, 2),
            lax.rem(self.c + (dc + 2), 2),
        )

    def chip(self, dx):
        x = lax.rem(self.x + (dx + 4), 4)
        return lax.rem(x, 2), lax.div(x, 2)

    def partner(self):
        return (1 - self.xl, self.y, self.z, self.xh, self.c)


class Wires:
    def __init__(self, send, recv, near):
        self.send, self.recv, self.near = send, recv, near
        self.count, self.near_count = 0, 0

    def to(self, device, src, dst):
        k, self.count = self.count, self.count + 1
        copy = pltpu.make_async_remote_copy(
            src_ref=src,
            dst_ref=dst,
            send_sem=self.send.at[k],
            recv_sem=self.recv.at[k],
            device_id=device,
            device_id_type=LOGICAL,
        )
        copy.start()
        return copy

    def here(self, src, dst):
        k, self.near_count = self.near_count, self.near_count + 1
        copy = pltpu.make_async_copy(src, dst, self.near.at[k])
        copy.start()
        return copy


def wire_scratch(copies, local):
    return [
        pltpu.SemaphoreType.DMA((copies,)),
        pltpu.SemaphoreType.DMA((copies,)),
        pltpu.SemaphoreType.DMA((local,)),
    ]


def greet(devices):
    barrier = pltpu.get_barrier_semaphore()
    for device in devices:
        pl.semaphore_signal(barrier, inc=1, device_id=device, device_id_type=LOGICAL)
    pl.semaphore_wait(barrier, len(devices))


def params(collective_id=None, vmem=56):
    if collective_id is None:
        return pltpu.CompilerParams(vmem_limit_bytes=vmem * MIB)
    return pltpu.CompilerParams(
        collective_id=collective_id, has_side_effects=True, vmem_limit_bytes=vmem * MIB
    )


def each_rows(total, step, body):
    def run(i, carry):
        body(pl.ds(pl.multiple_of(i * step, step), step))
        return carry

    lax.fori_loop(0, total // step, run, 0)


class Spread:
    def __init__(self, wires, place, block, out):
        self.wires, self.place, self.out = wires, place, out
        mine = out.at[place.xl, place.xh, place.c]
        self.far = {k: wires.to(place.at(dx=k), block, mine) for k in (1, 3, 2)}
        self.rest = [wires.to(place.at(dc=1), block, mine)]
        self.local = wires.here(block, mine)

    def forward(self):
        for k in (1, 3, 2):
            self.far[k].wait_recv()
            xl, xh = self.place.chip(-k)
            got = self.out.at[xl, xh, self.place.c]
            self.rest.append(self.wires.to(self.place.at(dc=1), got, got))

    def arrived(self):
        self.local.wait()
        for copy in self.rest:
            copy.wait_recv()

    def finish(self):
        for copy in self.rest + list(self.far.values()):
            copy.wait_send()


class Collect:
    def __init__(self, wires, place, parts, got, own, half, arrived):
        self.wires, self.place, self.parts = wires, place, parts
        self.got, self.own, self.half, self.arrived = got, own, half, arrived
        self.swap, self.load, self.far = {}, {}, {}

    def begin(self, steps=(1, 3, 2, 0)):
        for k in steps:
            xl, xh = self.place.chip(k)
            self.swap[k] = self.wires.to(
                self.place.at(dc=1), self.parts.at[xl, xh, 1 - self.place.c], self.got.at[k]
            )
            if self.own is not None:
                self.load[k] = self.wires.here(
                    self.parts.at[xl, xh, self.place.c], self.own.at[k]
                )

    def mine(self, k, rows):
        if self.own is not None:
            return self.own[k, rows]
        xl, xh = self.place.chip(k)
        return self.parts[xl, xh, self.place.c, rows]

    def pass_on(self, steps=(1, 3, 2)):
        for k in steps:
            self.swap[k].wait_recv()
            if self.own is not None:
                self.load[k].wait()

            def add(rows, k=k):
                both = self.mine(k, rows).astype(F32) + self.got[k, rows].astype(F32)
                self.half[k - 1, rows] = both.astype(self.half.dtype)

            each_rows(BLK, 16, add)
            self.far[k] = self.wires.to(
                self.place.at(dx=k), self.half.at[k - 1], self.arrived.at[k - 1]
            )

    def arrive(self):
        self.swap[0].wait_recv()
        if self.own is not None:
            self.load[0].wait()
        for k in (1, 3, 2):
            self.far[k].wait_recv()

    def total(self, rows):
        total = self.mine(0, rows).astype(F32) + self.got[0, rows].astype(F32)
        for k in range(3):
            total = total + self.arrived[k, rows].astype(F32)
        return total

    def finish(self):
        for copy in self.swap.values():
            copy.wait_send()
        for copy in self.far.values():
            copy.wait_send()


def collect_scratch(width, dtype):
    return [
        pltpu.VMEM((4, BLK, width), dtype),
        pltpu.VMEM((4, BLK, width), dtype),
        pltpu.VMEM((3, BLK, width), dtype),
        pltpu.VMEM((3, BLK, width), dtype),
    ]


def dot(a, b, dims=((1,), (0,))):
    return lax.dot_general(a, b, (dims, ((), ())), preferred_element_type=F32)


def turn_half(v):
    return pltpu.roll(v, HD // 2, 1)


def cell_peers(place):
    return [place.at(dx=1), place.at(dx=2), place.at(dx=3), place.at(dc=1)]


def plane_peers(place):
    return [place.at(dy=k) for k in (1, 2, 3)] + [place.at(dz=k) for k in (1, 2, 3)]


def forward_kernel(
    x_own, cot_own, att, small, exp, mask, live, cos, sin,
    cot_all, mid_all, exp_full, att_out, normed_out, proj_out, qkv, attended, state, gains,
    head_gains, mask_both, live_out,
    x_all, att_full, live_both, near_rows, far_rows, normed, proj, branch,
    got, half, arrived, block, send, recv, near,
):
    p = Place()
    w = Wires(send, recv, near)
    greet(cell_peers(p) + plane_peers(p) + [p.at(dx=2, dc=1)])
    xl, y, z, t = p.xl, p.y, p.z, p.t

    rows_t = pl.ds(pl.multiple_of(t * 16, 16), 16)
    mine = att_full.at[xl, y, z]
    small_mine = mine.at[rows_t, pl.ds(1024, 128)]
    smalls = [w.to(p.at(dx=a, dc=b), small, small_mine) for a, b in ((0, 1), (2, 0), (2, 1))]
    att_swap = w.to(p.partner(), att.at[1 - xl], mine.at[:, pl.ds(0, 1024)])
    tokens = Spread(w, p, x_own, x_all)
    mine[:, 0:1024] = att[xl]
    mine[rows_t, 1024:1152] = small[...]
    live_both[xl] = live[...]
    for copy in smalls:
        copy.wait_recv()
    strip = mine.at[:, pl.ds(1024, 128)]
    small_swap = w.to(p.partner(), strip, strip)
    att_near = [w.to(p.at(dy=k), mine, mine) for k in (1, 3, 2)]
    att_swap.wait_recv()
    small_swap.wait_recv()
    theirs = att_full.at[1 - xl, y, z]
    att_far = [w.to(p.at(dz=k), theirs, theirs) for k in (1, 3, 2)]
    exp_swap = w.to(p.partner(), exp.at[1 - xl], far_rows.at[z])
    masks = [
        w.to(p.partner(), live, live_both.at[xl]),
        w.to(p.partner(), mask, mask_both.at[xl]),
    ]
    local = [w.here(mask, mask_both.at[xl])]
    near_rows[y] = exp[xl]
    for copy in att_near + att_far:
        copy.wait_recv()
    whole = att_full.at[xl, :, z]
    att_end = [w.to(p.at(dz=k), whole, whole) for k in (1, 3, 2)]
    whole = att_full.at[1 - xl, y]
    att_end += [w.to(p.at(dy=k), whole, whole) for k in (1, 3, 2)]
    tokens.forward()
    exp_near = [w.to(p.at(dy=k), exp.at[xl], near_rows.at[y]) for k in (1, 3, 2)]
    exp_swap.wait_recv()
    exp_far = [w.to(p.at(dz=k), far_rows.at[z], far_rows.at[z]) for k in (1, 3, 2)]
    cots = Spread(w, p, cot_own, cot_all)
    for copy in att_end:
        copy.wait_recv()
    tokens.arrived()

    for n in range(16):
        column = att_full[n // 8, n % 8 // 2, pl.ds(n % 2 * 2, 2), :, 1024:1152]
        column = jnp.transpose(column.astype(F32).reshape(128, 128))
        gains[:, n * 128 : (n + 1) * 128] = column[:8]
    start = pl.multiple_of(t * 512 + xl * 256, 256)
    head_gains[...] = jnp.zeros_like(head_gains)
    head_gains[0:2] = gains[2:4, pl.ds(start, 256)]
    masks[0].wait_recv()
    local.append(w.here(att_full, att_out))
    local.append(w.here(live_both, live_out))

    sums = Collect(w, p, branch, got, None, half, arrived)

    def project(s):
        for b in range(4):

            def norm(rows, b=b):
                v = x_all[s, b // 2, b % 2, rows].astype(F32)
                scale = lax.rsqrt(jnp.mean(v * v, axis=-1, keepdims=True) + EPS)
                value = (v * scale * gains[0:1]).astype(BF16)
                normed[s, pl.ds(pl.multiple_of(b * BLK + rows.start, 16), 16)] = value

            each_rows(BLK, 16, norm)
        for c in range(3):
            cols = pl.ds(c * 256, 256)
            weight = att_full[:, :, :, :, cols].reshape(D, 256)
            proj[s, :, cols] = dot(normed[s], weight)

    def attend(s):
        for h in range(2):
            for c, factor in ((0, HD ** (-0.5)), (1, 1.0)):
                cols = pl.ds(c * 256 + h * HD, HD)
                v = proj[s, :, cols]
                scale = lax.rsqrt(jnp.mean(v * v, axis=-1, keepdims=True) + EPS)
                v = v * scale * head_gains[c : c + 1, h * HD : (h + 1) * HD]
                v = (v * cos[...] + turn_half(v) * sin[...]) * factor
                qkv[s, :, cols] = v.astype(BF16)
        qkv[s, :, 512:768] = proj[s, :, 512:768].astype(BF16)
        for h in range(2):
            q, k, v = (qkv[s, :, pl.ds(c * 256 + h * HD, HD)] for c in range(3))
            scores = dot(q, k, ((1,), (1,)))
            weights = jnp.exp(scores - jnp.max(scores, axis=-1, keepdims=True))
            weights = weights * live_both[s, 0:1].astype(F32)
            probs = (weights / jnp.sum(weights, axis=-1, keepdims=True)).astype(BF16)
            attended[s, :, pl.ds(h * HD, HD)] = dot(probs, v).astype(BF16)
        for n in range(4):
            weight = att_full[n // 2, pl.ds(n % 2 * 2, 2), :, :, 768:1024].reshape(512, 256)
            part = dot(attended[s], weight, ((1,), (1,))).astype(BF16)
            branch[s, :, :, :, pl.ds(n * 512, 512)] = part.reshape(2, 2, BLK, 512)

    first, second = 1 - xl, xl
    project(first)
    attend(first)
    sums.begin((1, 3))
    cots.forward()
    for copy in exp_near + exp_far:
        copy.wait_recv()
    mine_z = exp_full.at[xl, :, z]
    mine_y = exp_full.at[1 - xl, y]
    near_up = w.to(p.at(dz=1), near_rows, mine_z)
    near_down = w.to(p.at(dz=3), near_rows, mine_z)
    far_up = w.to(p.at(dy=1), far_rows, mine_y)
    far_down = w.to(p.at(dy=3), far_rows, mine_y)
    local += [w.here(near_rows, mine_z), w.here(far_rows, mine_y)]
    sums.pass_on((1, 3))
    project(second)
    attend(second)
    sums.begin((2, 0))
    local += [w.here(normed, normed_out), w.here(proj, proj_out)]
    sums.pass_on((2,))
    sums.arrive()

    def norm(rows):
        now = x_own[rows].astype(F32) + sums.total(rows)
        state[rows] = now
        scale = lax.rsqrt(jnp.mean(now * now, axis=-1, keepdims=True) + EPS)
        block[rows] = (now * scale * gains[1:2]).astype(BF16)

    each_rows(BLK, 16, norm)
    mids = Spread(w, p, block, mid_all)
    below, above = lax.rem(z + 3, 4), lax.rem(z + 1, 4)
    left, right = lax.rem(y + 3, 4), lax.rem(y + 1, 4)
    relays = []
    near_up.wait_recv()
    part = exp_full.at[xl, pl.ds(0, 2), below]
    relays.append(w.to(p.at(dz=1), part, part))
    far_up.wait_recv()
    part = exp_full.at[1 - xl, left, pl.ds(0, 2)]
    relays.append(w.to(p.at(dy=1), part, part))
    near_down.wait_recv()
    part = exp_full.at[xl, pl.ds(2, 2), above]
    relays.append(w.to(p.at(dz=3), part, part))
    far_down.wait_recv()
    part = exp_full.at[1 - xl, right, pl.ds(2, 2)]
    relays.append(w.to(p.at(dy=3), part, part))
    mids.forward()
    mids.arrived()
    cots.arrived()
    for copy in masks[1:]:
        copy.wait_recv()
    for copy in relays:
        copy.wait_recv()
    for copy in local:
        copy.wait()
    for group in (tokens, cots, mids, sums):
        group.finish()
    for copy in (
        smalls + [att_swap, small_swap, exp_swap] + masks + att_near + att_far + att_end
        + exp_near + exp_far + relays + [near_up, near_down, far_up, far_down]
    ):
        copy.wait_send()


def forward(x_own, cot_own, att, small, exp, mask, live, cos, sin):
    cell = jax.ShapeDtypeStruct((2, 2, 2, BLK, D), BF16)
    return pl.pallas_call(
        forward_kernel,
        name="forward",
        out_shape=[
            cell,
            cell,
            jax.ShapeDtypeStruct((2, 4, 4, 64, EW), BF16),
            jax.ShapeDtypeStruct((2, 4, 4, 64, AW), BF16),
            jax.ShapeDtypeStruct((2, SEQ, D), BF16),
            jax.ShapeDtypeStruct((2, SEQ, 768), F32),
            jax.ShapeDtypeStruct((2, SEQ, 768), BF16),
            jax.ShapeDtypeStruct((2, SEQ, 256), BF16),
            jax.ShapeDtypeStruct((BLK, D), F32),
            jax.ShapeDtypeStruct((8, D), F32),
            jax.ShapeDtypeStruct((8, 256), F32),
            jax.ShapeDtypeStruct((2, SEQ, 128), BF16),
            jax.ShapeDtypeStruct((2, 16, SEQ), BF16),
        ],
        in_specs=[VMEM] * 9,
        out_specs=[ANY] * 6 + [VMEM] * 5 + [ANY] * 2,
        scratch_shapes=[
            pltpu.VMEM((2, 2, 2, BLK, D), BF16),
            pltpu.VMEM((2, 4, 4, 64, AW), BF16),
            pltpu.VMEM((2, 16, SEQ), BF16),
            pltpu.VMEM((4, 64, EW), BF16),
            pltpu.VMEM((4, 64, EW), BF16),
            pltpu.VMEM((2, SEQ, D), BF16),
            pltpu.VMEM((2, SEQ, 768), F32),
            pltpu.VMEM((2, 2, 2, BLK, D), BF16),
            pltpu.VMEM((4, BLK, D), BF16),
            pltpu.VMEM((3, BLK, D), BF16),
            pltpu.VMEM((3, BLK, D), BF16),
            pltpu.VMEM((BLK, D), BF16),
        ]
        + wire_scratch(80, 16),
        compiler_params=params(0, 60),
    )(x_own, cot_own, att, small, exp, mask, live, cos, sin)


def split_dot(value, other, dims):
    high = value.astype(BF16)
    low = (value - high.astype(F32)).astype(BF16)
    dot = functools.partial(
        lax.dot_general, dimension_numbers=(dims, ((), ())), preferred_element_type=F32
    )
    return dot(high, other) + dot(low, other)


def norm_back(value, gain, grad):
    scale = lax.rsqrt(jnp.mean(value * value, axis=-1, keepdims=True) + EPS)
    shaped = grad * gain
    along = jnp.mean(shaped * value, axis=-1, keepdims=True)
    return scale * shaped - value * (scale * scale * scale * along), grad * value * scale


class Reduce:
    def __init__(self, wires, up, down, blocks, here, halves, mains):
        self.wires, self.up, self.down = wires, up, down
        self.blocks, self.here, self.halves, self.mains = blocks, here, halves, mains
        self.first, self.second = {}, {}

    def begin(self, cols):
        opposite = self.blocks(lax.rem(self.here + 2, 4))
        low, high = pl.ds(0, 2), pl.ds(2, 2)
        self.first[cols] = (
            self.wires.to(self.up, opposite.at[low, :, self.span(cols)], self.half(0, cols)),
            self.wires.to(self.down, opposite.at[high, :, self.span(cols)], self.half(1, cols)),
        )

    @staticmethod
    def span(cols):
        return pl.ds(*cols)

    def half(self, side, cols):
        return self.halves.at[side, :, :, self.span(cols)]

    def relay(self, cols):
        span = self.span(cols)
        sent = []
        for side, device in ((0, self.up), (1, self.down)):
            self.first[cols][side].wait_recv()
            block = self.blocks(lax.rem(self.here + (1 if side == 0 else 3), 4))
            for b in range(2):
                at = (side * 2 + b, slice(None), span)
                total = block[at].astype(F32) + self.halves[side, b, :, span].astype(F32)
                block[at] = total.astype(BF16)
            sent.append(
                self.wires.to(device, block.at[:, :, span], self.mains.at[side, :, :, span])
            )
        self.second[cols] = sent

    def total(self, cols, store):
        span = self.span(cols)
        for copy in self.second[cols]:
            copy.wait_recv()
        own = self.blocks(self.here)
        for b in range(4):
            total = own[b, :, span].astype(F32)
            for side in range(2):
                total = total + self.mains[side, b, :, span].astype(F32)
            store(b, span, total)

    def finish(self):
        for copies in list(self.first.values()) + list(self.second.values()):
            for copy in copies:
                copy.wait_send()


def turn_kernel(
    mid_part, route, mid, cot, pre_grad, gated, state, cot_own, soft, small, gains,
    branch_grad, state_grad, gain_grad, logit_grad, near_rows, far_rows,
    got, own, half, arrived, rgot, rown, rhalf, rarrived, from_router, block,
    mid_here, cot_here, pre_here, gated_here, dw, near_half, far_half, near_main, far_main,
    send, recv, near,
):
    p = Place()
    w = Wires(send, recv, near)
    xl, y, z = p.xl, p.y, p.z
    greet(cell_peers(p) + [p.at(dy=1), p.at(dy=3), p.at(dz=1), p.at(dz=3)])
    routes = Collect(w, p, route, rgot, rown, rhalf, rarrived)
    sums = Collect(w, p, mid_part, got, own, half, arrived)
    routes.begin()
    sums.begin()
    loads = [w.here(mid, mid_here), w.here(cot, cot_here)]

    def fetch(e):
        return (
            w.here(pre_grad.at[:, pl.ds(e * 512, 512)], pre_here.at[e % 2]),
            w.here(gated.at[:, pl.ds(e * FFS, FFS)], gated_here.at[e % 2]),
        )

    ready = {0: fetch(0), 1: fetch(1)}
    along_z = Reduce(
        w, p.at(dz=1), p.at(dz=3), lambda k: dw.at[xl, :, k], z, near_half, near_main
    )
    along_y = Reduce(
        w, p.at(dy=1), p.at(dy=3), lambda k: dw.at[1 - xl, k], y, far_half, far_main
    )
    routes.pass_on()
    sums.pass_on()
    for copy in loads:
        copy.wait()
    groups = [(e * 768, 768) for e in range(HALF_E)]
    for e in range(HALF_E):
        for copy in ready[e]:
            copy.wait()
        for n in range(4):
            at = pl.ds(n * 512, 512)
            to = (n // 2, pl.ds(n % 2 * 2, 2))
            grad = dot(mid_here[:, at], pre_here[e % 2], ((0,), (0,)))
            dw[(*to, slice(None), slice(None), pl.ds(e * 768, 512))] = grad.astype(
                BF16
            ).reshape(2, 4, 64, 512)
            grad = dot(cot_here[:, at], gated_here[e % 2], ((0,), (0,)))
            dw[(*to, slice(None), slice(None), pl.ds(e * 768 + 512, 256))] = grad.astype(
                BF16
            ).reshape(2, 4, 64, 256)
        along_z.begin(groups[e])
        along_y.begin(groups[e])
        if e + 2 < HALF_E:
            ready[e + 2] = fetch(e + 2)
        if e > 0:
            along_z.relay(groups[e - 1])
            along_y.relay(groups[e - 1])
    routes.arrive()

    def router(rows):
        chance = soft[rows]
        grad = routes.total(rows)
        grad = chance * (grad - jnp.sum(chance * grad, axis=-1, keepdims=True))
        logit_grad[rows] = grad

    each_rows(BLK, 16, router)
    from_router[...] = split_dot(logit_grad[...], small[...], ((1,), (1,)))
    along_z.relay(groups[-1])
    along_y.relay(groups[-1])
    sums.arrive()
    gain_grad[...] = jnp.zeros_like(gain_grad)

    def back(rows):
        grad = sums.total(rows) + from_router[rows]
        change, gain_part = norm_back(state[rows], gains[1:2], grad)
        total = cot_own[rows].astype(F32) + change
        state_grad[rows] = total
        block[rows] = total.astype(BF16)
        gain_grad[0:1] += jnp.sum(gain_part, axis=0, keepdims=True)

    each_rows(BLK, 16, back)
    tokens = Spread(w, p, block, branch_grad)

    def keep(rows_ref):
        def store(b, span, total):
            rows_ref[b, :, span] = total.astype(BF16)

        return store

    for e in range(HALF_E):
        if e == 3:
            tokens.forward()
        along_z.total(groups[e], keep(near_rows))
        along_y.total(groups[e], keep(far_rows))
    tokens.arrived()
    tokens.finish()
    sums.finish()
    routes.finish()
    along_z.finish()
    along_y.finish()


def turn(mid_part, route, mid, cot, pre_grad, gated, state, cot_own, soft, small, gains):
    part = jax.ShapeDtypeStruct((4, 64, EW), BF16)
    return pl.pallas_call(
        turn_kernel,
        name="turn",
        out_shape=[
            jax.ShapeDtypeStruct((2, 2, 2, BLK, D), BF16),
            jax.ShapeDtypeStruct((BLK, D), F32),
            jax.ShapeDtypeStruct((8, D), F32),
            jax.ShapeDtypeStruct((BLK, 128), F32),
            part,
            part,
        ],
        in_specs=[ANY] * 6 + [VMEM] * 5,
        out_specs=[ANY] + [VMEM] * 5,
        scratch_shapes=collect_scratch(D, BF16)
        + collect_scratch(128, F32)
        + [
            pltpu.VMEM((BLK, D), F32),
            pltpu.VMEM((BLK, D), BF16),
            pltpu.VMEM((ROWS, D), BF16),
            pltpu.VMEM((ROWS, D), BF16),
            pltpu.VMEM((2, ROWS, 512), BF16),
            pltpu.VMEM((2, ROWS, FFS), BF16),
            pltpu.VMEM((2, 4, 4, 64, EW), BF16),
            pltpu.VMEM((2, 2, 64, EW), BF16),
            pltpu.VMEM((2, 2, 64, EW), BF16),
            pltpu.VMEM((2, 4, 64, EW), BF16),
            pltpu.VMEM((2, 4, 64, EW), BF16),
        ]
        + wire_scratch(72, 40),
        compiler_params=params(2, 60),
    )(mid_part, route, mid, cot, pre_grad, gated, state, cot_own, soft, small, gains)


def close_kernel(
    in_part, mixed, near_rows, far_rows, att_grad, state, state_grad, x_own, gains,
    input_grad, output, exp_sum, att_sum, small_sum,
    got, own, half, arrived, mgot, mown, mhalf, marrived,
    near_in, far_in, far_sum, att_near_in, att_far_in, att_near, att_far,
    att_near_end, att_far_end, att_far_sum, exp_got, att_got, small_all, small_in,
    send, recv, near,
):
    p = Place()
    w = Wires(send, recv, near)
    xl, y, z = p.xl, p.y, p.z
    greet(cell_peers(p) + plane_peers(p) + [p.at(dx=2, dc=1)])
    sums = Collect(w, p, in_part, got, own, half, arrived)
    sums.begin()
    sent = []
    atts = []
    exps = []
    for k in (1, 3, 2):
        to_z, to_y = lax.rem(z + k, 4), lax.rem(y + k, 4)
        atts.append(w.to(p.at(dz=k), att_grad.at[xl, :, to_z], att_near_in.at[k - 1]))
        atts.append(w.to(p.at(dy=k), att_grad.at[1 - xl, to_y], att_far_in.at[k - 1]))
    for k in (1, 3, 2):
        to_z, to_y = lax.rem(z + k, 4), lax.rem(y + k, 4)
        exps.append(w.to(p.at(dy=k), near_rows.at[to_y], near_in.at[k - 1]))
        exps.append(w.to(p.at(dz=k), far_rows.at[to_z], far_in.at[k - 1]))
    local = [
        w.here(att_grad.at[xl, :, z], att_near),
        w.here(att_grad.at[1 - xl, y], att_far),
        w.here(near_rows.at[y], near_in.at[3]),
        w.here(far_rows.at[z], far_in.at[3]),
    ]
    sums.pass_on()
    mixes = Collect(w, p, mixed, mgot, mown, mhalf, marrived)
    mixes.begin()
    sums.arrive()

    def back(rows):
        change, _ = norm_back(x_own[rows].astype(F32), gains[0:1], sums.total(rows))
        input_grad[rows] = state_grad[rows] + change

    each_rows(BLK, 16, back)
    mixes.pass_on()
    for copy in local:
        copy.wait()
    for copy in atts:
        copy.wait_recv()
    for rows_ref, in_ref in ((att_near, att_near_in), (att_far, att_far_in)):
        for b in range(4):

            def add(rows, b=b, rows_ref=rows_ref, in_ref=in_ref):
                total = rows_ref[b, rows].astype(F32)
                for k in range(3):
                    total = total + in_ref[k, b, rows].astype(F32)
                rows_ref[b, rows] = total.astype(BF16)

            each_rows(64, 16, add)
    ends = []
    for k in (1, 3, 2):
        to_z, to_y = lax.rem(z + k, 4), lax.rem(y + k, 4)
        ends.append(w.to(p.at(dy=k), att_near.at[to_y], att_near_end.at[k - 1]))
        ends.append(w.to(p.at(dz=k), att_far.at[to_z], att_far_end.at[k - 1]))
    for copy in exps:
        copy.wait_recv()

    def exp_far(rows):
        total = far_in[3, rows].astype(F32)
        for k in range(3):
            total = total + far_in[k, rows].astype(F32)
        far_sum[rows] = total.astype(BF16)

    each_rows(64, 16, exp_far)
    exp_swap = w.to(p.partner(), far_sum, exp_got)

    def exp_near(rows):
        total = near_in[3, rows].astype(F32)
        for k in range(3):
            total = total + near_in[k, rows].astype(F32)
        exp_sum[0, rows] = total

    each_rows(64, 16, exp_near)
    mixes.arrive()

    def finish(rows):
        output[rows] = (state[rows] + mixes.total(rows)).astype(BF16)

    each_rows(BLK, 16, finish)
    for copy in ends:
        copy.wait_recv()

    def att_far_add(rows):
        total = att_far[z, rows].astype(F32)
        for k in range(3):
            total = total + att_far_end[k, rows].astype(F32)
        att_far_sum[rows] = total.astype(BF16)

    each_rows(64, 16, att_far_add)
    att_swap = w.to(p.partner(), att_far_sum, att_got)

    def att_near_add(rows):
        total = att_near[y, rows].astype(F32)
        for k in range(3):
            total = total + att_near_end[k, rows].astype(F32)
        att_sum[0, rows] = total

    each_rows(64, 16, att_near_add)
    exp_swap.wait_recv()
    exp_sum[1] = exp_got[...].astype(F32)
    att_swap.wait_recv()
    att_sum[1] = att_got[...].astype(F32)
    small_all[...] = att_sum[0, :, 1024:] + att_sum[1, :, 1024:]
    smalls = []
    for n, (a, b) in enumerate(((0, 1), (2, 0), (2, 1))):
        dest = lax.rem(p.xh + a // 2, 2) * 2 + lax.rem(p.c + b, 2)
        smalls.append(
            w.to(
                p.at(dx=a, dc=b),
                small_all.at[pl.ds(pl.multiple_of(dest * 16, 16), 16)],
                small_in.at[n],
            )
        )
    for copy in smalls:
        copy.wait_recv()
    total = small_all[pl.ds(pl.multiple_of(p.t * 16, 16), 16)]
    for n in range(3):
        total = total + small_in[n]
    small_sum[...] = total
    sums.finish()
    mixes.finish()
    for copy in atts + exps + ends + [exp_swap, att_swap] + smalls:
        copy.wait_send()


def closing(in_part, mixed, near_rows, far_rows, att_grad, state, state_grad, x_own, gains):
    return pl.pallas_call(
        close_kernel,
        name="closing",
        out_shape=[
            jax.ShapeDtypeStruct((BLK, D), F32),
            jax.ShapeDtypeStruct((BLK, D), BF16),
            jax.ShapeDtypeStruct((2, 64, EW), F32),
            jax.ShapeDtypeStruct((2, 64, AW), F32),
            jax.ShapeDtypeStruct((16, 128), F32),
        ],
        in_specs=[ANY] * 5 + [VMEM] * 4,
        out_specs=[VMEM] * 5,
        scratch_shapes=collect_scratch(D, BF16)
        + collect_scratch(D, BF16)
        + [
            pltpu.VMEM((4, 64, EW), BF16),
            pltpu.VMEM((4, 64, EW), BF16),
            pltpu.VMEM((64, EW), BF16),
            pltpu.VMEM((3, 4, 64, AW), BF16),
            pltpu.VMEM((3, 4, 64, AW), BF16),
            pltpu.VMEM((4, 64, AW), BF16),
            pltpu.VMEM((4, 64, AW), BF16),
            pltpu.VMEM((3, 64, AW), BF16),
            pltpu.VMEM((3, 64, AW), BF16),
            pltpu.VMEM((64, AW), BF16),
            pltpu.VMEM((64, EW), BF16),
            pltpu.VMEM((64, AW), BF16),
            pltpu.VMEM((64, 128), F32),
            pltpu.VMEM((3, 16, 128), F32),
        ]
        + wire_scratch(48, 16),
        compiler_params=params(3),
    )(in_part, mixed, near_rows, far_rows, att_grad, state, state_grad, x_own, gains)


def whole(shape):
    return pl.BlockSpec(shape, lambda s: (0,) * len(shape), pipeline_mode=pl.Buffered(1))


def by_seq(width):
    return pl.BlockSpec((SEQ, width), lambda s: (s, 0))


def attend_back_kernel(
    bg, normed, w_att, gains, head_gains, cos, sin, live, proj, qkv,
    proj_grad, in_part, in_gain, head_gain, att_bg,
):
    first = pl.program_id(0) == 0

    @pl.when(first)
    def _():
        in_gain[...] = jnp.zeros_like(in_gain)
        head_gain[...] = jnp.zeros_like(head_gain)

    att_bg[...] = dot(bg[...], w_att[:, 768:1024]).astype(BF16)
    for h in range(2):
        head = pl.ds(h * HD, HD)
        q, k, v = (qkv[:, pl.ds(c * 256 + h * HD, HD)] for c in range(3))
        scores = dot(q, k, ((1,), (1,)))
        weights = jnp.exp(scores - jnp.max(scores, axis=-1, keepdims=True)) * live[0, 0:1].astype(F32)
        probs = weights / jnp.sum(weights, axis=-1, keepdims=True)
        prob_grad = dot(att_bg[:, head], v, ((1,), (1,)))
        inner = jnp.sum(probs * prob_grad, axis=-1, keepdims=True)
        score_grad = (probs * (prob_grad - inner)).astype(BF16)
        value_grad = dot(probs.astype(BF16), att_bg[:, head], ((0,), (0,)))
        proj_grad[:, pl.ds(512 + h * HD, HD)] = value_grad.astype(BF16)
        both = (
            (0, dot(score_grad, k) * HD ** (-0.5)),
            (1, dot(score_grad, q, ((0,), (0,)))),
        )
        for c, grad in both:
            cols = pl.ds(c * 256 + h * HD, HD)
            grad = grad * cos[...] - turn_half(grad) * sin[...]
            gain = head_gains[c : c + 1, h * HD : (h + 1) * HD]
            change, gain_part = norm_back(proj[:, cols], gain, grad)
            proj_grad[:, cols] = change.astype(BF16)
            head_gain[c : c + 1, h * HD : (h + 1) * HD] += jnp.sum(
                gain_part, axis=0, keepdims=True
            )
    for n in range(4):
        rows = pl.ds(n * 128, 128)
        part = dot(proj_grad[rows], w_att[:, :768], ((1,), (1,)))
        in_part[rows] = part.astype(BF16)
        in_gain[0:1] += jnp.sum(part * normed[rows].astype(F32), axis=0, keepdims=True)

    @pl.when(jnp.logical_not(first))
    def _():
        in_gain[0:1] = in_gain[0:1] / gains[0:1]


def attend_back(bg, normed, w_att, gains, head_gains, cos, sin, live, proj, qkv):
    flops = 2 * ROWS * D * 1024 + 2 * 2 * 10 * SEQ * SEQ * HD
    return pl.pallas_call(
        attend_back_kernel,
        name="attend_back",
        grid=(2,),
        out_shape=[
            jax.ShapeDtypeStruct((ROWS, 768), BF16),
            jax.ShapeDtypeStruct((ROWS, D), BF16),
            jax.ShapeDtypeStruct((8, D), F32),
            jax.ShapeDtypeStruct((8, 256), F32),
        ],
        in_specs=[
            by_seq(D),
            by_seq(D),
            whole((D, AW)),
            whole((8, D)),
            whole((8, 256)),
            whole((SEQ, HD)),
            whole((SEQ, HD)),
            pl.BlockSpec((1, 16, SEQ), lambda s: (s, 0, 0)),
            by_seq(768),
            by_seq(768),
        ],
        out_specs=[by_seq(768), by_seq(D), whole((8, D)), whole((8, 256))],
        scratch_shapes=[pltpu.VMEM((SEQ, 256), BF16)],
        compiler_params=params(),
        cost_estimate=pl.CostEstimate(flops=flops, bytes_accessed=20 * MIB, transcendentals=0),
    )(bg, normed, w_att, gains, head_gains, cos, sin, live, proj, qkv)


TILE = 256


def expert_kernel(
    mid, cot, w_exp, small, mask, pre_grad, gated, mid_part, mixed_part, soft, route, acc, acc2
):
    xl = lax.axis_index("xl")
    logits = dot(mid[...], small[...])
    on = mask[...] > 0
    peak = jnp.max(jnp.where(on, logits, -1e30), axis=-1, keepdims=True)
    chance = jnp.where(on, jnp.exp(jnp.where(on, logits - peak, 0.0)), 0.0)
    chance = chance / jnp.maximum(jnp.sum(chance, axis=-1, keepdims=True), 1.0)
    soft[...] = chance
    lane = lax.broadcasted_iota(jnp.int32, (TILE, 128), 1)
    routed = jnp.zeros((TILE, 128), F32)
    for e in range(HALF_E):
        here = lane == ROUTER_AT + xl * HALF_E + e
        gate = jnp.sum(jnp.where(here, chance, 0.0), axis=-1, keepdims=True)
        pre = dot(mid[...], w_exp[:, pl.ds(e * 512, 512)])
        hidden = dot(cot[...], w_exp[:, pl.ds(GU + e * 256, 256)])
        gate_pre, up_pre = pre[:, :FFS], pre[:, FFS:]
        sig = 1.0 / (1.0 + jnp.exp(-gate_pre))
        silu = gate_pre * sig
        inner = (silu * up_pre).astype(BF16).astype(F32)
        routed = jnp.where(here, jnp.sum(inner * hidden, axis=-1, keepdims=True), routed)
        gated[:, pl.ds(e * FFS, FFS)] = (gate * inner).astype(BF16)
        hidden = gate * hidden
        pre_grad[:, pl.ds(e * 512, FFS)] = (
            hidden * up_pre * (sig + silu * (1.0 - sig))
        ).astype(BF16)
        pre_grad[:, pl.ds(e * 512 + FFS, FFS)] = (hidden * silu).astype(BF16)
    route[...] = routed
    for n in range(4):
        rows = pl.ds(n * 512, 512)
        mid_part[:, rows] = dot(pre_grad[...], w_exp[rows, :GU], ((1,), (1,))).astype(BF16)
        mixed_part[:, rows] = dot(gated[...], w_exp[rows, GU:], ((1,), (1,))).astype(BF16)


def experts(mid, cot, w_exp, small, mask):
    def tile(width):
        return pl.BlockSpec((TILE, width), lambda s: (s, 0))

    return pl.pallas_call(
        expert_kernel,
        name="experts",
        grid=(ROWS // TILE,),
        out_shape=[
            jax.ShapeDtypeStruct((ROWS, GU), BF16),
            jax.ShapeDtypeStruct((ROWS, EW - GU), BF16),
            jax.ShapeDtypeStruct((ROWS, D), BF16),
            jax.ShapeDtypeStruct((ROWS, D), BF16),
            jax.ShapeDtypeStruct((ROWS, 128), F32),
            jax.ShapeDtypeStruct((ROWS, 128), F32),
        ],
        in_specs=[tile(D), tile(D), whole((D, EW)), whole((D, 128)), tile(128)],
        out_specs=[tile(GU), tile(EW - GU), tile(D), tile(D), tile(128), tile(128)],
        scratch_shapes=[pltpu.VMEM((8, 128), F32), pltpu.VMEM((8, 128), F32)],
        compiler_params=params(),
        cost_estimate=pl.CostEstimate(
            flops=2 * ROWS * D * 256 * 30, bytes_accessed=40 * MIB, transcendentals=0
        ),
    )(mid, cot, w_exp, small, mask)


def rotary_tables():
    half = HD // 2
    freqs = np.float32(THETA) ** (-(np.arange(half, dtype=np.float32) * np.float32(2.0 / HD)))
    angles = np.arange(SEQ, dtype=np.float32)[:, None] * freqs[None, :].astype(np.float32)
    cos, sin = np.cos(angles), np.sin(angles)
    return (
        np.concatenate([cos, cos], axis=1).astype(np.float32),
        np.concatenate([-sin, sin], axis=1).astype(np.float32),
    )


def local(
    layer_input, cotangent, lengths, expert_ids, gains, w_qkv, w_out, w_router, w_gate_up, w_down
):
    xl, xh, c = (lax.axis_index(a) for a in ("xl", "xh", "c"))
    t = xh * 2 + c

    small = jnp.concatenate([gains.T, w_router], axis=1)
    small = jnp.pad(small, ((0, 0), (0, 128 - small.shape[1])))
    out_rows = w_out.reshape(2, 256, 64).transpose(0, 2, 1)
    qkv_rows = w_qkv.reshape(3, 64, 2, 256).transpose(2, 1, 0, 3).reshape(2, 64, 768)
    att = jnp.concatenate([qkv_rows, out_rows], axis=2)
    exp = jnp.concatenate(
        [
            w_gate_up.reshape(2, HALF_E, 2, 64, FFS).transpose(0, 3, 1, 2, 4).reshape(2, 64, GU),
            w_down.reshape(2, HALF_E, FFS, 64).transpose(0, 3, 1, 2).reshape(2, 64, EW - GU),
        ],
        axis=2,
    )
    on = jnp.arange(SEQ, dtype=jnp.int32) < lengths[0]
    number = jnp.arange(128, dtype=jnp.int32) - ROUTER_AT
    named = jnp.zeros((SEQ, 128), bool)
    for k in range(TOPK):
        named = named | (expert_ids[:, k][:, None] == number[None, :])
    mask = (named & on[:, None]).astype(BF16)
    live = jnp.broadcast_to(on[None, :], (16, SEQ)).astype(BF16)

    cos, sin = (jnp.asarray(table) for table in rotary_tables())
    (
        cot_all, mid_all, exp_full, att_full, normed, proj, qkv, attended, state, gain_rows,
        head_gains, mask_both, live_both,
    ) = forward(layer_input, cotangent, att, small, exp, mask, live, cos, sin)
    cot_all = cot_all.reshape(ROWS, D)
    w_att = att_full.reshape(D, AW)
    w_small = w_att[:, 1024:]
    normed = normed.reshape(ROWS, D)
    attended = attended.reshape(ROWS, 256)
    mid = mid_all.reshape(ROWS, D)
    w_exp = exp_full.reshape(D, EW)
    head_start = t * 512 + xl * 256
    pre_grad, gated, mid_part, mixed_part, soft, route = experts(
        mid, cot_all, w_exp, w_small, mask_both.reshape(ROWS, 128)
    )
    own_start = xl * SEQ + t * BLK
    soft_own = lax.dynamic_slice_in_dim(soft, own_start, BLK)
    branch_grad, state_grad, mid_gain, logit_grad, near_sum, far_sum = turn(
        mid_part.reshape(2, 2, 2, BLK, D),
        route.reshape(2, 2, 2, BLK, 128),
        mid,
        cot_all,
        pre_grad,
        gated,
        state,
        cotangent,
        soft_own,
        w_small,
        gain_rows,
    )
    bg = branch_grad.reshape(ROWS, D)
    proj_grad, in_part, in_gain, head_gain = attend_back(
        bg, normed, w_att, gain_rows, head_gains, cos, sin, live_both,
        proj.reshape(ROWS, 768), qkv.reshape(ROWS, 768),
    )
    qkv_grad = jnp.einsum("sd,sf->df", normed, proj_grad, preferred_element_type=F32)
    out_grad = jnp.einsum("sd,sf->df", bg, attended, preferred_element_type=F32)
    mid_own = lax.dynamic_slice_in_dim(mid, own_start, BLK)
    router_grad = jnp.dot(
        mid_own.astype(F32).T, logit_grad, precision=lax.Precision.HIGHEST
    )[:, ROUTER_AT : ROUTER_AT + E]
    head_rows = lax.dynamic_update_slice(jnp.zeros((2, D), F32), head_gain[:2], (0, head_start))
    gain_part = jnp.concatenate([in_gain[:1], mid_gain[:1], head_rows]).T
    smalls = jnp.concatenate([gain_part, router_grad], axis=1)
    smalls = jnp.pad(smalls, ((0, 0), (0, 128 - smalls.shape[1])))
    att_grad = jnp.concatenate([qkv_grad, out_grad, smalls], axis=1).astype(BF16)
    input_grad, output, exp_sum, att_sum, small_sum = closing(
        in_part.reshape(2, 2, 2, BLK, D),
        mixed_part.reshape(2, 2, 2, BLK, D),
        near_sum,
        far_sum,
        att_grad.reshape(2, 4, 4, 64, AW),
        state,
        state_grad,
        layer_input,
        gain_rows,
    )

    def in_order(sums):
        return jnp.where(xl == 0, sums, sums[::-1])

    exp_sum = in_order(exp_sum).reshape(2, 64, HALF_E, 3, FFS)
    gate_up_out = exp_sum[:, :, :, :2].transpose(0, 2, 3, 1, 4).reshape(E, 2, 64, FFS)
    down_out = exp_sum[:, :, :, 2].transpose(0, 2, 3, 1).reshape(E, FFS, 64)
    qkv_out = in_order(att_sum[:, :, :768]).reshape(2, 64, 3, 256)
    qkv_out = qkv_out.transpose(2, 1, 0, 3).reshape(3, 64, 512)
    out_out = in_order(att_sum[:, :, 768:1024]).transpose(0, 2, 1).reshape(512, 64)
    gains_out = small_sum[:, :4].T
    router_out = small_sum[:, ROUTER_AT : ROUTER_AT + E]
    return (output, input_grad, gains_out, qkv_out, out_out, router_out, gate_up_out, down_out)


def solution(mesh):
    split = Mesh(mesh.devices.reshape(SIZES), AXES)
    rows, tensor = P(AXES, None), ("xh", "c")
    return jax.shard_map(
        local,
        mesh=split,
        in_specs=(
            rows,
            rows,
            P(DP),
            P(DP, None),
            P(None, AXES),
            P(None, DP, tensor),
            P(tensor, DP),
            rows,
            P(None, None, DP, tensor),
            P(None, tensor, DP),
        ),
        out_specs=(
            rows,
            rows,
            P(None, AXES),
            P(None, DP, tensor),
            P(tensor, DP),
            rows,
            P(None, None, DP, tensor),
            P(None, tensor, DP),
        ),
        check_vma=False,
    )
```

```python
import functools

import jax
import jax.numpy as jnp
import numpy as np
from jax import lax
from jax.experimental import pallas as pl
from jax.experimental.pallas import tpu as pltpu
from jax.sharding import Mesh
from jax.sharding import PartitionSpec as P

HD = 128
TOPK = 8
E = 10
D = 2048
SEQ = 512
ROWS = 1024
BLK = 128
HALF_E = 5
FFS = 256
GU = HALF_E * 2 * FFS
EW = HALF_E * 3 * FFS
AW = 1152
ROUTER_AT = 4
AXES = ("xl", "y", "z", "xh", "c")
SIZES = (2, 4, 4, 2, 2)
DP = ("xl", "y", "z")
EPS = 1e-06
THETA = 10000.0
F32 = jnp.float32
BF16 = jnp.bfloat16
MIB = 1 << 20
LOGICAL = pl.DeviceIdType.MESH
VMEM = pl.BlockSpec(memory_space=pltpu.VMEM)
ANY = pl.BlockSpec(memory_space=pl.ANY)


class Place:
    def __init__(self):
        self.xl, self.y, self.z, self.xh, self.c = (lax.axis_index(a) for a in AXES)
        self.x = self.xh * 2 + self.xl
        self.t = self.xh * 2 + self.c

    def at(self, dx=0, dy=0, dz=0, dc=0):
        x = lax.rem(self.x + (dx + 4), 4)
        return (
            lax.rem(x, 2),
            lax.rem(self.y + (dy + 4), 4),
            lax.rem(self.z + (dz + 4), 4),
            lax.div(x, 2),
            lax.rem(self.c + (dc + 2), 2),
        )

    def chip(self, dx):
        x = lax.rem(self.x + (dx + 4), 4)
        return lax.rem(x, 2), lax.div(x, 2)

    def partner(self):
        return (1 - self.xl, self.y, self.z, self.xh, self.c)


class Wires:
    def __init__(self, send, recv, near):
        self.send, self.recv, self.near = send, recv, near
        self.count, self.near_count = 0, 0

    def to(self, device, src, dst):
        k, self.count = self.count, self.count + 1
        copy = pltpu.make_async_remote_copy(
            src_ref=src,
            dst_ref=dst,
            send_sem=self.send.at[k],
            recv_sem=self.recv.at[k],
            device_id=device,
            device_id_type=LOGICAL,
        )
        copy.start()
        return copy

    def here(self, src, dst):
        k, self.near_count = self.near_count, self.near_count + 1
        copy = pltpu.make_async_copy(src, dst, self.near.at[k])
        copy.start()
        return copy


def wire_scratch(copies, local):
    return [
        pltpu.SemaphoreType.DMA((copies,)),
        pltpu.SemaphoreType.DMA((copies,)),
        pltpu.SemaphoreType.DMA((local,)),
    ]


def greet(devices):
    barrier = pltpu.get_barrier_semaphore()
    for device in devices:
        pl.semaphore_signal(barrier, inc=1, device_id=device, device_id_type=LOGICAL)
    pl.semaphore_wait(barrier, len(devices))


def params(collective_id=None, vmem=56):
    if collective_id is None:
        return pltpu.CompilerParams(vmem_limit_bytes=vmem * MIB)
    return pltpu.CompilerParams(
        collective_id=collective_id, has_side_effects=True, vmem_limit_bytes=vmem * MIB
    )


def each_rows(total, step, body):
    def run(i, carry):
        body(pl.ds(pl.multiple_of(i * step, step), step))
        return carry

    lax.fori_loop(0, total // step, run, 0)


class Spread:
    def __init__(self, wires, place, block, out):
        self.wires, self.place, self.out = wires, place, out
        mine = out.at[place.xl, place.xh, place.c]
        self.up = wires.to(place.at(dx=1), block, mine)
        self.down = wires.to(place.at(dx=3), block, mine)
        self.rest = [wires.to(place.at(dc=1), block, mine)]
        self.local = wires.here(block, mine)

    def of(self, dx):
        xl, xh = self.place.chip(dx)
        return self.out.at[xl, xh, self.place.c]

    def across(self, part):
        self.rest.append(self.wires.to(self.place.at(dc=1), part, part))

    def relay(self):
        self.up.wait_recv()
        low = self.of(-1).at[pl.ds(0, BLK // 2)]
        self.up_relay = self.wires.to(self.place.at(dx=1), low, low)
        self.across(self.of(-1))
        self.down.wait_recv()
        high = self.of(1).at[pl.ds(BLK // 2, BLK // 2)]
        self.down_relay = self.wires.to(self.place.at(dx=3), high, high)
        self.across(self.of(1))

    def forward(self):
        self.up_relay.wait_recv()
        self.across(self.of(2).at[pl.ds(0, BLK // 2)])
        self.down_relay.wait_recv()
        self.across(self.of(2).at[pl.ds(BLK // 2, BLK // 2)])

    def arrived(self):
        self.local.wait()
        for copy in self.rest:
            copy.wait_recv()

    def finish(self):
        for copy in self.rest + [self.up, self.down, self.up_relay, self.down_relay]:
            copy.wait_send()


class Collect:
    def __init__(self, wires, place, parts, got, own, half, arrived):
        self.wires, self.place, self.parts = wires, place, parts
        self.got, self.own, self.half, self.arrived = got, own, half, arrived
        self.swap, self.load, self.far = {}, {}, {}

    def begin(self, steps=(1, 3, 2, 0)):
        for k in steps:
            xl, xh = self.place.chip(k)
            self.swap[k] = self.wires.to(
                self.place.at(dc=1), self.parts.at[xl, xh, 1 - self.place.c], self.got.at[k]
            )
            if self.own is not None:
                self.load[k] = self.wires.here(
                    self.parts.at[xl, xh, self.place.c], self.own.at[k]
                )

    def mine(self, k, rows):
        if self.own is not None:
            return self.own[k, rows]
        xl, xh = self.place.chip(k)
        return self.parts[xl, xh, self.place.c, rows]

    def pass_on(self, steps=(1, 3, 2)):
        for k in steps:
            self.swap[k].wait_recv()
            if self.own is not None:
                self.load[k].wait()

            def add(rows, k=k):
                both = self.mine(k, rows).astype(F32) + self.got[k, rows].astype(F32)
                self.half[k - 1, rows] = both.astype(self.half.dtype)

            each_rows(BLK, 16, add)
            self.far[k] = self.wires.to(
                self.place.at(dx=k), self.half.at[k - 1], self.arrived.at[k - 1]
            )

    def arrive(self):
        self.swap[0].wait_recv()
        if self.own is not None:
            self.load[0].wait()
        for k in (1, 3, 2):
            self.far[k].wait_recv()

    def total(self, rows):
        total = self.mine(0, rows).astype(F32) + self.got[0, rows].astype(F32)
        for k in range(3):
            total = total + self.arrived[k, rows].astype(F32)
        return total

    def finish(self):
        for copy in self.swap.values():
            copy.wait_send()
        for copy in self.far.values():
            copy.wait_send()


def collect_scratch(width, dtype):
    return [
        pltpu.VMEM((4, BLK, width), dtype),
        pltpu.VMEM((4, BLK, width), dtype),
        pltpu.VMEM((3, BLK, width), dtype),
        pltpu.VMEM((3, BLK, width), dtype),
    ]


def dot(a, b, dims=((1,), (0,))):
    return lax.dot_general(a, b, (dims, ((), ())), preferred_element_type=F32)


def turn_half(v):
    return pltpu.roll(v, HD // 2, 1)


def cell_peers(place):
    return [place.at(dx=1), place.at(dx=2), place.at(dx=3), place.at(dc=1)]


def plane_peers(place):
    return [place.at(dy=k) for k in (1, 2, 3)] + [place.at(dz=k) for k in (1, 2, 3)]


def forward_kernel(
    x_own, cot_own, att, small, exp, mask, live, cos, sin,
    cot_all, mid_all, exp_full, att_out, normed_out, proj_out, qkv, attended, state, gains,
    head_gains, mask_both, live_out,
    x_all, att_full, live_both, near_rows, far_rows, normed, proj, branch,
    got, half, arrived, block, send, recv, near,
):
    p = Place()
    w = Wires(send, recv, near)
    greet(cell_peers(p) + plane_peers(p) + [p.at(dx=2, dc=1)])
    xl, y, z, t = p.xl, p.y, p.z, p.t

    rows_t = pl.ds(pl.multiple_of(t * 16, 16), 16)
    mine = att_full.at[xl, y, z]
    small_mine = mine.at[rows_t, pl.ds(1024, 128)]
    smalls = [w.to(p.at(dx=a, dc=b), small, small_mine) for a, b in ((0, 1), (2, 0), (2, 1))]
    att_swap = w.to(p.partner(), att.at[1 - xl], mine.at[:, pl.ds(0, 1024)])
    mine[:, 0:1024] = att[xl]
    mine[rows_t, 1024:1152] = small[...]
    live_both[xl] = live[...]
    for copy in smalls:
        copy.wait_recv()
    strip = mine.at[:, pl.ds(1024, 128)]
    small_swap = w.to(p.partner(), strip, strip)
    att_near = [w.to(p.at(dy=k), mine, mine) for k in (1, 3, 2)]
    att_swap.wait_recv()
    small_swap.wait_recv()
    theirs = att_full.at[1 - xl, y, z]
    att_far = [w.to(p.at(dz=k), theirs, theirs) for k in (1, 3, 2)]
    tokens = Spread(w, p, x_own, x_all)
    masks = [
        w.to(p.partner(), live, live_both.at[xl]),
        w.to(p.partner(), mask, mask_both.at[xl]),
    ]
    local = [w.here(mask, mask_both.at[xl])]
    near_rows[y] = exp[xl]
    for copy in att_near + att_far:
        copy.wait_recv()
    whole = att_full.at[xl, :, z]
    att_up = [w.to(p.at(dz=k), whole, whole) for k in (1, 3)]
    whole = att_full.at[1 - xl, y]
    att_up += [w.to(p.at(dy=k), whole, whole) for k in (1, 3)]
    below, above = lax.rem(z + 3, 4), lax.rem(z + 1, 4)
    left, right = lax.rem(y + 3, 4), lax.rem(y + 1, 4)

    def pass_along(copies, full):
        steps = (
            (p.at(dz=1), full.at[xl, pl.ds(0, 2), below]),
            (p.at(dz=3), full.at[xl, pl.ds(2, 2), above]),
            (p.at(dy=1), full.at[1 - xl, left, pl.ds(0, 2)]),
            (p.at(dy=3), full.at[1 - xl, right, pl.ds(2, 2)]),
        )
        sent = []
        for copy, (device, part) in zip(copies, steps):
            copy.wait_recv()
            sent.append(w.to(device, part, part))
        return sent

    tokens.relay()
    exp_swap = w.to(p.partner(), exp.at[1 - xl], far_rows.at[z])
    att_end = pass_along(att_up, att_full)
    tokens.forward()
    exp_swap.wait_recv()
    cots = Spread(w, p, cot_own, cot_all)
    for copy in att_end:
        copy.wait_recv()
    exp_near = [w.to(p.at(dy=k), exp.at[xl], near_rows.at[y]) for k in (1, 3, 2)]
    exp_far = [w.to(p.at(dz=k), far_rows.at[z], far_rows.at[z]) for k in (1, 3, 2)]
    tokens.arrived()

    for n in range(16):
        column = att_full[n // 8, n % 8 // 2, pl.ds(n % 2 * 2, 2), :, 1024:1152]
        column = jnp.transpose(column.astype(F32).reshape(128, 128))
        gains[:, n * 128 : (n + 1) * 128] = column[:8]
    start = pl.multiple_of(t * 512 + xl * 256, 256)
    head_gains[...] = jnp.zeros_like(head_gains)
    head_gains[0:2] = gains[2:4, pl.ds(start, 256)]
    masks[0].wait_recv()
    local.append(w.here(att_full, att_out))
    local.append(w.here(live_both, live_out))

    sums = Collect(w, p, branch, got, None, half, arrived)

    def project(s):
        for b in range(4):

            def norm(rows, b=b):
                v = x_all[s, b // 2, b % 2, rows].astype(F32)
                scale = lax.rsqrt(jnp.mean(v * v, axis=-1, keepdims=True) + EPS)
                value = (v * scale * gains[0:1]).astype(BF16)
                normed[s, pl.ds(pl.multiple_of(b * BLK + rows.start, 16), 16)] = value

            each_rows(BLK, 16, norm)
        for c in range(3):
            cols = pl.ds(c * 256, 256)
            weight = att_full[:, :, :, :, cols].reshape(D, 256)
            proj[s, :, cols] = dot(normed[s], weight)

    def attend(s):
        for h in range(2):
            for c, factor in ((0, HD ** (-0.5)), (1, 1.0)):
                cols = pl.ds(c * 256 + h * HD, HD)
                v = proj[s, :, cols]
                scale = lax.rsqrt(jnp.mean(v * v, axis=-1, keepdims=True) + EPS)
                v = v * scale * head_gains[c : c + 1, h * HD : (h + 1) * HD]
                v = (v * cos[...] + turn_half(v) * sin[...]) * factor
                qkv[s, :, cols] = v.astype(BF16)
        qkv[s, :, 512:768] = proj[s, :, 512:768].astype(BF16)
        for h in range(2):
            q, k, v = (qkv[s, :, pl.ds(c * 256 + h * HD, HD)] for c in range(3))
            scores = dot(q, k, ((1,), (1,)))
            weights = jnp.exp(scores - jnp.max(scores, axis=-1, keepdims=True))
            weights = weights * live_both[s, 0:1].astype(F32)
            probs = (weights / jnp.sum(weights, axis=-1, keepdims=True)).astype(BF16)
            attended[s, :, pl.ds(h * HD, HD)] = dot(probs, v).astype(BF16)
        for n in range(4):
            weight = att_full[n // 2, pl.ds(n % 2 * 2, 2), :, :, 768:1024].reshape(512, 256)
            part = dot(attended[s], weight, ((1,), (1,))).astype(BF16)
            branch[s, :, :, :, pl.ds(n * 512, 512)] = part.reshape(2, 2, BLK, 512)

    first, second = 1 - xl, xl
    project(first)
    attend(first)
    sums.begin((1, 3))
    project(second)
    cots.relay()
    sums.pass_on((1, 3))
    for copy in exp_near + exp_far:
        copy.wait_recv()
    mine_z = exp_full.at[xl, :, z]
    mine_y = exp_full.at[1 - xl, y]
    exp_up = [w.to(p.at(dz=k), near_rows, mine_z) for k in (1, 3)]
    exp_up += [w.to(p.at(dy=k), far_rows, mine_y) for k in (1, 3)]
    local += [w.here(near_rows, mine_z), w.here(far_rows, mine_y)]
    attend(second)
    sums.begin((2, 0))
    cots.forward()
    local += [w.here(normed, normed_out), w.here(proj, proj_out)]
    sums.pass_on((2,))
    sums.arrive()

    def norm(rows):
        now = x_own[rows].astype(F32) + sums.total(rows)
        state[rows] = now
        scale = lax.rsqrt(jnp.mean(now * now, axis=-1, keepdims=True) + EPS)
        block[rows] = (now * scale * gains[1:2]).astype(BF16)

    each_rows(BLK, 16, norm)
    mids = Spread(w, p, block, mid_all)
    mids.relay()
    exp_end = pass_along(exp_up, exp_full)
    mids.forward()
    mids.arrived()
    cots.arrived()
    for copy in masks[1:]:
        copy.wait_recv()
    for copy in exp_end:
        copy.wait_recv()
    for copy in local:
        copy.wait()
    for group in (tokens, cots, mids, sums):
        group.finish()
    for copy in (
        smalls + [att_swap, small_swap, exp_swap] + masks + att_near + att_far + att_up
        + att_end + exp_near + exp_far + exp_up + exp_end
    ):
        copy.wait_send()


def forward(x_own, cot_own, att, small, exp, mask, live, cos, sin):
    cell = jax.ShapeDtypeStruct((2, 2, 2, BLK, D), BF16)
    return pl.pallas_call(
        forward_kernel,
        name="forward",
        out_shape=[
            cell,
            cell,
            jax.ShapeDtypeStruct((2, 4, 4, 64, EW), BF16),
            jax.ShapeDtypeStruct((2, 4, 4, 64, AW), BF16),
            jax.ShapeDtypeStruct((2, SEQ, D), BF16),
            jax.ShapeDtypeStruct((2, SEQ, 768), F32),
            jax.ShapeDtypeStruct((2, SEQ, 768), BF16),
            jax.ShapeDtypeStruct((2, SEQ, 256), BF16),
            jax.ShapeDtypeStruct((BLK, D), F32),
            jax.ShapeDtypeStruct((8, D), F32),
            jax.ShapeDtypeStruct((8, 256), F32),
            jax.ShapeDtypeStruct((2, SEQ, 128), BF16),
            jax.ShapeDtypeStruct((2, 16, SEQ), BF16),
        ],
        in_specs=[VMEM] * 9,
        out_specs=[ANY] * 6 + [VMEM] * 5 + [ANY] * 2,
        scratch_shapes=[
            pltpu.VMEM((2, 2, 2, BLK, D), BF16),
            pltpu.VMEM((2, 4, 4, 64, AW), BF16),
            pltpu.VMEM((2, 16, SEQ), BF16),
            pltpu.VMEM((4, 64, EW), BF16),
            pltpu.VMEM((4, 64, EW), BF16),
            pltpu.VMEM((2, SEQ, D), BF16),
            pltpu.VMEM((2, SEQ, 768), F32),
            pltpu.VMEM((2, 2, 2, BLK, D), BF16),
            pltpu.VMEM((4, BLK, D), BF16),
            pltpu.VMEM((3, BLK, D), BF16),
            pltpu.VMEM((3, BLK, D), BF16),
            pltpu.VMEM((BLK, D), BF16),
        ]
        + wire_scratch(80, 16),
        compiler_params=params(0, 60),
    )(x_own, cot_own, att, small, exp, mask, live, cos, sin)


def split_dot(value, other, dims):
    high = value.astype(BF16)
    low = (value - high.astype(F32)).astype(BF16)
    dot = functools.partial(
        lax.dot_general, dimension_numbers=(dims, ((), ())), preferred_element_type=F32
    )
    return dot(high, other) + dot(low, other)


def norm_back(value, gain, grad):
    scale = lax.rsqrt(jnp.mean(value * value, axis=-1, keepdims=True) + EPS)
    shaped = grad * gain
    along = jnp.mean(shaped * value, axis=-1, keepdims=True)
    return scale * shaped - value * (scale * scale * scale * along), grad * value * scale


class Reduce:
    def __init__(self, wires, up, down, blocks, here, halves, mains):
        self.wires, self.up, self.down = wires, up, down
        self.blocks, self.here, self.halves, self.mains = blocks, here, halves, mains
        self.first, self.second = {}, {}

    def begin(self, cols):
        opposite = self.blocks(lax.rem(self.here + 2, 4))
        low, high = pl.ds(0, 2), pl.ds(2, 2)
        self.first[cols] = (
            self.wires.to(self.up, opposite.at[low, :, self.span(cols)], self.half(0, cols)),
            self.wires.to(self.down, opposite.at[high, :, self.span(cols)], self.half(1, cols)),
        )

    @staticmethod
    def span(cols):
        return pl.ds(*cols)

    def half(self, side, cols):
        return self.halves.at[side, :, :, self.span(cols)]

    def relay(self, cols):
        span = self.span(cols)
        sent = []
        for side, device in ((0, self.up), (1, self.down)):
            self.first[cols][side].wait_recv()
            block = self.blocks(lax.rem(self.here + (1 if side == 0 else 3), 4))
            for b in range(2):
                at = (side * 2 + b, slice(None), span)
                total = block[at].astype(F32) + self.halves[side, b, :, span].astype(F32)
                block[at] = total.astype(BF16)
            sent.append(
                self.wires.to(device, block.at[:, :, span], self.mains.at[side, :, :, span])
            )
        self.second[cols] = sent

    def total(self, cols, store):
        span = self.span(cols)
        for copy in self.second[cols]:
            copy.wait_recv()
        own = self.blocks(self.here)
        for b in range(4):
            total = own[b, :, span].astype(F32)
            for side in range(2):
                total = total + self.mains[side, b, :, span].astype(F32)
            store(b, span, total)

    def finish(self):
        for copies in list(self.first.values()) + list(self.second.values()):
            for copy in copies:
                copy.wait_send()


def turn_kernel(
    mid_part, route, mid, cot, pre_grad, gated, state, cot_own, soft, small, gains,
    branch_grad, state_grad, gain_grad, logit_grad, near_rows, far_rows,
    got, own, half, arrived, rgot, rown, rhalf, rarrived, from_router, block,
    mid_here, cot_here, pre_here, gated_here, dw, near_half, far_half, near_main, far_main,
    send, recv, near,
):
    p = Place()
    w = Wires(send, recv, near)
    xl, y, z = p.xl, p.y, p.z
    greet(cell_peers(p) + [p.at(dy=1), p.at(dy=3), p.at(dz=1), p.at(dz=3)])
    routes = Collect(w, p, route, rgot, rown, rhalf, rarrived)
    sums = Collect(w, p, mid_part, got, own, half, arrived)
    routes.begin()
    sums.begin()
    loads = [w.here(mid, mid_here), w.here(cot, cot_here)]

    def fetch(e):
        return (
            w.here(pre_grad.at[:, pl.ds(e * 512, 512)], pre_here.at[e % 2]),
            w.here(gated.at[:, pl.ds(e * FFS, FFS)], gated_here.at[e % 2]),
        )

    ready = {0: fetch(0), 1: fetch(1)}
    along_z = Reduce(
        w, p.at(dz=1), p.at(dz=3), lambda k: dw.at[xl, :, k], z, near_half, near_main
    )
    along_y = Reduce(
        w, p.at(dy=1), p.at(dy=3), lambda k: dw.at[1 - xl, k], y, far_half, far_main
    )
    routes.pass_on()
    sums.pass_on()
    for copy in loads:
        copy.wait()
    groups = [(e * 768, 768) for e in range(HALF_E)]
    for e in range(HALF_E):
        for copy in ready[e]:
            copy.wait()
        for n in range(4):
            at = pl.ds(n * 512, 512)
            to = (n // 2, pl.ds(n % 2 * 2, 2))
            grad = dot(mid_here[:, at], pre_here[e % 2], ((0,), (0,)))
            dw[(*to, slice(None), slice(None), pl.ds(e * 768, 512))] = grad.astype(
                BF16
            ).reshape(2, 4, 64, 512)
            grad = dot(cot_here[:, at], gated_here[e % 2], ((0,), (0,)))
            dw[(*to, slice(None), slice(None), pl.ds(e * 768 + 512, 256))] = grad.astype(
                BF16
            ).reshape(2, 4, 64, 256)
        along_z.begin(groups[e])
        along_y.begin(groups[e])
        if e + 2 < HALF_E:
            ready[e + 2] = fetch(e + 2)
        if e > 0:
            along_z.relay(groups[e - 1])
            along_y.relay(groups[e - 1])
    routes.arrive()

    def router(rows):
        chance = soft[rows]
        grad = routes.total(rows)
        grad = chance * (grad - jnp.sum(chance * grad, axis=-1, keepdims=True))
        logit_grad[rows] = grad

    each_rows(BLK, 16, router)
    from_router[...] = split_dot(logit_grad[...], small[...], ((1,), (1,)))
    along_z.relay(groups[-1])
    along_y.relay(groups[-1])
    sums.arrive()
    gain_grad[...] = jnp.zeros_like(gain_grad)

    def back(rows):
        grad = sums.total(rows) + from_router[rows]
        change, gain_part = norm_back(state[rows], gains[1:2], grad)
        total = cot_own[rows].astype(F32) + change
        state_grad[rows] = total
        block[rows] = total.astype(BF16)
        gain_grad[0:1] += jnp.sum(gain_part, axis=0, keepdims=True)

    each_rows(BLK, 16, back)
    tokens = Spread(w, p, block, branch_grad)
    tokens.relay()

    def keep(rows_ref):
        def store(b, span, total):
            rows_ref[b, :, span] = total.astype(BF16)

        return store

    for e in range(HALF_E):
        if e == 3:
            tokens.forward()
        along_z.total(groups[e], keep(near_rows))
        along_y.total(groups[e], keep(far_rows))
    tokens.arrived()
    tokens.finish()
    sums.finish()
    routes.finish()
    along_z.finish()
    along_y.finish()


def turn(mid_part, route, mid, cot, pre_grad, gated, state, cot_own, soft, small, gains):
    part = jax.ShapeDtypeStruct((4, 64, EW), BF16)
    return pl.pallas_call(
        turn_kernel,
        name="turn",
        out_shape=[
            jax.ShapeDtypeStruct((2, 2, 2, BLK, D), BF16),
            jax.ShapeDtypeStruct((BLK, D), F32),
            jax.ShapeDtypeStruct((8, D), F32),
            jax.ShapeDtypeStruct((BLK, 128), F32),
            part,
            part,
        ],
        in_specs=[ANY] * 6 + [VMEM] * 5,
        out_specs=[ANY] + [VMEM] * 5,
        scratch_shapes=collect_scratch(D, BF16)
        + collect_scratch(128, F32)
        + [
            pltpu.VMEM((BLK, D), F32),
            pltpu.VMEM((BLK, D), BF16),
            pltpu.VMEM((ROWS, D), BF16),
            pltpu.VMEM((ROWS, D), BF16),
            pltpu.VMEM((2, ROWS, 512), BF16),
            pltpu.VMEM((2, ROWS, FFS), BF16),
            pltpu.VMEM((2, 4, 4, 64, EW), BF16),
            pltpu.VMEM((2, 2, 64, EW), BF16),
            pltpu.VMEM((2, 2, 64, EW), BF16),
            pltpu.VMEM((2, 4, 64, EW), BF16),
            pltpu.VMEM((2, 4, 64, EW), BF16),
        ]
        + wire_scratch(72, 40),
        compiler_params=params(2, 60),
    )(mid_part, route, mid, cot, pre_grad, gated, state, cot_own, soft, small, gains)


QKV_GROUP = (0, 896)
OUT_GROUP = (896, 256)


def backward_kernel(
    bg_in, w_att_in, normed_in, proj_in, qkv_in, attended_in, mixed, near_rows, far_rows, mid_all,
    logit_grad, mid_gain, state, state_grad, x_own, gains, head_gains, cos, sin, live,
    input_grad, output, exp_sum, att_sum, small_sum,
    bg, w_att, normed, proj, qkv, attended, mid_own, att_bg, proj_grad, in_part, in_gain,
    head_gain, small_rows, attg, near_half, far_half, near_main, far_main,
    got, half, arrived, mgot, mown, mhalf, marrived,
    near_in, far_in, far_sum, att_near, att_far, att_near_end, att_far_end, att_far_sum,
    exp_got, att_got, small_all, small_in, send, recv, near,
):
    p = Place()
    w = Wires(send, recv, near)
    xl, y, z, t = p.xl, p.y, p.z, p.t
    greet(cell_peers(p) + plane_peers(p) + [p.at(dx=2, dc=1)])
    mixes = Collect(w, p, mixed, mgot, mown, mhalf, marrived)
    mixes.begin()
    loads = [
        w.here(a, b)
        for a, b in (
            (bg_in, bg),
            (w_att_in, w_att),
            (attended_in, attended),
            (qkv_in, qkv),
            (proj_in, proj),
            (normed_in, normed),
            (mid_all.at[xl, p.xh, p.c], mid_own),
        )
    ]
    exps = []
    for k in (1, 3, 2):
        to_z, to_y = lax.rem(z + k, 4), lax.rem(y + k, 4)
        exps.append(w.to(p.at(dy=k), near_rows.at[to_y], near_in.at[k - 1]))
        exps.append(w.to(p.at(dz=k), far_rows.at[to_z], far_in.at[k - 1]))
    local = [
        w.here(near_rows.at[y], near_in.at[3]),
        w.here(far_rows.at[z], far_in.at[3]),
    ]
    along_z = Reduce(
        w, p.at(dz=1), p.at(dz=3), lambda k: attg.at[xl, :, k], z, near_half, near_main
    )
    along_y = Reduce(
        w, p.at(dy=1), p.at(dy=3), lambda k: attg.at[1 - xl, k], y, far_half, far_main
    )
    in_gain[...] = jnp.zeros_like(in_gain)
    head_gain[...] = jnp.zeros_like(head_gain)
    for copy in loads[:3]:
        copy.wait()
    for s in range(2):
        att_bg[s] = dot(bg[s], w_att[:, 768:1024]).astype(BF16)
    mixes.pass_on()
    for copy in loads[3:]:
        copy.wait()

    def heads(s):
        for h in range(2):
            head = pl.ds(h * HD, HD)
            q, k, v = (qkv[s, :, pl.ds(c * 256 + h * HD, HD)] for c in range(3))
            scores = dot(q, k, ((1,), (1,)))
            weights = jnp.exp(scores - jnp.max(scores, axis=-1, keepdims=True))
            weights = weights * live[s, 0:1].astype(F32)
            probs = weights / jnp.sum(weights, axis=-1, keepdims=True)
            out_grad = att_bg[s, :, head]
            prob_grad = dot(out_grad, v, ((1,), (1,)))
            inner = jnp.sum(probs * prob_grad, axis=-1, keepdims=True)
            score_grad = (probs * (prob_grad - inner)).astype(BF16)
            value_grad = dot(probs.astype(BF16), out_grad, ((0,), (0,)))
            proj_grad[s, :, pl.ds(512 + h * HD, HD)] = value_grad.astype(BF16)
            both = (
                (0, dot(score_grad, k) * HD ** (-0.5)),
                (1, dot(score_grad, q, ((0,), (0,)))),
            )
            for c, grad in both:
                cols = pl.ds(c * 256 + h * HD, HD)
                grad = grad * cos[...] - turn_half(grad) * sin[...]
                gain = head_gains[c : c + 1, h * HD : (h + 1) * HD]
                change, gain_part = norm_back(proj[s, :, cols], gain, grad)
                proj_grad[s, :, cols] = change.astype(BF16)
                head_gain[c : c + 1, h * HD : (h + 1) * HD] += jnp.sum(
                    gain_part, axis=0, keepdims=True
                )

    def inputs(s):
        for b in range(4):
            rows = pl.ds(b * BLK, BLK)
            part = dot(proj_grad[s, rows], w_att[:, :768], ((1,), (1,)))
            in_part[s, b // 2, b % 2] = part.astype(BF16)
            in_gain[0:1] += jnp.sum(part * normed[s, rows].astype(F32), axis=0, keepdims=True)

    def weight_rows(left, right, at, width):
        for n in range(4):
            cols = pl.ds(n * 512, 512)
            grad = dot(left(0, cols), right(0), ((0,), (0,)))
            grad = grad + dot(left(1, cols), right(1), ((0,), (0,)))
            attg[n // 2, pl.ds(n % 2 * 2, 2), :, :, pl.ds(at, width)] = grad.astype(BF16).reshape(
                2, 4, 64, width
            )

    sums = Collect(w, p, in_part, got, None, half, arrived)
    first, second = 1 - xl, xl
    heads(first)
    inputs(first)
    sums.begin((1, 3))
    weight_rows(lambda s, cols: bg[s, :, cols], lambda s: attended[s], 896, 256)
    along_z.begin(OUT_GROUP)
    along_y.begin(OUT_GROUP)
    sums.pass_on((1, 3))
    heads(second)
    inputs(second)
    sums.begin((2, 0))
    along_z.relay(OUT_GROUP)
    along_y.relay(OUT_GROUP)
    weight_rows(lambda s, cols: normed[s, :, cols], lambda s: proj_grad[s], 0, 768)
    sums.pass_on((2,))

    small_rows[...] = jnp.zeros_like(small_rows)
    small_rows[0:1] = in_gain[0:1] / gains[0:1]
    small_rows[1:2] = mid_gain[0:1]
    start = pl.multiple_of(t * 512 + xl * 256, 256)
    small_rows[2:4, pl.ds(start, 256)] = head_gain[0:2]
    high = logit_grad[...].astype(BF16)
    low = (logit_grad[...] - high.astype(F32)).astype(BF16)
    for n in range(16):
        cols = pl.ds(n * 128, 128)
        strip = dot(mid_own[:, cols], high, ((0,), (0,))) + dot(mid_own[:, cols], low, ((0,), (0,)))
        strip = strip + jnp.transpose(small_rows[:, cols])
        attg[n // 8, n % 8 // 2, pl.ds(n % 2 * 2, 2), :, pl.ds(768, 128)] = strip.astype(
            BF16
        ).reshape(2, 64, 128)
    along_z.begin(QKV_GROUP)
    along_y.begin(QKV_GROUP)

    for copy in local:
        copy.wait()
    for copy in exps:
        copy.wait_recv()

    def exp_far(rows):
        total = far_in[3, rows].astype(F32)
        for k in range(3):
            total = total + far_in[k, rows].astype(F32)
        far_sum[rows] = total.astype(BF16)

    each_rows(64, 16, exp_far)
    exp_swap = w.to(p.partner(), far_sum, exp_got)
    mixes.arrive()

    def finish(rows):
        output[rows] = (state[rows] + mixes.total(rows)).astype(BF16)

    each_rows(BLK, 16, finish)
    along_z.relay(QKV_GROUP)
    along_y.relay(QKV_GROUP)

    def exp_near(rows):
        total = near_in[3, rows].astype(F32)
        for k in range(3):
            total = total + near_in[k, rows].astype(F32)
        exp_sum[xl, rows] = total

    each_rows(64, 16, exp_near)
    sums.arrive()

    def back(rows):
        change, _ = norm_back(x_own[rows].astype(F32), gains[0:1], sums.total(rows))
        input_grad[rows] = state_grad[rows] + change

    each_rows(BLK, 16, back)
    exp_swap.wait_recv()
    exp_sum[1 - xl] = exp_got[...].astype(F32)

    def keep(rows_ref):
        def store(b, span, total):
            rows_ref[b, :, span] = total.astype(BF16)

        return store

    for group in (OUT_GROUP, QKV_GROUP):
        along_z.total(group, keep(att_near))
        along_y.total(group, keep(att_far))
    ends = []
    for k in (1, 3, 2):
        to_z, to_y = lax.rem(z + k, 4), lax.rem(y + k, 4)
        ends.append(w.to(p.at(dz=k), att_far.at[to_z], att_far_end.at[k - 1]))
        ends.append(w.to(p.at(dy=k), att_near.at[to_y], att_near_end.at[k - 1]))
    for copy in ends:
        copy.wait_recv()

    def att_far_add(rows):
        total = att_far[z, rows].astype(F32)
        for k in range(3):
            total = total + att_far_end[k, rows].astype(F32)
        att_far_sum[rows] = total.astype(BF16)

    each_rows(64, 16, att_far_add)
    att_swap = w.to(p.partner(), att_far_sum, att_got)

    def att_near_add(rows):
        total = att_near[y, rows].astype(F32)
        for k in range(3):
            total = total + att_near_end[k, rows].astype(F32)
        att_sum[xl, rows] = total

    each_rows(64, 16, att_near_add)
    att_swap.wait_recv()
    att_sum[1 - xl] = att_got[...].astype(F32)
    small_all[...] = att_sum[0, :, 768:896] + att_sum[1, :, 768:896]
    smalls = []
    for n, (a, b) in enumerate(((0, 1), (2, 0), (2, 1))):
        dest = lax.rem(p.xh + a // 2, 2) * 2 + lax.rem(p.c + b, 2)
        smalls.append(
            w.to(
                p.at(dx=a, dc=b),
                small_all.at[pl.ds(pl.multiple_of(dest * 16, 16), 16)],
                small_in.at[n],
            )
        )
    for copy in smalls:
        copy.wait_recv()
    total = small_all[pl.ds(pl.multiple_of(t * 16, 16), 16)]
    for n in range(3):
        total = total + small_in[n]
    small_sum[...] = total
    for group in (sums, mixes, along_z, along_y):
        group.finish()
    for copy in exps + ends + [exp_swap, att_swap] + smalls:
        copy.wait_send()


def backward(
    bg, w_att, normed, proj, qkv, attended, mixed, near_rows, far_rows, mid_all,
    logit_grad, mid_gain, state, state_grad, x_own, gains, head_gains, cos, sin, live,
):
    return pl.pallas_call(
        backward_kernel,
        name="backward",
        out_shape=[
            jax.ShapeDtypeStruct((BLK, D), F32),
            jax.ShapeDtypeStruct((BLK, D), BF16),
            jax.ShapeDtypeStruct((2, 64, EW), F32),
            jax.ShapeDtypeStruct((2, 64, AW), F32),
            jax.ShapeDtypeStruct((16, 128), F32),
        ],
        in_specs=[ANY] * 10 + [VMEM] * 10,
        out_specs=[VMEM] * 5,
        scratch_shapes=[
            pltpu.VMEM((2, SEQ, D), BF16),
            pltpu.VMEM((D, AW), BF16),
            pltpu.VMEM((2, SEQ, D), BF16),
            pltpu.VMEM((2, SEQ, 768), F32),
            pltpu.VMEM((2, SEQ, 768), BF16),
            pltpu.VMEM((2, SEQ, 256), BF16),
            pltpu.VMEM((BLK, D), BF16),
            pltpu.VMEM((2, SEQ, 256), BF16),
            pltpu.VMEM((2, SEQ, 768), BF16),
            pltpu.VMEM((2, 2, 2, BLK, D), BF16),
            pltpu.VMEM((8, D), F32),
            pltpu.VMEM((8, 256), F32),
            pltpu.VMEM((128, D), F32),
            pltpu.VMEM((2, 4, 4, 64, AW), BF16),
            pltpu.VMEM((2, 2, 64, AW), BF16),
            pltpu.VMEM((2, 2, 64, AW), BF16),
            pltpu.VMEM((2, 4, 64, AW), BF16),
            pltpu.VMEM((2, 4, 64, AW), BF16),
            pltpu.VMEM((4, BLK, D), BF16),
            pltpu.VMEM((3, BLK, D), BF16),
            pltpu.VMEM((3, BLK, D), BF16),
        ]
        + collect_scratch(D, BF16)
        + [
            pltpu.VMEM((4, 64, EW), BF16),
            pltpu.VMEM((4, 64, EW), BF16),
            pltpu.VMEM((64, EW), BF16),
            pltpu.VMEM((4, 64, AW), BF16),
            pltpu.VMEM((4, 64, AW), BF16),
            pltpu.VMEM((3, 64, AW), BF16),
            pltpu.VMEM((3, 64, AW), BF16),
            pltpu.VMEM((64, AW), BF16),
            pltpu.VMEM((64, EW), BF16),
            pltpu.VMEM((64, AW), BF16),
            pltpu.VMEM((64, 128), F32),
            pltpu.VMEM((3, 16, 128), F32),
        ]
        + wire_scratch(64, 20),
        compiler_params=params(3, 62),
    )(
        bg, w_att, normed, proj, qkv, attended, mixed, near_rows, far_rows, mid_all,
        logit_grad, mid_gain, state, state_grad, x_own, gains, head_gains, cos, sin, live,
    )


def whole(shape):
    return pl.BlockSpec(shape, lambda s: (0,) * len(shape), pipeline_mode=pl.Buffered(1))


TILE = 256


def expert_kernel(
    mid, cot, w_exp, small, mask, pre_grad, gated, mid_part, mixed_part, soft, route, acc, acc2
):
    xl = lax.axis_index("xl")
    logits = dot(mid[...], small[...])
    on = mask[...] > 0
    peak = jnp.max(jnp.where(on, logits, -1e30), axis=-1, keepdims=True)
    chance = jnp.where(on, jnp.exp(jnp.where(on, logits - peak, 0.0)), 0.0)
    chance = chance / jnp.maximum(jnp.sum(chance, axis=-1, keepdims=True), 1.0)
    soft[...] = chance
    lane = lax.broadcasted_iota(jnp.int32, (TILE, 128), 1)
    routed = jnp.zeros((TILE, 128), F32)
    for e in range(HALF_E):
        here = lane == ROUTER_AT + xl * HALF_E + e
        gate = jnp.sum(jnp.where(here, chance, 0.0), axis=-1, keepdims=True)
        pre = dot(mid[...], w_exp[:, pl.ds(e * 512, 512)])
        hidden = dot(cot[...], w_exp[:, pl.ds(GU + e * 256, 256)])
        gate_pre, up_pre = pre[:, :FFS], pre[:, FFS:]
        sig = 1.0 / (1.0 + jnp.exp(-gate_pre))
        silu = gate_pre * sig
        inner = (silu * up_pre).astype(BF16).astype(F32)
        routed = jnp.where(here, jnp.sum(inner * hidden, axis=-1, keepdims=True), routed)
        gated[:, pl.ds(e * FFS, FFS)] = (gate * inner).astype(BF16)
        hidden = gate * hidden
        pre_grad[:, pl.ds(e * 512, FFS)] = (
            hidden * up_pre * (sig + silu * (1.0 - sig))
        ).astype(BF16)
        pre_grad[:, pl.ds(e * 512 + FFS, FFS)] = (hidden * silu).astype(BF16)
    route[...] = routed
    for n in range(4):
        rows = pl.ds(n * 512, 512)
        mid_part[:, rows] = dot(pre_grad[...], w_exp[rows, :GU], ((1,), (1,))).astype(BF16)
        mixed_part[:, rows] = dot(gated[...], w_exp[rows, GU:], ((1,), (1,))).astype(BF16)


def experts(mid, cot, w_exp, small, mask):
    def tile(width):
        return pl.BlockSpec((TILE, width), lambda s: (s, 0))

    return pl.pallas_call(
        expert_kernel,
        name="experts",
        grid=(ROWS // TILE,),
        out_shape=[
            jax.ShapeDtypeStruct((ROWS, GU), BF16),
            jax.ShapeDtypeStruct((ROWS, EW - GU), BF16),
            jax.ShapeDtypeStruct((ROWS, D), BF16),
            jax.ShapeDtypeStruct((ROWS, D), BF16),
            jax.ShapeDtypeStruct((ROWS, 128), F32),
            jax.ShapeDtypeStruct((ROWS, 128), F32),
        ],
        in_specs=[tile(D), tile(D), whole((D, EW)), whole((D, 128)), tile(128)],
        out_specs=[tile(GU), tile(EW - GU), tile(D), tile(D), tile(128), tile(128)],
        scratch_shapes=[pltpu.VMEM((8, 128), F32), pltpu.VMEM((8, 128), F32)],
        compiler_params=params(),
        cost_estimate=pl.CostEstimate(
            flops=2 * ROWS * D * 256 * 30, bytes_accessed=40 * MIB, transcendentals=0
        ),
    )(mid, cot, w_exp, small, mask)


def rotary_tables():
    half = HD // 2
    freqs = np.float32(THETA) ** (-(np.arange(half, dtype=np.float32) * np.float32(2.0 / HD)))
    angles = np.arange(SEQ, dtype=np.float32)[:, None] * freqs[None, :].astype(np.float32)
    cos, sin = np.cos(angles), np.sin(angles)
    return (
        np.concatenate([cos, cos], axis=1).astype(np.float32),
        np.concatenate([-sin, sin], axis=1).astype(np.float32),
    )


def local(
    layer_input, cotangent, lengths, expert_ids, gains, w_qkv, w_out, w_router, w_gate_up, w_down
):
    xl, xh, c = (lax.axis_index(a) for a in ("xl", "xh", "c"))
    t = xh * 2 + c

    small = jnp.concatenate([gains.T, w_router], axis=1)
    small = jnp.pad(small, ((0, 0), (0, 128 - small.shape[1])))
    out_rows = w_out.reshape(2, 256, 64).transpose(0, 2, 1)
    qkv_rows = w_qkv.reshape(3, 64, 2, 256).transpose(2, 1, 0, 3).reshape(2, 64, 768)
    att = jnp.concatenate([qkv_rows, out_rows], axis=2)
    exp = jnp.concatenate(
        [
            w_gate_up.reshape(2, HALF_E, 2, 64, FFS).transpose(0, 3, 1, 2, 4).reshape(2, 64, GU),
            w_down.reshape(2, HALF_E, FFS, 64).transpose(0, 3, 1, 2).reshape(2, 64, EW - GU),
        ],
        axis=2,
    )
    on = jnp.arange(SEQ, dtype=jnp.int32) < lengths[0]
    number = jnp.arange(128, dtype=jnp.int32) - ROUTER_AT
    named = jnp.zeros((SEQ, 128), bool)
    for k in range(TOPK):
        named = named | (expert_ids[:, k][:, None] == number[None, :])
    mask = (named & on[:, None]).astype(BF16)
    live = jnp.broadcast_to(on[None, :], (16, SEQ)).astype(BF16)

    cos, sin = (jnp.asarray(table) for table in rotary_tables())
    (
        cot_all, mid_all, exp_full, att_full, normed, proj, qkv, attended, state, gain_rows,
        head_gains, mask_both, live_both,
    ) = forward(layer_input, cotangent, att, small, exp, mask, live, cos, sin)
    cot_all = cot_all.reshape(ROWS, D)
    w_att = att_full.reshape(D, AW)
    w_small = w_att[:, 1024:]
    mid = mid_all.reshape(ROWS, D)
    w_exp = exp_full.reshape(D, EW)
    pre_grad, gated, mid_part, mixed_part, soft, route = experts(
        mid, cot_all, w_exp, w_small, mask_both.reshape(ROWS, 128)
    )
    own_start = xl * SEQ + t * BLK
    soft_own = lax.dynamic_slice_in_dim(soft, own_start, BLK)
    branch_grad, state_grad, mid_gain, logit_grad, near_sum, far_sum = turn(
        mid_part.reshape(2, 2, 2, BLK, D),
        route.reshape(2, 2, 2, BLK, 128),
        mid,
        cot_all,
        pre_grad,
        gated,
        state,
        cotangent,
        soft_own,
        w_small,
        gain_rows,
    )
    input_grad, output, exp_sum, att_sum, small_sum = backward(
        branch_grad.reshape(2, SEQ, D),
        w_att,
        normed,
        proj,
        qkv,
        attended,
        mixed_part.reshape(2, 2, 2, BLK, D),
        near_sum,
        far_sum,
        mid_all,
        logit_grad,
        mid_gain,
        state,
        state_grad,
        layer_input,
        gain_rows,
        head_gains,
        cos,
        sin,
        live_both,
    )
    exp_sum = exp_sum.reshape(2, 64, HALF_E, 3, FFS)
    gate_up_out = exp_sum[:, :, :, :2].transpose(0, 2, 3, 1, 4).reshape(E, 2, 64, FFS)
    down_out = exp_sum[:, :, :, 2].transpose(0, 2, 3, 1).reshape(E, FFS, 64)
    qkv_out = att_sum[:, :, :768].reshape(2, 64, 3, 256)
    qkv_out = qkv_out.transpose(2, 1, 0, 3).reshape(3, 64, 512)
    out_out = att_sum[:, :, 896:].transpose(0, 2, 1).reshape(512, 64)
    gains_out = small_sum[:, :4].T
    router_out = small_sum[:, ROUTER_AT : ROUTER_AT + E]
    return (output, input_grad, gains_out, qkv_out, out_out, router_out, gate_up_out, down_out)


def solution(mesh):
    split = Mesh(mesh.devices.reshape(SIZES), AXES)
    rows, tensor = P(AXES, None), ("xh", "c")
    return jax.shard_map(
        local,
        mesh=split,
        in_specs=(
            rows,
            rows,
            P(DP),
            P(DP, None),
            P(None, AXES),
            P(None, DP, tensor),
            P(tensor, DP),
            rows,
            P(None, None, DP, tensor),
            P(None, tensor, DP),
        ),
        out_specs=(
            rows,
            rows,
            P(None, AXES),
            P(None, DP, tensor),
            P(tensor, DP),
            rows,
            P(None, None, DP, tensor),
            P(None, tensor, DP),
        ),
        check_vma=False,
    )
```

```python
import functools

import jax
import jax.numpy as jnp
import numpy as np
from jax import lax
from jax.experimental import pallas as pl
from jax.experimental.pallas import tpu as pltpu
from jax.sharding import Mesh
from jax.sharding import PartitionSpec as P

HD = 128
TOPK = 8
E = 10
D = 2048
SEQ = 512
ROWS = 1024
BLK = 128
HALF_E = 5
FFS = 256
GU = HALF_E * 2 * FFS
EW = HALF_E * 3 * FFS
AW = 1152
ROUTER_AT = 4
AXES = ("xl", "y", "z", "xh", "c")
SIZES = (2, 4, 4, 2, 2)
DP = ("xl", "y", "z")
EPS = 1e-06
THETA = 10000.0
F32 = jnp.float32
BF16 = jnp.bfloat16
MIB = 1 << 20
LOGICAL = pl.DeviceIdType.MESH
VMEM = pl.BlockSpec(memory_space=pltpu.VMEM)
ANY = pl.BlockSpec(memory_space=pl.ANY)


class Place:
    def __init__(self):
        self.xl, self.y, self.z, self.xh, self.c = (lax.axis_index(a) for a in AXES)
        self.x = self.xh * 2 + self.xl
        self.t = self.xh * 2 + self.c

    def at(self, dx=0, dy=0, dz=0, dc=0):
        x = lax.rem(self.x + (dx + 4), 4)
        return (
            lax.rem(x, 2),
            lax.rem(self.y + (dy + 4), 4),
            lax.rem(self.z + (dz + 4), 4),
            lax.div(x, 2),
            lax.rem(self.c + (dc + 2), 2),
        )

    def chip(self, dx):
        x = lax.rem(self.x + (dx + 4), 4)
        return lax.rem(x, 2), lax.div(x, 2)

    def partner(self):
        return (1 - self.xl, self.y, self.z, self.xh, self.c)


class Wires:
    def __init__(self, send, recv, near):
        self.send, self.recv, self.near = send, recv, near
        self.count, self.near_count = 0, 0

    def to(self, device, src, dst):
        k, self.count = self.count, self.count + 1
        copy = pltpu.make_async_remote_copy(
            src_ref=src,
            dst_ref=dst,
            send_sem=self.send.at[k],
            recv_sem=self.recv.at[k],
            device_id=device,
            device_id_type=LOGICAL,
        )
        copy.start()
        return copy

    def here(self, src, dst):
        k, self.near_count = self.near_count, self.near_count + 1
        copy = pltpu.make_async_copy(src, dst, self.near.at[k])
        copy.start()
        return copy


def wire_scratch(copies, local):
    return [
        pltpu.SemaphoreType.DMA((copies,)),
        pltpu.SemaphoreType.DMA((copies,)),
        pltpu.SemaphoreType.DMA((local,)),
    ]


def greet(devices, meanwhile=None):
    barrier = pltpu.get_barrier_semaphore()
    for device in devices:
        pl.semaphore_signal(barrier, inc=1, device_id=device, device_id_type=LOGICAL)
    if meanwhile is not None:
        meanwhile()
    pl.semaphore_wait(barrier, len(devices))


def params(collective_id=None, vmem=56):
    if collective_id is None:
        return pltpu.CompilerParams(vmem_limit_bytes=vmem * MIB)
    return pltpu.CompilerParams(
        collective_id=collective_id, has_side_effects=True, vmem_limit_bytes=vmem * MIB
    )


def each_rows(total, step, body):
    def run(i, carry):
        body(pl.ds(pl.multiple_of(i * step, step), step))
        return carry

    lax.fori_loop(0, total // step, run, 0)


class Spread:
    def __init__(self, wires, place, block, out):
        self.wires, self.place, self.out = wires, place, out
        mine = out.at[place.xl, place.xh, place.c]
        self.up = wires.to(place.at(dx=1), block, mine)
        self.down = wires.to(place.at(dx=3), block, mine)
        self.rest = [wires.to(place.at(dc=1), block, mine)]
        self.local = wires.here(block, mine)

    def of(self, dx):
        xl, xh = self.place.chip(dx)
        return self.out.at[xl, xh, self.place.c]

    def across(self, part):
        self.rest.append(self.wires.to(self.place.at(dc=1), part, part))

    def relay(self):
        self.up.wait_recv()
        low = self.of(-1).at[pl.ds(0, BLK // 2)]
        self.up_relay = self.wires.to(self.place.at(dx=1), low, low)
        self.across(self.of(-1))
        self.down.wait_recv()
        high = self.of(1).at[pl.ds(BLK // 2, BLK // 2)]
        self.down_relay = self.wires.to(self.place.at(dx=3), high, high)
        self.across(self.of(1))

    def forward(self):
        self.up_relay.wait_recv()
        self.across(self.of(2).at[pl.ds(0, BLK // 2)])
        self.down_relay.wait_recv()
        self.across(self.of(2).at[pl.ds(BLK // 2, BLK // 2)])

    def arrived(self):
        self.local.wait()
        for copy in self.rest:
            copy.wait_recv()

    def finish(self):
        for copy in self.rest + [self.up, self.down, self.up_relay, self.down_relay]:
            copy.wait_send()


class Collect:
    def __init__(self, wires, place, parts, got, own, half, arrived):
        self.wires, self.place, self.parts = wires, place, parts
        self.got, self.own, self.half, self.arrived = got, own, half, arrived
        self.swap, self.load, self.far = {}, {}, {}

    def begin(self, steps=(1, 3, 2, 0)):
        for k in steps:
            xl, xh = self.place.chip(k)
            self.swap[k] = self.wires.to(
                self.place.at(dc=1), self.parts.at[xl, xh, 1 - self.place.c], self.got.at[k]
            )
            if self.own is not None:
                self.load[k] = self.wires.here(
                    self.parts.at[xl, xh, self.place.c], self.own.at[k]
                )

    def mine(self, k, rows):
        if self.own is not None:
            return self.own[k, rows]
        xl, xh = self.place.chip(k)
        return self.parts[xl, xh, self.place.c, rows]

    def pass_on(self, steps=(1, 3, 2)):
        for k in steps:
            self.swap[k].wait_recv()
            if self.own is not None:
                self.load[k].wait()

            def add(rows, k=k):
                both = self.mine(k, rows).astype(F32) + self.got[k, rows].astype(F32)
                self.half[k - 1, rows] = both.astype(self.half.dtype)

            each_rows(BLK, 16, add)
            self.far[k] = self.wires.to(
                self.place.at(dx=k), self.half.at[k - 1], self.arrived.at[k - 1]
            )

    def arrive(self):
        self.swap[0].wait_recv()
        if self.own is not None:
            self.load[0].wait()
        for k in (1, 3, 2):
            self.far[k].wait_recv()

    def total(self, rows):
        total = self.mine(0, rows).astype(F32) + self.got[0, rows].astype(F32)
        for k in range(3):
            total = total + self.arrived[k, rows].astype(F32)
        return total

    def finish(self):
        for copy in self.swap.values():
            copy.wait_send()
        for copy in self.far.values():
            copy.wait_send()


def collect_scratch(width, dtype):
    return [
        pltpu.VMEM((4, BLK, width), dtype),
        pltpu.VMEM((4, BLK, width), dtype),
        pltpu.VMEM((3, BLK, width), dtype),
        pltpu.VMEM((3, BLK, width), dtype),
    ]


def dot(a, b, dims=((1,), (0,))):
    return lax.dot_general(a, b, (dims, ((), ())), preferred_element_type=F32)


def turn_half(v):
    return pltpu.roll(v, HD // 2, 1)


def cell_peers(place):
    return [place.at(dx=1), place.at(dx=2), place.at(dx=3), place.at(dc=1)]


def plane_peers(place):
    return [place.at(dy=k) for k in (1, 2, 3)] + [place.at(dz=k) for k in (1, 2, 3)]


def forward_kernel(
    lengths, x_own, cot_own, w_qkv, w_out, w_gate_up, w_down, gains_own, router_own, ids, cos, sin,
    cot_all, mid_all, exp_full, att_out, normed_out, proj_out, qkv, attended, state, gains,
    head_gains, w_small, mask_both, live_out,
    x_all, att_full, live_both, near_rows, far_rows, normed, proj, branch,
    got, half, arrived, block, att, exp, square, small, mask, live, send, recv, near,
):
    p = Place()
    w = Wires(send, recv, near)

    def arrange():
        square[...] = jnp.zeros_like(square)
        square[0:4, 0:16] = gains_own[...].astype(F32)
        left = jnp.transpose(square[...])[0:16]
        square[0:4] = jnp.zeros((4, 128), F32)
        square[0:16, 0:E] = router_own[...].astype(F32)
        small[...] = (left + pltpu.roll(square[0:16], ROUTER_AT, 1)).astype(BF16)
        for h in range(2):
            for c in range(3):
                att[h, :, c * 256 : (c + 1) * 256] = w_qkv[c, :, h * 256 : (h + 1) * 256]
            att[h, :, 768:1024] = w_out[:, h * 256 : (h + 1) * 256]

    greet(cell_peers(p) + plane_peers(p) + [p.at(dx=2, dc=1)], arrange)
    xl, y, z, t = p.xl, p.y, p.z, p.t

    rows_t = pl.ds(pl.multiple_of(t * 16, 16), 16)
    mine = att_full.at[xl, y, z]
    small_mine = mine.at[rows_t, pl.ds(1024, 128)]
    smalls = [w.to(p.at(dx=a, dc=b), small, small_mine) for a, b in ((0, 1), (2, 0), (2, 1))]
    att_swap = w.to(p.partner(), att.at[1 - xl], mine.at[:, pl.ds(0, 1024)])
    mine[:, 0:1024] = att[xl]
    mine[rows_t, 1024:1152] = small[...]
    length = lengths[0]
    live[...] = (lax.broadcasted_iota(jnp.int32, (16, SEQ), 1) < length).astype(F32).astype(BF16)
    live_both[xl] = live[...]
    number = lax.broadcasted_iota(jnp.int32, (SEQ, 128), 1) - ROUTER_AT
    named = jnp.zeros((SEQ, 128), F32)
    for k in range(TOPK):
        named = jnp.where(ids[:, k : k + 1] == number, 1.0, named)
    on = lax.broadcasted_iota(jnp.int32, (SEQ, 128), 0) < length
    mask[...] = jnp.where(on, named, 0.0).astype(BF16)
    for copy in smalls:
        copy.wait_recv()
    strip = mine.at[:, pl.ds(1024, 128)]
    small_swap = w.to(p.partner(), strip, strip)
    att_near = [w.to(p.at(dy=k), mine, mine) for k in (1, 3, 2)]
    att_swap.wait_recv()
    small_swap.wait_recv()
    theirs = att_full.at[1 - xl, y, z]
    att_far = [w.to(p.at(dz=k), theirs, theirs) for k in (1, 3, 2)]
    tokens = Spread(w, p, x_own, x_all)
    masks = [
        w.to(p.partner(), live, live_both.at[xl]),
        w.to(p.partner(), mask, mask_both.at[xl]),
    ]
    local = [w.here(mask, mask_both.at[xl])]
    for h in range(2):
        for e in range(HALF_E):
            for g in range(2):
                at = (e * 3 + g) * FFS
                exp[h, :, at : at + FFS] = w_gate_up[h * HALF_E + e, g]
            at = (e * 3 + 2) * FFS
            exp[h, :, at : at + FFS] = w_down[h * HALF_E + e]
    near_rows[y] = exp[xl]
    for copy in att_near + att_far:
        copy.wait_recv()
    whole = att_full.at[xl, :, z]
    att_up = [w.to(p.at(dz=k), whole, whole) for k in (1, 3)]
    whole = att_full.at[1 - xl, y]
    att_up += [w.to(p.at(dy=k), whole, whole) for k in (1, 3)]
    below, above = lax.rem(z + 3, 4), lax.rem(z + 1, 4)
    left, right = lax.rem(y + 3, 4), lax.rem(y + 1, 4)

    def pass_along(copies, full):
        steps = (
            (p.at(dz=1), full.at[xl, pl.ds(0, 2), below]),
            (p.at(dz=3), full.at[xl, pl.ds(2, 2), above]),
            (p.at(dy=1), full.at[1 - xl, left, pl.ds(0, 2)]),
            (p.at(dy=3), full.at[1 - xl, right, pl.ds(2, 2)]),
        )
        sent = []
        for copy, (device, part) in zip(copies, steps):
            copy.wait_recv()
            sent.append(w.to(device, part, part))
        return sent

    tokens.relay()
    exp_swap = w.to(p.partner(), exp.at[1 - xl], far_rows.at[z])
    att_end = pass_along(att_up, att_full)
    tokens.forward()
    exp_swap.wait_recv()
    cots = Spread(w, p, cot_own, cot_all)
    for copy in att_end:
        copy.wait_recv()
    exp_near = [w.to(p.at(dy=k), exp.at[xl], near_rows.at[y]) for k in (1, 3, 2)]
    exp_far = [w.to(p.at(dz=k), far_rows.at[z], far_rows.at[z]) for k in (1, 3, 2)]
    tokens.arrived()

    for n in range(16):
        column = att_full[n // 8, n % 8 // 2, pl.ds(n % 2 * 2, 2), :, 1024:1152]
        column = jnp.transpose(column.astype(F32).reshape(128, 128))
        gains[:, n * 128 : (n + 1) * 128] = column[:8]
    start = pl.multiple_of(t * 512 + xl * 256, 256)
    head_gains[...] = jnp.zeros_like(head_gains)
    head_gains[0:2] = gains[2:4, pl.ds(start, 256)]
    w_small[...] = att_full[:, :, :, :, 1024:1152].reshape(D, 128)
    masks[0].wait_recv()
    local.append(w.here(att_full, att_out))
    local.append(w.here(live_both, live_out))

    sums = Collect(w, p, branch, got, None, half, arrived)

    def project(s):
        for b in range(4):

            def norm(rows, b=b):
                v = x_all[s, b // 2, b % 2, rows].astype(F32)
                scale = lax.rsqrt(jnp.mean(v * v, axis=-1, keepdims=True) + EPS)
                value = (v * scale * gains[0:1]).astype(BF16)
                normed[s, pl.ds(pl.multiple_of(b * BLK + rows.start, 16), 16)] = value

            each_rows(BLK, 16, norm)
        for c in range(3):
            cols = pl.ds(c * 256, 256)
            weight = att_full[:, :, :, :, cols].reshape(D, 256)
            proj[s, :, cols] = dot(normed[s], weight)

    def attend(s):
        for h in range(2):
            for c, factor in ((0, HD ** (-0.5)), (1, 1.0)):
                cols = pl.ds(c * 256 + h * HD, HD)
                v = proj[s, :, cols]
                scale = lax.rsqrt(jnp.mean(v * v, axis=-1, keepdims=True) + EPS)
                v = v * scale * head_gains[c : c + 1, h * HD : (h + 1) * HD]
                v = (v * cos[...] + turn_half(v) * sin[...]) * factor
                qkv[s, :, cols] = v.astype(BF16)
        qkv[s, :, 512:768] = proj[s, :, 512:768].astype(BF16)
        for h in range(2):
            q, k, v = (qkv[s, :, pl.ds(c * 256 + h * HD, HD)] for c in range(3))
            scores = dot(q, k, ((1,), (1,)))
            weights = jnp.exp(scores - jnp.max(scores, axis=-1, keepdims=True))
            weights = weights * live_both[s, 0:1].astype(F32)
            probs = (weights / jnp.sum(weights, axis=-1, keepdims=True)).astype(BF16)
            attended[s, :, pl.ds(h * HD, HD)] = dot(probs, v).astype(BF16)
        for n in range(4):
            weight = att_full[n // 2, pl.ds(n % 2 * 2, 2), :, :, 768:1024].reshape(512, 256)
            part = dot(attended[s], weight, ((1,), (1,))).astype(BF16)
            branch[s, :, :, :, pl.ds(n * 512, 512)] = part.reshape(2, 2, BLK, 512)

    first, second = 1 - xl, xl
    project(first)
    attend(first)
    sums.begin((1, 3))
    project(second)
    cots.relay()
    sums.pass_on((1, 3))
    for copy in exp_near + exp_far:
        copy.wait_recv()
    mine_z = exp_full.at[xl, :, z]
    mine_y = exp_full.at[1 - xl, y]
    exp_up = [w.to(p.at(dz=k), near_rows, mine_z) for k in (1, 3)]
    exp_up += [w.to(p.at(dy=k), far_rows, mine_y) for k in (1, 3)]
    local += [w.here(near_rows, mine_z), w.here(far_rows, mine_y)]
    attend(second)
    sums.begin((2, 0))
    cots.forward()
    local += [w.here(normed, normed_out), w.here(proj, proj_out)]
    sums.pass_on((2,))
    sums.arrive()

    def norm(rows):
        now = x_own[rows].astype(F32) + sums.total(rows)
        state[rows] = now
        scale = lax.rsqrt(jnp.mean(now * now, axis=-1, keepdims=True) + EPS)
        block[rows] = (now * scale * gains[1:2]).astype(BF16)

    each_rows(BLK, 16, norm)
    mids = Spread(w, p, block, mid_all)
    mids.relay()
    exp_end = pass_along(exp_up, exp_full)
    mids.forward()
    mids.arrived()
    cots.arrived()
    for copy in masks[1:]:
        copy.wait_recv()
    for copy in exp_end:
        copy.wait_recv()
    for copy in local:
        copy.wait()
    for group in (tokens, cots, mids, sums):
        group.finish()
    for copy in (
        smalls + [att_swap, small_swap, exp_swap] + masks + att_near + att_far + att_up
        + att_end + exp_near + exp_far + exp_up + exp_end
    ):
        copy.wait_send()


def forward(
    lengths, x_own, cot_own, w_qkv, w_out, w_gate_up, w_down, gains, router, ids, cos, sin
):
    cell = jax.ShapeDtypeStruct((2, 2, 2, BLK, D), BF16)
    return pl.pallas_call(
        forward_kernel,
        name="forward",
        out_shape=[
            cell,
            cell,
            jax.ShapeDtypeStruct((2, 4, 4, 64, EW), BF16),
            jax.ShapeDtypeStruct((2, 4, 4, 64, AW), BF16),
            jax.ShapeDtypeStruct((2, SEQ, D), BF16),
            jax.ShapeDtypeStruct((2, SEQ, 768), F32),
            jax.ShapeDtypeStruct((2, SEQ, 768), BF16),
            jax.ShapeDtypeStruct((2, SEQ, 256), BF16),
            jax.ShapeDtypeStruct((BLK, D), F32),
            jax.ShapeDtypeStruct((8, D), F32),
            jax.ShapeDtypeStruct((8, 256), F32),
            jax.ShapeDtypeStruct((D, 128), BF16),
            jax.ShapeDtypeStruct((2, SEQ, 128), BF16),
            jax.ShapeDtypeStruct((2, 16, SEQ), BF16),
        ],
        in_specs=[pl.BlockSpec(memory_space=pltpu.SMEM)] + [VMEM] * 11,
        out_specs=[ANY] * 6 + [VMEM] * 6 + [ANY] * 2,
        scratch_shapes=[
            pltpu.VMEM((2, 2, 2, BLK, D), BF16),
            pltpu.VMEM((2, 4, 4, 64, AW), BF16),
            pltpu.VMEM((2, 16, SEQ), BF16),
            pltpu.VMEM((4, 64, EW), BF16),
            pltpu.VMEM((4, 64, EW), BF16),
            pltpu.VMEM((2, SEQ, D), BF16),
            pltpu.VMEM((2, SEQ, 768), F32),
            pltpu.VMEM((2, 2, 2, BLK, D), BF16),
            pltpu.VMEM((4, BLK, D), BF16),
            pltpu.VMEM((3, BLK, D), BF16),
            pltpu.VMEM((3, BLK, D), BF16),
            pltpu.VMEM((BLK, D), BF16),
            pltpu.VMEM((2, 64, 1024), BF16),
            pltpu.VMEM((2, 64, EW), BF16),
            pltpu.VMEM((128, 128), F32),
            pltpu.VMEM((16, 128), BF16),
            pltpu.VMEM((SEQ, 128), BF16),
            pltpu.VMEM((16, SEQ), BF16),
        ]
        + wire_scratch(80, 16),
        compiler_params=params(0, 60),
    )(lengths, x_own, cot_own, w_qkv, w_out, w_gate_up, w_down, gains, router, ids, cos, sin)


def split_dot(value, other, dims):
    high = value.astype(BF16)
    low = (value - high.astype(F32)).astype(BF16)
    dot = functools.partial(
        lax.dot_general, dimension_numbers=(dims, ((), ())), preferred_element_type=F32
    )
    return dot(high, other) + dot(low, other)


def norm_back(value, gain, grad):
    scale = lax.rsqrt(jnp.mean(value * value, axis=-1, keepdims=True) + EPS)
    shaped = grad * gain
    along = jnp.mean(shaped * value, axis=-1, keepdims=True)
    return scale * shaped - value * (scale * scale * scale * along), grad * value * scale


class Reduce:
    def __init__(self, wires, up, down, blocks, here, halves, mains, stage=None):
        self.wires, self.up, self.down = wires, up, down
        self.blocks, self.here, self.halves, self.mains = blocks, here, halves, mains
        self.stage = stage
        self.first, self.second, self.loading = {}, {}, {}

    def begin(self, group):
        at, to, width = group
        opposite = self.blocks(lax.rem(self.here + 2, 4))
        span = pl.ds(at, width)
        self.first[group] = [
            self.wires.to(
                device,
                opposite.at[pl.ds(side * 2, 2), :, span],
                self.halves.at[side, :, :, pl.ds(to, width)],
            )
            for side, device in ((0, self.up), (1, self.down))
        ]

    def relay(self, group):
        at, to, width = group
        span, wide = pl.ds(at, width), pl.ds(to, width)
        self.second[group] = []
        for side, device in ((0, self.up), (1, self.down)):
            self.first[group][side].wait_recv()
            block = self.blocks(lax.rem(self.here + (1 if side == 0 else 3), 4))
            for b in range(2):
                cell = (side * 2 + b, slice(None), span)
                total = block[cell].astype(F32) + self.halves[side, b, :, wide].astype(F32)
                block[cell] = total.astype(BF16)
            self.second[group].append(
                self.wires.to(device, block.at[:, :, span], self.mains.at[side, :, :, wide])
            )

    def fetch(self, group):
        _, to, width = group
        for copy in self.second[group]:
            copy.wait_recv()
        if self.stage is not None:
            self.loading[group] = self.wires.here(
                self.mains.at[:, :, :, pl.ds(to, width)], self.stage
            )

    def total(self, group, store):
        at, to, width = group
        span, wide = pl.ds(at, width), pl.ds(to, width)
        if self.stage is not None:
            self.loading[group].wait()
        own = self.blocks(self.here)
        for b in range(4):
            total = own[b, :, span].astype(F32)
            for side in range(2):
                if self.stage is not None:
                    total = total + self.stage[side, b].astype(F32)
                else:
                    total = total + self.mains[side, b, :, wide].astype(F32)
            store(b, total)

    def sent(self, group):
        for copy in self.first.pop(group) + self.second.pop(group):
            copy.wait_send()

    def finish(self):
        for group in list(self.first):
            self.sent(group)


TILE = 256
EXPERT = 3 * FFS
SLOTS = 3


def expert_kernel(
    mid, cot, w_exp, mask, small, state, cot_own, gains,
    branch_grad, mixed, near_rows, far_rows, near_main, far_main,
    state_grad, gain_grad, logit_grad,
    mid_here, cot_here, weight, pre_grad, gated, dw, near_half, far_half, near_stage, far_stage,
    mid_part, mix_out, soft, route, got, half, arrived, rgot, rhalf, rarrived, block,
    send, recv, near,
):
    p = Place()
    w = Wires(send, recv, near)
    xl, y, z, t = p.xl, p.y, p.z, p.t

    def fetch(e):
        return w.here(w_exp.at[:, pl.ds(e * EXPERT, EXPERT)], weight.at[e % 2])

    loads = [w.here(mid, mid_here), fetch(0), w.here(cot, cot_here)]
    ready = {0: loads[1], 1: fetch(1)}
    greet(cell_peers(p) + [p.at(dy=1), p.at(dy=3), p.at(dz=1), p.at(dz=3)])
    along_z = Reduce(
        w, p.at(dz=1), p.at(dz=3), lambda k: dw.at[xl, :, k], z,
        near_half, near_main, near_stage,
    )
    along_y = Reduce(
        w, p.at(dy=1), p.at(dy=3), lambda k: dw.at[1 - xl, k], y,
        far_half, far_main, far_stage,
    )
    groups = [(e % SLOTS * EXPERT, e * EXPERT, EXPERT) for e in range(HALF_E)]
    loads[0].wait()
    for n in range(ROWS // TILE):
        rows = pl.ds(n * TILE, TILE)
        logits = dot(mid_here[rows], small[...])
        on = mask[rows] > 0
        peak = jnp.max(jnp.where(on, logits, -1e30), axis=-1, keepdims=True)
        chance = jnp.where(on, jnp.exp(jnp.where(on, logits - peak, 0.0)), 0.0)
        soft[rows] = chance / jnp.maximum(jnp.sum(chance, axis=-1, keepdims=True), 1.0)
    route[...] = jnp.zeros_like(route)
    lane = lax.broadcasted_iota(jnp.int32, (TILE, 128), 1)
    loads[2].wait()

    def expert(e):
        ready[e].wait()
        here = lane == ROUTER_AT + xl * HALF_E + e
        for n in range(ROWS // TILE):
            rows = pl.ds(n * TILE, TILE)
            gate = jnp.sum(jnp.where(here, soft[rows], 0.0), axis=-1, keepdims=True)
            pre = dot(mid_here[rows], weight[e % 2, :, : 2 * FFS])
            hidden = dot(cot_here[rows], weight[e % 2, :, 2 * FFS :])
            gate_pre, up_pre = pre[:, :FFS], pre[:, FFS:]
            sig = 1.0 / (1.0 + jnp.exp(-gate_pre))
            silu = gate_pre * sig
            inner = (silu * up_pre).astype(BF16).astype(F32)
            routed = jnp.where(here, jnp.sum(inner * hidden, axis=-1, keepdims=True), 0.0)
            route[n // 2, n % 2] += routed.reshape(2, BLK, 128)
            gated[rows, pl.ds(e * FFS, FFS)] = (gate * inner).astype(BF16)
            hidden = gate * hidden
            pre_grad[rows, pl.ds(e * 512, FFS)] = (
                hidden * up_pre * (sig + silu * (1.0 - sig))
            ).astype(BF16)
            pre_grad[rows, pl.ds(e * 512 + FFS, FFS)] = (hidden * silu).astype(BF16)

    def weight_grads(e):
        at = groups[e][0]
        for n in range(4):
            cols = pl.ds(n * 512, 512)
            to = (n // 2, pl.ds(n % 2 * 2, 2), slice(None), slice(None))
            grad = dot(mid_here[:, cols], pre_grad[:, pl.ds(e * 512, 512)], ((0,), (0,)))
            dw[(*to, pl.ds(at, 512))] = grad.astype(BF16).reshape(2, 4, 64, 512)
            grad = dot(cot_here[:, cols], gated[:, pl.ds(e * FFS, FFS)], ((0,), (0,)))
            dw[(*to, pl.ds(at + 512, FFS))] = grad.astype(BF16).reshape(2, 4, 64, FFS)
        along_z.begin(groups[e])
        along_y.begin(groups[e])

    def relay(e):
        along_z.relay(groups[e])
        along_y.relay(groups[e])

    def retire(e):
        along_z.fetch(groups[e])
        along_y.fetch(groups[e])
        out = []
        for along, own, rows_out in (
            (along_z, dw.at[xl, :, z], near_rows),
            (along_y, dw.at[1 - xl, y], far_rows),
        ):
            at, to, width = groups[e]
            span = pl.ds(at, width)

            def store(b, total, own=own, span=span):
                own[b, :, span] = total.astype(BF16)

            along.total(groups[e], store)
            out.append(w.here(own.at[:, :, span], rows_out.at[:, :, pl.ds(to, width)]))
            along.sent(groups[e])
        return out

    def rows_fetch(n):
        return [
            w.here(
                w_exp.at[pl.ds(n * TILE, TILE), pl.ds(e * EXPERT, EXPERT)],
                weight.at[(n + 1) % 2, pl.ds(e * TILE, TILE)],
            )
            for e in range(HALF_E)
        ]

    expert(0)
    ready[2] = fetch(2)
    weight_grads(0)
    expert(1)
    ready[3] = fetch(3)
    relay(0)
    weight_grads(1)
    expert(2)
    ready[4] = fetch(4)
    relay(1)
    expert(3)
    chunk = {0: rows_fetch(0)}
    expert(4)
    chunk[1] = rows_fetch(1)
    routes = Collect(w, p, route, rgot, None, rhalf, rarrived)
    routes.begin()
    sums = Collect(w, p, mid_part, got, None, half, arrived)
    chunks = D // TILE
    for n in range(chunks):
        for copy in chunk[n]:
            copy.wait()
        slot = (n + 1) % 2
        for r in range(2):
            total = None
            for e in range(HALF_E):
                part = dot(
                    pre_grad[r * SEQ : (r + 1) * SEQ, e * 512 : (e + 1) * 512],
                    weight[slot, e * TILE : (e + 1) * TILE, :512],
                    ((1,), (1,)),
                )
                total = part if e == 0 else total + part
            mid_part[r, :, :, :, pl.ds(n * TILE, TILE)] = total.astype(BF16).reshape(
                2, 2, BLK, TILE
            )
        if n + 2 < chunks:
            chunk[n + 2] = rows_fetch(n + 2)

    def down_fetch(n):
        return [
            w.here(
                w_exp.at[pl.ds(n * 512, 512), pl.ds(e * EXPERT + 512, FFS)],
                weight.at[(n + 1) % 2, pl.ds(e // 3 * 512, 512), pl.ds(e % 3 * FFS, FFS)],
            )
            for e in range(HALF_E)
        ]

    sums.begin()
    downs = {0: down_fetch(0), 1: down_fetch(1)}
    routes.pass_on()
    weight_grads(2)
    sums.pass_on()
    out = retire(0)
    for copy in out:
        copy.wait()
    weight_grads(3)
    relay(2)
    out = retire(1)
    for copy in out:
        copy.wait()
    weight_grads(4)
    relay(3)
    mixing = {}
    for n in range(4):
        for copy in downs[n]:
            copy.wait()
        for r in range(2):
            if n > 0:
                mixing[n - 1, r].wait()
            total = None
            for e in range(HALF_E):
                at = e // 3 * 512
                part = dot(
                    gated[r * SEQ : (r + 1) * SEQ, e * FFS : (e + 1) * FFS],
                    weight[(n + 1) % 2, at : at + 512, e % 3 * FFS : (e % 3 + 1) * FFS],
                    ((1,), (1,)),
                )
                total = part if e == 0 else total + part
            mix_out[r] = total.astype(BF16)
            mixing[n, r] = w.here(
                mix_out.at[r], mixed.at[pl.ds(r * SEQ, SEQ), pl.ds(n * 512, 512)]
            )
        if n + 2 < 4:
            downs[n + 2] = down_fetch(n + 2)
    routes.arrive()

    def router(rows):
        chance = soft[pl.ds(pl.multiple_of((xl * 4 + t) * BLK + rows.start, 16), 16)]
        grad = routes.total(rows)
        grad = chance * (grad - jnp.sum(chance * grad, axis=-1, keepdims=True))
        logit_grad[rows] = grad

    each_rows(BLK, 16, router)
    state_grad[...] = split_dot(logit_grad[...], small[...], ((1,), (1,)))
    sums.arrive()
    gain_grad[...] = jnp.zeros_like(gain_grad)

    def back(rows):
        grad = sums.total(rows) + state_grad[rows]
        change, gain_part = norm_back(state[rows], gains[1:2], grad)
        total = cot_own[rows].astype(F32) + change
        state_grad[rows] = total
        block[rows] = total.astype(BF16)
        gain_grad[0:1] += jnp.sum(gain_part, axis=0, keepdims=True)

    each_rows(BLK, 16, back)
    tokens = Spread(w, p, block, branch_grad)
    relay(4)
    out = retire(2)
    tokens.relay()
    out += retire(3)
    tokens.forward()
    out += retire(4)
    tokens.arrived()
    for copy in out + [mixing[3, 0], mixing[3, 1]]:
        copy.wait()
    for group in (tokens, sums, routes, along_z, along_y):
        group.finish()


def experts(mid, cot, w_exp, mask, small, state, cot_own, gains):
    part = jax.ShapeDtypeStruct((4, 64, EW), BF16)
    landing = jax.ShapeDtypeStruct((2, 4, 64, EW), BF16)
    return pl.pallas_call(
        expert_kernel,
        name="experts",
        out_shape=[
            jax.ShapeDtypeStruct((2, 2, 2, BLK, D), BF16),
            jax.ShapeDtypeStruct((ROWS, D), BF16),
            part,
            part,
            landing,
            landing,
            jax.ShapeDtypeStruct((BLK, D), F32),
            jax.ShapeDtypeStruct((8, D), F32),
            jax.ShapeDtypeStruct((BLK, 128), F32),
        ],
        in_specs=[ANY] * 3 + [VMEM] * 5,
        out_specs=[ANY] * 6 + [VMEM] * 3,
        scratch_shapes=[
            pltpu.VMEM((ROWS, D), BF16),
            pltpu.VMEM((ROWS, D), BF16),
            pltpu.VMEM((2, D, EXPERT), BF16),
            pltpu.VMEM((ROWS, GU), BF16),
            pltpu.VMEM((ROWS, EW - GU), BF16),
            pltpu.VMEM((2, 4, 4, 64, SLOTS * EXPERT), BF16),
            pltpu.VMEM((2, 2, 64, EW), BF16),
            pltpu.VMEM((2, 2, 64, EW), BF16),
            pltpu.VMEM((2, 4, 64, EXPERT), BF16),
            pltpu.VMEM((2, 4, 64, EXPERT), BF16),
            pltpu.VMEM((2, 2, 2, BLK, D), BF16),
            pltpu.VMEM((2, SEQ, 512), BF16),
            pltpu.VMEM((ROWS, 128), F32),
            pltpu.VMEM((2, 2, 2, BLK, 128), F32),
            pltpu.VMEM((4, BLK, D), BF16),
            pltpu.VMEM((3, BLK, D), BF16),
            pltpu.VMEM((3, BLK, D), BF16),
            pltpu.VMEM((4, BLK, 128), F32),
            pltpu.VMEM((3, BLK, 128), F32),
            pltpu.VMEM((3, BLK, 128), F32),
            pltpu.VMEM((BLK, D), BF16),
        ]
        + wire_scratch(72, 112),
        compiler_params=params(2, 62),
    )(mid, cot, w_exp, mask, small, state, cot_own, gains)


QKV_GROUP = (0, 0, 768)
SMALL_GROUP = (768, 768, 128)
OUT_GROUP = (896, 896, 256)


def backward_kernel(
    bg_in, w_att_in, normed_in, proj_in, qkv_in, attended_in, mixed, near_rows, far_rows, mid_all,
    logit_grad, mid_gain, state, state_grad, x_own, gains, head_gains, cos, sin, live,
    input_grad, output, exp_sum, att_sum, small_sum,
    bg, w_att, normed, proj, qkv, attended, mid_own, att_bg, proj_grad, in_part, in_gain,
    head_gain, small_rows, attg, near_half, far_half, near_main, far_main,
    got, half, arrived, mgot, mown, mhalf, marrived,
    near_in, far_in, far_sum, att_near, att_far, att_near_end, att_far_end, att_far_sum,
    exp_got, att_got, small_all, small_in, send, recv, near,
):
    p = Place()
    w = Wires(send, recv, near)
    xl, y, z, t = p.xl, p.y, p.z, p.t
    greet(cell_peers(p) + plane_peers(p) + [p.at(dx=2, dc=1)])
    mixes = Collect(w, p, mixed, mgot, mown, mhalf, marrived)
    mixes.begin()
    loads = [
        w.here(a, b)
        for a, b in (
            (bg_in, bg),
            (w_att_in, w_att),
            (attended_in, attended),
            (qkv_in, qkv),
            (proj_in, proj),
            (normed_in, normed),
            (mid_all.at[xl, p.xh, p.c], mid_own),
        )
    ]
    exps = []
    for k in (1, 3, 2):
        to_z, to_y = lax.rem(z + k, 4), lax.rem(y + k, 4)
        exps.append(w.to(p.at(dy=k), near_rows.at[to_y], near_in.at[k - 1]))
        exps.append(w.to(p.at(dz=k), far_rows.at[to_z], far_in.at[k - 1]))
    local = [
        w.here(near_rows.at[y], near_in.at[3]),
        w.here(far_rows.at[z], far_in.at[3]),
    ]
    along_z = Reduce(
        w, p.at(dz=1), p.at(dz=3), lambda k: attg.at[xl, :, k], z, near_half, near_main
    )
    along_y = Reduce(
        w, p.at(dy=1), p.at(dy=3), lambda k: attg.at[1 - xl, k], y, far_half, far_main
    )
    in_gain[...] = jnp.zeros_like(in_gain)
    head_gain[...] = jnp.zeros_like(head_gain)
    for copy in loads[:3]:
        copy.wait()
    for s in range(2):
        att_bg[s] = dot(bg[s], w_att[:, 768:1024]).astype(BF16)
    for copy in loads[3:]:
        copy.wait()

    def heads(s):
        for h in range(2):
            head = pl.ds(h * HD, HD)
            q, k, v = (qkv[s, :, pl.ds(c * 256 + h * HD, HD)] for c in range(3))
            scores = dot(q, k, ((1,), (1,)))
            weights = jnp.exp(scores - jnp.max(scores, axis=-1, keepdims=True))
            weights = weights * live[s, 0:1].astype(F32)
            probs = weights / jnp.sum(weights, axis=-1, keepdims=True)
            out_grad = att_bg[s, :, head]
            prob_grad = dot(out_grad, v, ((1,), (1,)))
            inner = jnp.sum(probs * prob_grad, axis=-1, keepdims=True)
            score_grad = (probs * (prob_grad - inner)).astype(BF16)
            value_grad = dot(probs.astype(BF16), out_grad, ((0,), (0,)))
            proj_grad[s, :, pl.ds(512 + h * HD, HD)] = value_grad.astype(BF16)
            both = (
                (0, dot(score_grad, k) * HD ** (-0.5)),
                (1, dot(score_grad, q, ((0,), (0,)))),
            )
            for c, grad in both:
                cols = pl.ds(c * 256 + h * HD, HD)
                grad = grad * cos[...] - turn_half(grad) * sin[...]
                gain = head_gains[c : c + 1, h * HD : (h + 1) * HD]
                change, gain_part = norm_back(proj[s, :, cols], gain, grad)
                proj_grad[s, :, cols] = change.astype(BF16)
                head_gain[c : c + 1, h * HD : (h + 1) * HD] += jnp.sum(
                    gain_part, axis=0, keepdims=True
                )

    def inputs(s):
        for b in range(4):
            rows = pl.ds(b * BLK, BLK)
            part = dot(proj_grad[s, rows], w_att[:, :768], ((1,), (1,)))
            in_part[s, b // 2, b % 2] = part.astype(BF16)
            in_gain[0:1] += jnp.sum(part * normed[s, rows].astype(F32), axis=0, keepdims=True)

    def weight_rows(left, right, at, width):
        for n in range(4):
            cols = pl.ds(n * 512, 512)
            grad = dot(left(0, cols), right(0), ((0,), (0,)))
            grad = grad + dot(left(1, cols), right(1), ((0,), (0,)))
            attg[n // 2, pl.ds(n % 2 * 2, 2), :, :, pl.ds(at, width)] = grad.astype(BF16).reshape(
                2, 4, 64, width
            )

    sums = Collect(w, p, in_part, got, None, half, arrived)
    first, second = 1 - xl, xl
    weight_rows(lambda s, cols: bg[s, :, cols], lambda s: attended[s], 896, 256)
    along_z.begin(OUT_GROUP)
    along_y.begin(OUT_GROUP)
    heads(first)
    mixes.pass_on()
    heads(second)
    along_z.relay(OUT_GROUP)
    along_y.relay(OUT_GROUP)
    weight_rows(lambda s, cols: normed[s, :, cols], lambda s: proj_grad[s], 0, 768)
    along_z.begin(QKV_GROUP)
    along_y.begin(QKV_GROUP)
    inputs(first)
    sums.begin((1, 3))
    inputs(second)
    sums.begin((2, 0))
    sums.pass_on((1, 3, 2))

    small_rows[...] = jnp.zeros_like(small_rows)
    small_rows[0:1] = in_gain[0:1] / gains[0:1]
    small_rows[1:2] = mid_gain[0:1]
    start = pl.multiple_of(t * 512 + xl * 256, 256)
    small_rows[2:4, pl.ds(start, 256)] = head_gain[0:2]
    high = logit_grad[...].astype(BF16)
    low = (logit_grad[...] - high.astype(F32)).astype(BF16)
    for n in range(16):
        cols = pl.ds(n * 128, 128)
        strip = dot(mid_own[:, cols], high, ((0,), (0,))) + dot(mid_own[:, cols], low, ((0,), (0,)))
        strip = strip + jnp.transpose(small_rows[:, cols])
        attg[n // 8, n % 8 // 2, pl.ds(n % 2 * 2, 2), :, pl.ds(768, 128)] = strip.astype(
            BF16
        ).reshape(2, 64, 128)
    along_z.begin(SMALL_GROUP)
    along_y.begin(SMALL_GROUP)
    along_z.relay(QKV_GROUP)
    along_y.relay(QKV_GROUP)

    for copy in local:
        copy.wait()
    for copy in exps:
        copy.wait_recv()

    def exp_far(rows):
        total = far_in[3, rows].astype(F32)
        for k in range(3):
            total = total + far_in[k, rows].astype(F32)
        far_sum[rows] = total.astype(BF16)

    each_rows(64, 16, exp_far)
    exp_swap = w.to(p.partner(), far_sum, exp_got)
    along_z.relay(SMALL_GROUP)
    along_y.relay(SMALL_GROUP)
    mixes.arrive()

    def finish(rows):
        output[rows] = (state[rows] + mixes.total(rows)).astype(BF16)

    each_rows(BLK, 16, finish)

    def exp_near(rows):
        total = near_in[3, rows].astype(F32)
        for k in range(3):
            total = total + near_in[k, rows].astype(F32)
        exp_sum[xl, rows] = total

    each_rows(64, 16, exp_near)
    for group in (OUT_GROUP, QKV_GROUP, SMALL_GROUP):
        for along, rows_ref in ((along_z, att_near), (along_y, att_far)):

            def store(b, total, rows_ref=rows_ref, group=group):
                rows_ref[b, :, pl.ds(group[1], group[2])] = total.astype(BF16)

            along.fetch(group)
            along.total(group, store)
    ends = []
    for k in (1, 3, 2):
        to_z, to_y = lax.rem(z + k, 4), lax.rem(y + k, 4)
        ends.append(w.to(p.at(dz=k), att_far.at[to_z], att_far_end.at[k - 1]))
        ends.append(w.to(p.at(dy=k), att_near.at[to_y], att_near_end.at[k - 1]))
    sums.arrive()

    def back(rows):
        change, _ = norm_back(x_own[rows].astype(F32), gains[0:1], sums.total(rows))
        input_grad[rows] = state_grad[rows] + change

    each_rows(BLK, 16, back)
    exp_swap.wait_recv()
    exp_sum[1 - xl] = exp_got[...].astype(F32)

    for copy in ends:
        copy.wait_recv()

    def att_far_add(rows):
        total = att_far[z, rows].astype(F32)
        for k in range(3):
            total = total + att_far_end[k, rows].astype(F32)
        att_far_sum[rows] = total.astype(BF16)

    each_rows(64, 16, att_far_add)
    att_swap = w.to(p.partner(), att_far_sum, att_got)

    def att_near_add(rows):
        total = att_near[y, rows].astype(F32)
        for k in range(3):
            total = total + att_near_end[k, rows].astype(F32)
        att_sum[xl, rows] = total

    each_rows(64, 16, att_near_add)
    att_swap.wait_recv()
    att_sum[1 - xl] = att_got[...].astype(F32)
    small_all[...] = att_sum[0, :, 768:896] + att_sum[1, :, 768:896]
    smalls = []
    for n, (a, b) in enumerate(((0, 1), (2, 0), (2, 1))):
        dest = lax.rem(p.xh + a // 2, 2) * 2 + lax.rem(p.c + b, 2)
        smalls.append(
            w.to(
                p.at(dx=a, dc=b),
                small_all.at[pl.ds(pl.multiple_of(dest * 16, 16), 16)],
                small_in.at[n],
            )
        )
    for copy in smalls:
        copy.wait_recv()
    total = small_all[pl.ds(pl.multiple_of(t * 16, 16), 16)]
    for n in range(3):
        total = total + small_in[n]
    small_sum[...] = total
    for group in (sums, mixes, along_z, along_y):
        group.finish()
    for copy in exps + ends + [exp_swap, att_swap] + smalls:
        copy.wait_send()


def backward(
    bg, w_att, normed, proj, qkv, attended, mixed, near_rows, far_rows, mid_all,
    logit_grad, mid_gain, state, state_grad, x_own, gains, head_gains, cos, sin, live,
):
    return pl.pallas_call(
        backward_kernel,
        name="backward",
        out_shape=[
            jax.ShapeDtypeStruct((BLK, D), F32),
            jax.ShapeDtypeStruct((BLK, D), BF16),
            jax.ShapeDtypeStruct((2, 64, EW), F32),
            jax.ShapeDtypeStruct((2, 64, AW), F32),
            jax.ShapeDtypeStruct((16, 128), F32),
        ],
        in_specs=[ANY] * 10 + [VMEM] * 10,
        out_specs=[VMEM] * 5,
        scratch_shapes=[
            pltpu.VMEM((2, SEQ, D), BF16),
            pltpu.VMEM((D, AW), BF16),
            pltpu.VMEM((2, SEQ, D), BF16),
            pltpu.VMEM((2, SEQ, 768), F32),
            pltpu.VMEM((2, SEQ, 768), BF16),
            pltpu.VMEM((2, SEQ, 256), BF16),
            pltpu.VMEM((BLK, D), BF16),
            pltpu.VMEM((2, SEQ, 256), BF16),
            pltpu.VMEM((2, SEQ, 768), BF16),
            pltpu.VMEM((2, 2, 2, BLK, D), BF16),
            pltpu.VMEM((8, D), F32),
            pltpu.VMEM((8, 256), F32),
            pltpu.VMEM((128, D), F32),
            pltpu.VMEM((2, 4, 4, 64, AW), BF16),
            pltpu.VMEM((2, 2, 64, AW), BF16),
            pltpu.VMEM((2, 2, 64, AW), BF16),
            pltpu.VMEM((2, 4, 64, AW), BF16),
            pltpu.VMEM((2, 4, 64, AW), BF16),
            pltpu.VMEM((4, BLK, D), BF16),
            pltpu.VMEM((3, BLK, D), BF16),
            pltpu.VMEM((3, BLK, D), BF16),
        ]
        + collect_scratch(D, BF16)
        + [
            pltpu.VMEM((4, 64, EW), BF16),
            pltpu.VMEM((4, 64, EW), BF16),
            pltpu.VMEM((64, EW), BF16),
            pltpu.VMEM((4, 64, AW), BF16),
            pltpu.VMEM((4, 64, AW), BF16),
            pltpu.VMEM((3, 64, AW), BF16),
            pltpu.VMEM((3, 64, AW), BF16),
            pltpu.VMEM((64, AW), BF16),
            pltpu.VMEM((64, EW), BF16),
            pltpu.VMEM((64, AW), BF16),
            pltpu.VMEM((64, 128), F32),
            pltpu.VMEM((3, 16, 128), F32),
        ]
        + wire_scratch(64, 20),
        compiler_params=params(3, 62),
    )(
        bg, w_att, normed, proj, qkv, attended, mixed, near_rows, far_rows, mid_all,
        logit_grad, mid_gain, state, state_grad, x_own, gains, head_gains, cos, sin, live,
    )


def finish_kernel(
    input_grad, output, exp_sum, att_sum, small_sum,
    output_out, input_out, gains_out, qkv_out, out_out, router_out, gate_up_out, down_out,
):
    output_out[...] = output[...]
    input_out[...] = input_grad[...]
    gains_out[...] = jnp.transpose(small_sum[...])[:4]
    router_out[...] = pltpu.roll(small_sum[...], 128 - ROUTER_AT, 1)[:, :E]
    for h in range(2):
        for c in range(3):
            qkv_out[c, :, h * 256 : (h + 1) * 256] = att_sum[h, :, c * 256 : (c + 1) * 256]
        out_out[:, h * 256 : (h + 1) * 256] = att_sum[h, :, 896:1152]
        for e in range(HALF_E):
            for g in range(2):
                at = (e * 3 + g) * FFS
                gate_up_out[h * HALF_E + e, g] = exp_sum[h, :, at : at + FFS]
            at = (e * 3 + 2) * FFS
            down_out[h * HALF_E + e] = exp_sum[h, :, at : at + FFS]


def finish(input_grad, output, exp_sum, att_sum, small_sum):
    return pl.pallas_call(
        finish_kernel,
        name="finish",
        out_shape=[
            jax.ShapeDtypeStruct((BLK, D), BF16),
            jax.ShapeDtypeStruct((BLK, D), F32),
            jax.ShapeDtypeStruct((4, 16), F32),
            jax.ShapeDtypeStruct((3, 64, 512), F32),
            jax.ShapeDtypeStruct((64, 512), F32),
            jax.ShapeDtypeStruct((16, E), F32),
            jax.ShapeDtypeStruct((E, 2, 64, FFS), F32),
            jax.ShapeDtypeStruct((E, 64, FFS), F32),
        ],
        in_specs=[VMEM] * 5,
        out_specs=[VMEM] * 8,
        compiler_params=params(),
    )(input_grad, output, exp_sum, att_sum, small_sum)


def rotary_tables():
    half = HD // 2
    freqs = np.float32(THETA) ** (-(np.arange(half, dtype=np.float32) * np.float32(2.0 / HD)))
    angles = np.arange(SEQ, dtype=np.float32)[:, None] * freqs[None, :].astype(np.float32)
    cos, sin = np.cos(angles), np.sin(angles)
    return (
        np.concatenate([cos, cos], axis=1).astype(np.float32),
        np.concatenate([-sin, sin], axis=1).astype(np.float32),
    )


def local(
    layer_input, cotangent, lengths, expert_ids, gains, w_qkv, w_out, w_router, w_gate_up, w_down
):
    cos, sin = (jnp.asarray(table) for table in rotary_tables())
    (
        cot_all, mid_all, exp_full, att_full, normed, proj, qkv, attended, state, gain_rows,
        head_gains, w_small, mask_both, live_both,
    ) = forward(
        lengths, layer_input, cotangent, w_qkv, w_out.T, w_gate_up, w_down.transpose(0, 2, 1),
        gains, w_router, expert_ids, cos, sin,
    )
    cot_all = cot_all.reshape(ROWS, D)
    w_att = att_full.reshape(D, AW)
    mid = mid_all.reshape(ROWS, D)
    w_exp = exp_full.reshape(D, EW)
    branch_grad, mixed, near_sum, far_sum, _, _, state_grad, mid_gain, logit_grad = experts(
        mid, cot_all, w_exp, mask_both.reshape(ROWS, 128), w_small, state, cotangent, gain_rows
    )
    input_grad, output, exp_sum, att_sum, small_sum = backward(
        branch_grad.reshape(2, SEQ, D),
        w_att,
        normed,
        proj,
        qkv,
        attended,
        mixed.reshape(2, 2, 2, BLK, D),
        near_sum,
        far_sum,
        mid_all,
        logit_grad,
        mid_gain,
        state,
        state_grad,
        layer_input,
        gain_rows,
        head_gains,
        cos,
        sin,
        live_both,
    )
    results = finish(input_grad, output, exp_sum, att_sum, small_sum)
    output, input_grad, gains_out, qkv_out, out_out, router_out, gate_up_out, down_out = results
    down_out = down_out.transpose(0, 2, 1)
    return (
        output, input_grad, gains_out, qkv_out, out_out.T, router_out, gate_up_out, down_out
    )


def solution(mesh):
    split = Mesh(mesh.devices.reshape(SIZES), AXES)
    rows, tensor = P(AXES, None), ("xh", "c")
    return jax.shard_map(
        local,
        mesh=split,
        in_specs=(
            rows,
            rows,
            P(DP),
            P(DP, None),
            P(None, AXES),
            P(None, DP, tensor),
            P(tensor, DP),
            rows,
            P(None, None, DP, tensor),
            P(None, tensor, DP),
        ),
        out_specs=(
            rows,
            rows,
            P(None, AXES),
            P(None, DP, tensor),
            P(tensor, DP),
            rows,
            P(None, None, DP, tensor),
            P(None, tensor, DP),
        ),
        check_vma=False,
    )
```

```python
import functools

import jax
import jax.numpy as jnp
import numpy as np
from jax import lax
from jax.experimental import pallas as pl
from jax.experimental.pallas import tpu as pltpu
from jax.sharding import Mesh
from jax.sharding import PartitionSpec as P

HD = 128
TOPK = 8
E = 10
D = 2048
SEQ = 512
ROWS = 1024
BLK = 128
HALF_E = 5
FFS = 256
GU = HALF_E * 2 * FFS
EW = HALF_E * 3 * FFS
AW = 1152
KEPT = 4 * 3 * FFS
ROUTER_AT = 4
AXES = ("xl", "y", "z", "xh", "c")
SIZES = (2, 4, 4, 2, 2)
DP = ("xl", "y", "z")
EPS = 1e-06
THETA = 10000.0
F32 = jnp.float32
BF16 = jnp.bfloat16
MIB = 1 << 20
LOGICAL = pl.DeviceIdType.MESH
VMEM = pl.BlockSpec(memory_space=pltpu.VMEM)
ANY = pl.BlockSpec(memory_space=pl.ANY)


class Place:
    def __init__(self):
        self.xl, self.y, self.z, self.xh, self.c = (lax.axis_index(a) for a in AXES)
        self.x = self.xh * 2 + self.xl
        self.t = self.xh * 2 + self.c

    def at(self, dx=0, dy=0, dz=0, dc=0):
        x = lax.rem(self.x + (dx + 4), 4)
        return (
            lax.rem(x, 2),
            lax.rem(self.y + (dy + 4), 4),
            lax.rem(self.z + (dz + 4), 4),
            lax.div(x, 2),
            lax.rem(self.c + (dc + 2), 2),
        )

    def chip(self, dx):
        x = lax.rem(self.x + (dx + 4), 4)
        return lax.rem(x, 2), lax.div(x, 2)

    def partner(self):
        return (1 - self.xl, self.y, self.z, self.xh, self.c)


class Wires:
    def __init__(self, send, recv, near):
        self.send, self.recv, self.near = send, recv, near
        self.count, self.near_count = 0, 0

    def to(self, device, src, dst):
        k, self.count = self.count, self.count + 1
        copy = pltpu.make_async_remote_copy(
            src_ref=src,
            dst_ref=dst,
            send_sem=self.send.at[k],
            recv_sem=self.recv.at[k],
            device_id=device,
            device_id_type=LOGICAL,
        )
        copy.start()
        return copy

    def here(self, src, dst):
        k, self.near_count = self.near_count, self.near_count + 1
        copy = pltpu.make_async_copy(src, dst, self.near.at[k])
        copy.start()
        return copy


def wire_scratch(copies, local):
    return [
        pltpu.SemaphoreType.DMA((copies,)),
        pltpu.SemaphoreType.DMA((copies,)),
        pltpu.SemaphoreType.DMA((local,)),
    ]


def greet(devices, meanwhile=None):
    barrier = pltpu.get_barrier_semaphore()
    for device in devices:
        pl.semaphore_signal(barrier, inc=1, device_id=device, device_id_type=LOGICAL)
    if meanwhile is not None:
        meanwhile()
    pl.semaphore_wait(barrier, len(devices))


def params(collective_id=None, vmem=56):
    if collective_id is None:
        return pltpu.CompilerParams(vmem_limit_bytes=vmem * MIB)
    return pltpu.CompilerParams(
        collective_id=collective_id, has_side_effects=True, vmem_limit_bytes=vmem * MIB
    )


def each_rows(total, step, body):
    def run(i, carry):
        body(pl.ds(pl.multiple_of(i * step, step), step))
        return carry

    lax.fori_loop(0, total // step, run, 0)


class Spread:
    def __init__(self, wires, place, block, out):
        self.wires, self.place, self.out = wires, place, out
        mine = out.at[place.xl, place.xh, place.c]
        self.up = wires.to(place.at(dx=1), block, mine)
        self.down = wires.to(place.at(dx=3), block, mine)
        self.rest = [wires.to(place.at(dc=1), block, mine)]
        self.local = wires.here(block, mine)

    def of(self, dx):
        xl, xh = self.place.chip(dx)
        return self.out.at[xl, xh, self.place.c]

    def across(self, part):
        self.rest.append(self.wires.to(self.place.at(dc=1), part, part))

    def relay(self):
        self.up.wait_recv()
        low = self.of(-1).at[pl.ds(0, BLK // 2)]
        self.up_relay = self.wires.to(self.place.at(dx=1), low, low)
        self.across(self.of(-1))
        self.down.wait_recv()
        high = self.of(1).at[pl.ds(BLK // 2, BLK // 2)]
        self.down_relay = self.wires.to(self.place.at(dx=3), high, high)
        self.across(self.of(1))

    def forward(self):
        self.up_relay.wait_recv()
        self.across(self.of(2).at[pl.ds(0, BLK // 2)])
        self.down_relay.wait_recv()
        self.across(self.of(2).at[pl.ds(BLK // 2, BLK // 2)])

    def arrived(self):
        self.local.wait()
        for copy in self.rest:
            copy.wait_recv()

    def finish(self):
        for copy in self.rest + [self.up, self.down, self.up_relay, self.down_relay]:
            copy.wait_send()


class Collect:
    def __init__(self, wires, place, parts, got, own, half, arrived, across):
        self.wires, self.place, self.parts = wires, place, parts
        self.got, self.own, self.half, self.arrived = got, own, half, arrived
        self.across = across
        self.swap, self.load, self.sent = {}, {}, []
        self.low, self.high = pl.ds(0, BLK // 2), pl.ds(BLK // 2, BLK // 2)

    def begin(self, steps=(2, 1, 3, 0)):
        for k in steps:
            xl, xh = self.place.chip(k)
            self.swap[k] = self.wires.to(
                self.place.at(dc=1), self.parts.at[xl, xh, 1 - self.place.c], self.got.at[k]
            )
            if self.own is not None:
                self.load[k] = self.wires.here(
                    self.parts.at[xl, xh, self.place.c], self.own.at[k]
                )

    def ready(self, k):
        self.swap[k].wait_recv()
        if self.own is not None:
            self.load[k].wait()

    def mine(self, k, rows):
        if self.own is not None:
            return self.own[k, rows]
        xl, xh = self.place.chip(k)
        return self.parts[xl, xh, self.place.c, rows]

    def add(self, k, start, size, also=None):
        def run(rows):
            rows = pl.ds(pl.multiple_of(start + rows.start, 16), 16)
            both = self.mine(k, rows).astype(F32) + self.got[k, rows].astype(F32)
            if also is not None:
                beside = pl.ds(pl.multiple_of(rows.start - start, 16), 16)
                both = both + self.across[also, beside].astype(F32)
            self.half[k - 1, rows] = both.astype(self.half.dtype)

        each_rows(size, 16, run)

    def start(self):
        self.ready(2)
        self.add(2, 0, BLK)
        self.via = [
            self.wires.to(self.place.at(dx=1), self.half.at[1, self.low], self.across.at[0]),
            self.wires.to(self.place.at(dx=3), self.half.at[1, self.high], self.across.at[1]),
        ]

    def ahead(self):
        for k, side, rows in ((1, 0, self.high), (3, 1, self.low)):
            self.ready(k)
            self.add(k, rows.start, BLK // 2)
            self.send(k, side, rows)

    def pass_on(self):
        for k, side, rows in ((1, 0, self.low), (3, 1, self.high)):
            self.via[side].wait_recv()
            self.add(k, rows.start, BLK // 2, side)
            self.send(k, side, rows)

    def send(self, k, side, rows):
        self.sent.append(
            self.wires.to(
                self.place.at(dx=k), self.half.at[k - 1, rows], self.arrived.at[side, rows]
            )
        )

    def arrive(self):
        self.ready(0)
        for copy in self.sent:
            copy.wait_recv()

    def total(self, rows):
        total = self.mine(0, rows).astype(F32) + self.got[0, rows].astype(F32)
        for side in range(2):
            total = total + self.arrived[side, rows].astype(F32)
        return total

    def finish(self):
        for copy in list(self.swap.values()) + self.via + self.sent:
            copy.wait_send()


def collect_scratch(width, dtype, own):
    block = pltpu.VMEM((4, BLK, width), dtype)
    return [block] * (2 if own else 1) + [
        pltpu.VMEM((3, BLK, width), dtype),
        pltpu.VMEM((2, BLK, width), dtype),
        pltpu.VMEM((2, BLK // 2, width), dtype),
    ]


def dot(a, b, dims=((1,), (0,))):
    return lax.dot_general(a, b, (dims, ((), ())), preferred_element_type=F32)


def turn_half(v):
    return pltpu.roll(v, HD // 2, 1)


def cell_peers(place):
    return [place.at(dx=1), place.at(dx=2), place.at(dx=3), place.at(dc=1)]


def plane_peers(place):
    return [place.at(dy=k) for k in (1, 2, 3)] + [place.at(dz=k) for k in (1, 2, 3)]


def forward_kernel(
    lengths, x_own, cot_own, w_qkv, w_out, w_gate_up, w_down, gains_own, router_own, ids, cos, sin,
    cot_all, mid_all, exp_full, near_last, far_last, att_out, normed_out, proj_out, qkv, attended, state, gains,
    head_gains, w_small, mask_both, live_out,
    x_all, att_full, live_both, near_rows, far_rows, normed, proj, branch,
    got, half, arrived, across, block, att, exp, square, small, mask, live, send, recv, near,
):
    p = Place()
    w = Wires(send, recv, near)

    def arrange():
        square[...] = jnp.zeros_like(square)
        square[0:4, 0:16] = gains_own[...].astype(F32)
        left = jnp.transpose(square[...])[0:16]
        square[0:4] = jnp.zeros((4, 128), F32)
        square[0:16, 0:E] = router_own[...].astype(F32)
        small[...] = (left + pltpu.roll(square[0:16], ROUTER_AT, 1)).astype(BF16)
        for h in range(2):
            for c in range(3):
                att[h, :, c * 256 : (c + 1) * 256] = w_qkv[c, :, h * 256 : (h + 1) * 256]
            att[h, :, 768:1024] = w_out[:, h * 256 : (h + 1) * 256]

    greet(cell_peers(p) + plane_peers(p) + [p.at(dx=2, dc=1)], arrange)
    xl, y, z, t = p.xl, p.y, p.z, p.t

    rows_t = pl.ds(pl.multiple_of(t * 16, 16), 16)
    mine = att_full.at[xl, y, z]
    small_mine = mine.at[rows_t, pl.ds(1024, 128)]
    smalls = [w.to(p.at(dx=a, dc=b), small, small_mine) for a, b in ((0, 1), (2, 0), (2, 1))]
    att_swap = w.to(p.partner(), att.at[1 - xl], mine.at[:, pl.ds(0, 1024)])
    mine[:, 0:1024] = att[xl]
    mine[rows_t, 1024:1152] = small[...]
    body, side = pl.ds(0, 1024), pl.ds(1024, 128)
    att_near = [w.to(p.at(dy=k), mine.at[:, body], mine.at[:, body]) for k in (1, 3, 2)]
    length = lengths[0]
    live[...] = (lax.broadcasted_iota(jnp.int32, (16, SEQ), 1) < length).astype(F32).astype(BF16)
    live_both[xl] = live[...]
    theirs = att_full.at[1 - xl, y, z]
    att_swap.wait_recv()
    att_far = [w.to(p.at(dz=k), theirs.at[:, body], theirs.at[:, body]) for k in (1, 3, 2)]
    for copy in smalls:
        copy.wait_recv()
    strip = mine.at[:, side]
    small_swap = w.to(p.partner(), strip, strip)
    att_near += [w.to(p.at(dy=k), strip, strip) for k in (1, 3, 2)]
    number = lax.broadcasted_iota(jnp.int32, (SEQ, 128), 1) - ROUTER_AT
    named = jnp.zeros((SEQ, 128), F32)
    for k in range(TOPK):
        named = jnp.where(ids[:, k : k + 1] == number, 1.0, named)
    on = lax.broadcasted_iota(jnp.int32, (SEQ, 128), 0) < length
    mask[...] = jnp.where(on, named, 0.0).astype(BF16)
    small_swap.wait_recv()
    strip = theirs.at[:, side]
    att_far += [w.to(p.at(dz=k), strip, strip) for k in (1, 3, 2)]
    tokens = Spread(w, p, x_own, x_all)
    masks = [
        w.to(p.partner(), live, live_both.at[xl]),
        w.to(p.partner(), mask, mask_both.at[xl]),
    ]
    local = [w.here(mask, mask_both.at[xl])]
    for h in range(2):
        for e in range(HALF_E):
            for g in range(2):
                at = (e * 3 + g) * FFS
                exp[h, :, at : at + FFS] = w_gate_up[h * HALF_E + e, g]
            at = (e * 3 + 2) * FFS
            exp[h, :, at : at + FFS] = w_down[h * HALF_E + e]
    near_rows[y] = exp[xl]
    for copy in att_near + att_far:
        copy.wait_recv()
    whole = att_full.at[xl, :, z]
    att_up = [w.to(p.at(dz=k), whole, whole) for k in (1, 3)]
    whole = att_full.at[1 - xl, y]
    att_up += [w.to(p.at(dy=k), whole, whole) for k in (1, 3)]
    below, above = lax.rem(z + 3, 4), lax.rem(z + 1, 4)
    left, right = lax.rem(y + 3, 4), lax.rem(y + 1, 4)

    def pass_along(copies, full, cols):
        steps = (
            (p.at(dz=1), full.at[xl, pl.ds(0, 2), below, :, cols]),
            (p.at(dz=3), full.at[xl, pl.ds(2, 2), above, :, cols]),
            (p.at(dy=1), full.at[1 - xl, left, pl.ds(0, 2), :, cols]),
            (p.at(dy=3), full.at[1 - xl, right, pl.ds(2, 2), :, cols]),
        )
        sent = []
        for copy, (device, part) in zip(copies, steps):
            copy.wait_recv()
            sent.append(w.to(device, part, part))
        return sent

    tokens.relay()
    exp_swap = w.to(p.partner(), exp.at[1 - xl], far_rows.at[z])
    att_end = pass_along(att_up, att_full, pl.ds(0, AW))
    tokens.forward()
    exp_swap.wait_recv()
    cots = Spread(w, p, cot_own, cot_all)
    for copy in att_end:
        copy.wait_recv()
    exp_near = [w.to(p.at(dy=k), exp.at[xl], near_rows.at[y]) for k in (1, 3)]
    exp_far = [w.to(p.at(dz=k), far_rows.at[z], far_rows.at[z]) for k in (1, 3)]
    tokens.arrived()

    for n in range(16):
        column = att_full[n // 8, n % 8 // 2, pl.ds(n % 2 * 2, 2), :, 1024:1152]
        column = jnp.transpose(column.astype(F32).reshape(128, 128))
        gains[:, n * 128 : (n + 1) * 128] = column[:8]
    start = pl.multiple_of(t * 512 + xl * 256, 256)
    head_gains[...] = jnp.zeros_like(head_gains)
    head_gains[0:2] = gains[2:4, pl.ds(start, 256)]
    w_small[...] = att_full[:, :, :, :, 1024:1152].reshape(D, 128)
    masks[0].wait_recv()
    local.append(w.here(att_full, att_out))
    local.append(w.here(live_both, live_out))

    sums = Collect(w, p, branch, got, None, half, arrived, across)

    def project(s):
        for b in range(4):

            def norm(rows, b=b):
                v = x_all[s, b // 2, b % 2, rows].astype(F32)
                scale = lax.rsqrt(jnp.mean(v * v, axis=-1, keepdims=True) + EPS)
                value = (v * scale * gains[0:1]).astype(BF16)
                normed[s, pl.ds(pl.multiple_of(b * BLK + rows.start, 16), 16)] = value

            each_rows(BLK, 16, norm)
        for c in range(3):
            cols = pl.ds(c * 256, 256)
            weight = att_full[:, :, :, :, cols].reshape(D, 256)
            proj[s, :, cols] = dot(normed[s], weight)

    def attend(s):
        for h in range(2):
            for c, factor in ((0, HD ** (-0.5)), (1, 1.0)):
                cols = pl.ds(c * 256 + h * HD, HD)
                v = proj[s, :, cols]
                scale = lax.rsqrt(jnp.mean(v * v, axis=-1, keepdims=True) + EPS)
                v = v * scale * head_gains[c : c + 1, h * HD : (h + 1) * HD]
                v = (v * cos[...] + turn_half(v) * sin[...]) * factor
                qkv[s, :, cols] = v.astype(BF16)
        qkv[s, :, 512:768] = proj[s, :, 512:768].astype(BF16)
        for h in range(2):
            q, k, v = (qkv[s, :, pl.ds(c * 256 + h * HD, HD)] for c in range(3))
            scores = dot(q, k, ((1,), (1,)))
            weights = jnp.exp(scores - jnp.max(scores, axis=-1, keepdims=True))
            weights = weights * live_both[s, 0:1].astype(F32)
            probs = (weights / jnp.sum(weights, axis=-1, keepdims=True)).astype(BF16)
            attended[s, :, pl.ds(h * HD, HD)] = dot(probs, v).astype(BF16)
        for n in range(4):
            weight = att_full[n // 2, pl.ds(n % 2 * 2, 2), :, :, 768:1024].reshape(512, 256)
            part = dot(attended[s], weight, ((1,), (1,))).astype(BF16)
            branch[s, :, :, :, pl.ds(n * 512, 512)] = part.reshape(2, 2, BLK, 512)

    first, second = xl, 1 - xl
    project(first)
    attend(first)
    low, high = pl.ds(0, 32), pl.ds(32, 32)
    exp_relay = []
    for copy, device, part in (
        (exp_near[0], p.at(dy=1), near_rows.at[left, low]),
        (exp_near[1], p.at(dy=3), near_rows.at[right, high]),
        (exp_far[0], p.at(dz=1), far_rows.at[below, low]),
        (exp_far[1], p.at(dz=3), far_rows.at[above, high]),
    ):
        copy.wait_recv()
        exp_relay.append(w.to(device, part, part))
    sums.begin((2, 0))
    project(second)
    cots.relay()
    sums.start()
    for copy in exp_relay:
        copy.wait_recv()
    mine_z = exp_full.at[xl, :, z]
    mine_y = exp_full.at[1 - xl, y]
    kept, last = pl.ds(0, KEPT), pl.ds(KEPT, EW - KEPT)
    near_kept, far_kept = near_rows.at[:, :, kept], far_rows.at[:, :, kept]
    exp_up = [w.to(p.at(dz=k), near_kept, mine_z) for k in (1, 3)]
    exp_up += [w.to(p.at(dy=k), far_kept, mine_y) for k in (1, 3)]
    local += [w.here(near_kept, mine_z), w.here(far_kept, mine_y)]
    local += [
        w.here(near_rows.at[:, :, last], near_last),
        w.here(far_rows.at[:, :, last], far_last),
    ]
    attend(second)
    sums.begin((1, 3))
    cots.forward()
    local += [w.here(normed, normed_out), w.here(proj, proj_out)]
    sums.ahead()
    sums.pass_on()
    sums.arrive()

    def norm(rows):
        now = x_own[rows].astype(F32) + sums.total(rows)
        state[rows] = now
        scale = lax.rsqrt(jnp.mean(now * now, axis=-1, keepdims=True) + EPS)
        block[rows] = (now * scale * gains[1:2]).astype(BF16)

    each_rows(BLK, 16, norm)
    mids = Spread(w, p, block, mid_all)
    mids.relay()
    exp_end = pass_along(exp_up, exp_full, kept)
    mids.forward()
    mids.arrived()
    cots.arrived()
    for copy in masks[1:]:
        copy.wait_recv()
    for copy in exp_end:
        copy.wait_recv()
    for copy in local:
        copy.wait()
    for group in (tokens, cots, mids, sums):
        group.finish()
    for copy in (
        smalls + [att_swap, small_swap, exp_swap] + masks + att_near + att_far + att_up
        + att_end + exp_near + exp_far + exp_relay + exp_up + exp_end
    ):
        copy.wait_send()


def forward(
    lengths, x_own, cot_own, w_qkv, w_out, w_gate_up, w_down, gains, router, ids, cos, sin
):
    cell = jax.ShapeDtypeStruct((2, 2, 2, BLK, D), BF16)
    return pl.pallas_call(
        forward_kernel,
        name="forward",
        out_shape=[
            cell,
            cell,
            jax.ShapeDtypeStruct((2, 4, 4, 64, KEPT), BF16),
            jax.ShapeDtypeStruct((4, 64, EW - KEPT), BF16),
            jax.ShapeDtypeStruct((4, 64, EW - KEPT), BF16),
            jax.ShapeDtypeStruct((2, 4, 4, 64, AW), BF16),
            jax.ShapeDtypeStruct((2, SEQ, D), BF16),
            jax.ShapeDtypeStruct((2, SEQ, 768), F32),
            jax.ShapeDtypeStruct((2, SEQ, 768), BF16),
            jax.ShapeDtypeStruct((2, SEQ, 256), BF16),
            jax.ShapeDtypeStruct((BLK, D), F32),
            jax.ShapeDtypeStruct((8, D), F32),
            jax.ShapeDtypeStruct((8, 256), F32),
            jax.ShapeDtypeStruct((D, 128), BF16),
            jax.ShapeDtypeStruct((2, SEQ, 128), BF16),
            jax.ShapeDtypeStruct((2, 16, SEQ), BF16),
        ],
        in_specs=[pl.BlockSpec(memory_space=pltpu.SMEM)] + [VMEM] * 11,
        out_specs=[ANY] * 8 + [VMEM] * 6 + [ANY] * 2,
        scratch_shapes=[
            pltpu.VMEM((2, 2, 2, BLK, D), BF16),
            pltpu.VMEM((2, 4, 4, 64, AW), BF16),
            pltpu.VMEM((2, 16, SEQ), BF16),
            pltpu.VMEM((4, 64, EW), BF16),
            pltpu.VMEM((4, 64, EW), BF16),
            pltpu.VMEM((2, SEQ, D), BF16),
            pltpu.VMEM((2, SEQ, 768), F32),
            pltpu.VMEM((2, 2, 2, BLK, D), BF16),
        ]
        + collect_scratch(D, BF16, False)
        + [
            pltpu.VMEM((BLK, D), BF16),
            pltpu.VMEM((2, 64, 1024), BF16),
            pltpu.VMEM((2, 64, EW), BF16),
            pltpu.VMEM((128, 128), F32),
            pltpu.VMEM((16, 128), BF16),
            pltpu.VMEM((SEQ, 128), BF16),
            pltpu.VMEM((16, SEQ), BF16),
        ]
        + wire_scratch(96, 20),
        compiler_params=params(0, 60),
    )(lengths, x_own, cot_own, w_qkv, w_out, w_gate_up, w_down, gains, router, ids, cos, sin)


def split_dot(value, other, dims):
    high = value.astype(BF16)
    low = (value - high.astype(F32)).astype(BF16)
    dot = functools.partial(
        lax.dot_general, dimension_numbers=(dims, ((), ())), preferred_element_type=F32
    )
    return dot(high, other) + dot(low, other)


def norm_back(value, gain, grad):
    scale = lax.rsqrt(jnp.mean(value * value, axis=-1, keepdims=True) + EPS)
    shaped = grad * gain
    along = jnp.mean(shaped * value, axis=-1, keepdims=True)
    return scale * shaped - value * (scale * scale * scale * along), grad * value * scale


class Reduce:
    def __init__(self, wires, up, down, blocks, here, halves, mains, stage=None):
        self.wires, self.up, self.down = wires, up, down
        self.blocks, self.here, self.halves, self.mains = blocks, here, halves, mains
        self.stage = stage
        self.first, self.second, self.loading = {}, {}, {}

    def begin(self, group):
        at, to, width = group
        opposite = self.blocks(lax.rem(self.here + 2, 4))
        span = pl.ds(at, width)
        self.first[group] = [
            self.wires.to(
                device,
                opposite.at[pl.ds(side * 2, 2), :, span],
                self.halves.at[side, :, :, pl.ds(to, width)],
            )
            for side, device in ((0, self.up), (1, self.down))
        ]

    def relay(self, group):
        at, to, width = group
        span, wide = pl.ds(at, width), pl.ds(to, width)
        self.second[group] = []
        for side, device in ((0, self.up), (1, self.down)):
            self.first[group][side].wait_recv()
            block = self.blocks(lax.rem(self.here + (1 if side == 0 else 3), 4))
            for b in range(2):
                cell = (side * 2 + b, slice(None), span)
                total = block[cell].astype(F32) + self.halves[side, b, :, wide].astype(F32)
                block[cell] = total.astype(BF16)
            self.second[group].append(
                self.wires.to(device, block.at[:, :, span], self.mains.at[side, :, :, wide])
            )

    def fetch(self, group):
        _, to, width = group
        for copy in self.second[group]:
            copy.wait_recv()
        if self.stage is not None:
            self.loading[group] = self.wires.here(
                self.mains.at[:, :, :, pl.ds(to, width)], self.stage
            )

    def total(self, group, store):
        at, to, width = group
        span, wide = pl.ds(at, width), pl.ds(to, width)
        if self.stage is not None:
            self.loading[group].wait()
        own = self.blocks(self.here)
        for b in range(4):
            total = own[b, :, span].astype(F32)
            for side in range(2):
                if self.stage is not None:
                    total = total + self.stage[side, b].astype(F32)
                else:
                    total = total + self.mains[side, b, :, wide].astype(F32)
            store(b, total)

    def sent(self, group):
        for copy in self.first.pop(group) + self.second.pop(group):
            copy.wait_send()

    def finish(self):
        for group in list(self.first):
            self.sent(group)


TILE = 256
EXPERT = 3 * FFS
SLOTS = 3


def expert_kernel(
    mid, cot, w_exp, near_last, far_last, mask, small, state, cot_own, gains,
    branch_grad, w_last, mixed, near_rows, far_rows, near_main, far_main,
    state_grad, gain_grad, logit_grad,
    mid_here, cot_here, weight, pre_grad, gated, dw, near_half, far_half, near_stage, far_stage,
    mid_part, mix_out, soft, route, got, half, arrived, across,
    rgot, rhalf, rarrived, racross, block,
    send, recv, near,
):
    p = Place()
    w = Wires(send, recv, near)
    xl, y, z, t = p.xl, p.y, p.z, p.t

    def source(e, cols=(0, EXPERT)):
        if e == HALF_E - 1:
            return w_last, pl.ds(*cols)
        return w_exp, pl.ds(e * EXPERT + cols[0], cols[1])

    def fetch(e):
        full, cols = source(e)
        return w.here(full.at[:, :, :, :, cols], weight.at[e % 2])

    stage_in = [w.here(near_last, near_stage.at[0]), w.here(far_last, far_stage.at[0])]
    loads = [w.here(mid, mid_here), fetch(0), w.here(cot, cot_here)]
    ready = {0: loads[1], 1: fetch(1)}
    greet(cell_peers(p) + [p.at(dy=1), p.at(dy=3), p.at(dz=1), p.at(dz=3)])
    for copy in stage_in:
        copy.wait()
    mine_z, mine_y = w_last.at[xl, :, z], w_last.at[1 - xl, y]
    last_up = [w.to(p.at(dz=k), near_stage.at[0], mine_z) for k in (1, 3)]
    last_up += [w.to(p.at(dy=k), far_stage.at[0], mine_y) for k in (1, 3)]
    last_local = [w.here(near_stage.at[0], mine_z), w.here(far_stage.at[0], mine_y)]

    def pass_last():
        steps = (
            (p.at(dz=1), w_last.at[xl, pl.ds(0, 2), lax.rem(z + 3, 4)]),
            (p.at(dz=3), w_last.at[xl, pl.ds(2, 2), lax.rem(z + 1, 4)]),
            (p.at(dy=1), w_last.at[1 - xl, lax.rem(y + 3, 4), pl.ds(0, 2)]),
            (p.at(dy=3), w_last.at[1 - xl, lax.rem(y + 1, 4), pl.ds(2, 2)]),
        )
        sent = []
        for copy, (device, part) in zip(last_up, steps):
            copy.wait_recv()
            sent.append(w.to(device, part, part))
        return sent

    along_z = Reduce(
        w, p.at(dz=1), p.at(dz=3), lambda k: dw.at[xl, :, k], z,
        near_half, near_main, near_stage,
    )
    along_y = Reduce(
        w, p.at(dy=1), p.at(dy=3), lambda k: dw.at[1 - xl, k], y,
        far_half, far_main, far_stage,
    )
    groups = [(e % SLOTS * EXPERT, e * EXPERT, EXPERT) for e in range(HALF_E)]
    loads[0].wait()
    for n in range(ROWS // TILE):
        rows = pl.ds(n * TILE, TILE)
        logits = dot(mid_here[rows], small[...])
        on = mask[rows] > 0
        peak = jnp.max(jnp.where(on, logits, -1e30), axis=-1, keepdims=True)
        chance = jnp.where(on, jnp.exp(jnp.where(on, logits - peak, 0.0)), 0.0)
        soft[rows] = chance / jnp.maximum(jnp.sum(chance, axis=-1, keepdims=True), 1.0)
    route[...] = jnp.zeros_like(route)
    lane = lax.broadcasted_iota(jnp.int32, (TILE, 128), 1)
    loads[2].wait()

    def expert(e):
        ready[e].wait()
        here = lane == ROUTER_AT + xl * HALF_E + e
        for n in range(ROWS // TILE):
            rows = pl.ds(n * TILE, TILE)
            gate = jnp.sum(jnp.where(here, soft[rows], 0.0), axis=-1, keepdims=True)
            pre = dot(
                mid_here[rows], weight[e % 2, :, :, :, :, : 2 * FFS].reshape(D, 2 * FFS)
            )
            hidden = dot(cot_here[rows], weight[e % 2, :, :, :, :, 2 * FFS :].reshape(D, FFS))
            gate_pre, up_pre = pre[:, :FFS], pre[:, FFS:]
            sig = 1.0 / (1.0 + jnp.exp(-gate_pre))
            silu = gate_pre * sig
            inner = (silu * up_pre).astype(BF16).astype(F32)
            routed = jnp.where(here, jnp.sum(inner * hidden, axis=-1, keepdims=True), 0.0)
            route[n // 2, n % 2] += routed.reshape(2, BLK, 128)
            gated[rows, pl.ds(e * FFS, FFS)] = (gate * inner).astype(BF16)
            hidden = gate * hidden
            pre_grad[rows, pl.ds(e * 512, FFS)] = (
                hidden * up_pre * (sig + silu * (1.0 - sig))
            ).astype(BF16)
            pre_grad[rows, pl.ds(e * 512 + FFS, FFS)] = (hidden * silu).astype(BF16)

    def weight_grads(e):
        at = groups[e][0]
        for n in range(4):
            cols = pl.ds(n * 512, 512)
            to = (n // 2, pl.ds(n % 2 * 2, 2), slice(None), slice(None))
            grad = dot(mid_here[:, cols], pre_grad[:, pl.ds(e * 512, 512)], ((0,), (0,)))
            dw[(*to, pl.ds(at, 512))] = grad.astype(BF16).reshape(2, 4, 64, 512)
            grad = dot(cot_here[:, cols], gated[:, pl.ds(e * FFS, FFS)], ((0,), (0,)))
            dw[(*to, pl.ds(at + 512, FFS))] = grad.astype(BF16).reshape(2, 4, 64, FFS)
        along_z.begin(groups[e])
        along_y.begin(groups[e])

    def relay(e):
        along_z.relay(groups[e])
        along_y.relay(groups[e])

    def retire(e):
        along_z.fetch(groups[e])
        along_y.fetch(groups[e])
        out = []
        for along, own, rows_out in (
            (along_z, dw.at[xl, :, z], near_rows),
            (along_y, dw.at[1 - xl, y], far_rows),
        ):
            at, to, width = groups[e]
            span = pl.ds(at, width)

            def store(b, total, own=own, span=span):
                own[b, :, span] = total.astype(BF16)

            along.total(groups[e], store)
            out.append(w.here(own.at[:, :, span], rows_out.at[:, :, pl.ds(to, width)]))
            along.sent(groups[e])
        return out

    def rows_fetch(n):
        copies = []
        for e in range(HALF_E):
            full, cols = source(e)
            copies.append(
                w.here(
                    full.at[n // 4, n % 4, :, :, cols], weight.at[(n + 1) % 2, e // 4, e % 4]
                )
            )
        return copies

    expert(0)
    last_end = pass_last()
    ready[2] = fetch(2)
    weight_grads(0)
    expert(1)
    ready[3] = fetch(3)
    relay(0)
    weight_grads(1)
    expert(2)
    for copy in last_end:
        copy.wait_recv()
    for copy in last_local:
        copy.wait()
    for copy in last_up:
        copy.wait_send()
    ready[4] = fetch(4)
    relay(1)
    weight_grads(2)
    expert(3)
    chunk = {0: rows_fetch(0)}
    expert(4)
    relay(2)
    chunk[1] = rows_fetch(1)
    routes = Collect(w, p, route, rgot, None, rhalf, rarrived, racross)
    routes.begin()
    sums = Collect(w, p, mid_part, got, None, half, arrived, across)
    chunks = D // TILE
    for n in range(chunks):
        for copy in chunk[n]:
            copy.wait()
        slot = (n + 1) % 2
        for r in range(2):
            total = None
            for e in range(HALF_E):
                part = dot(
                    pre_grad[r * SEQ : (r + 1) * SEQ, e * 512 : (e + 1) * 512],
                    weight[slot, e // 4, e % 4, :, :, :512].reshape(TILE, 512),
                    ((1,), (1,)),
                )
                total = part if e == 0 else total + part
            mid_part[r, :, :, :, pl.ds(n * TILE, TILE)] = total.astype(BF16).reshape(
                2, 2, BLK, TILE
            )
        if n + 2 < chunks:
            chunk[n + 2] = rows_fetch(n + 2)

    def down_fetch(n):
        copies = []
        for e in range(HALF_E):
            full, cols = source(e, (512, FFS))
            copies.append(
                w.here(
                    full.at[n // 2, pl.ds(n % 2 * 2, 2), :, :, cols],
                    weight.at[
                        (n + 1) % 2, 0, pl.ds(e // 3 * 2, 2), :, :, pl.ds(e % 3 * FFS, FFS)
                    ],
                )
            )
        return copies

    sums.begin()
    downs = {0: down_fetch(0), 1: down_fetch(1)}
    routes.start()
    routes.ahead()
    out = retire(0)
    for copy in out:
        copy.wait()
    weight_grads(3)
    sums.start()
    sums.ahead()
    routes.pass_on()
    out = retire(1)
    for copy in out:
        copy.wait()
    weight_grads(4)
    sums.pass_on()
    relay(3)
    mixing = {}
    for n in range(4):
        for copy in downs[n]:
            copy.wait()
        for r in range(2):
            if n > 0:
                mixing[n - 1, r].wait()
            total = None
            for e in range(HALF_E):
                at, cols = e // 3 * 2, pl.ds(e % 3 * FFS, FFS)
                part = dot(
                    gated[r * SEQ : (r + 1) * SEQ, e * FFS : (e + 1) * FFS],
                    weight[(n + 1) % 2, 0, at : at + 2, :, :, cols].reshape(512, FFS),
                    ((1,), (1,)),
                )
                total = part if e == 0 else total + part
            mix_out[r] = total.astype(BF16)
            mixing[n, r] = w.here(
                mix_out.at[r], mixed.at[pl.ds(r * SEQ, SEQ), pl.ds(n * 512, 512)]
            )
        if n + 2 < 4:
            downs[n + 2] = down_fetch(n + 2)
    routes.arrive()

    def router(rows):
        chance = soft[pl.ds(pl.multiple_of((xl * 4 + t) * BLK + rows.start, 16), 16)]
        grad = routes.total(rows)
        grad = chance * (grad - jnp.sum(chance * grad, axis=-1, keepdims=True))
        logit_grad[rows] = grad

    each_rows(BLK, 16, router)
    state_grad[...] = split_dot(logit_grad[...], small[...], ((1,), (1,)))
    sums.arrive()
    gain_grad[...] = jnp.zeros_like(gain_grad)

    def back(rows):
        grad = sums.total(rows) + state_grad[rows]
        change, gain_part = norm_back(state[rows], gains[1:2], grad)
        total = cot_own[rows].astype(F32) + change
        state_grad[rows] = total
        block[rows] = total.astype(BF16)
        gain_grad[0:1] += jnp.sum(gain_part, axis=0, keepdims=True)

    each_rows(BLK, 16, back)
    tokens = Spread(w, p, block, branch_grad)
    relay(4)
    out = retire(2)
    tokens.relay()
    out += retire(3)
    tokens.forward()
    out += retire(4)
    tokens.arrived()
    for copy in out + [mixing[3, 0], mixing[3, 1]]:
        copy.wait()
    for group in (tokens, sums, routes, along_z, along_y):
        group.finish()
    for copy in last_end:
        copy.wait_send()


def experts(mid, cot, w_exp, near_last, far_last, mask, small, state, cot_own, gains):
    part = jax.ShapeDtypeStruct((4, 64, EW), BF16)
    landing = jax.ShapeDtypeStruct((2, 4, 64, EW), BF16)
    return pl.pallas_call(
        expert_kernel,
        name="experts",
        out_shape=[
            jax.ShapeDtypeStruct((2, 2, 2, BLK, D), BF16),
            jax.ShapeDtypeStruct((2, 4, 4, 64, EW - KEPT), BF16),
            jax.ShapeDtypeStruct((ROWS, D), BF16),
            part,
            part,
            landing,
            landing,
            jax.ShapeDtypeStruct((BLK, D), F32),
            jax.ShapeDtypeStruct((8, D), F32),
            jax.ShapeDtypeStruct((BLK, 128), F32),
        ],
        in_specs=[ANY] * 5 + [VMEM] * 5,
        out_specs=[ANY] * 7 + [VMEM] * 3,
        scratch_shapes=[
            pltpu.VMEM((ROWS, D), BF16),
            pltpu.VMEM((ROWS, D), BF16),
            pltpu.VMEM((2, 2, 4, 4, 64, EXPERT), BF16),
            pltpu.VMEM((ROWS, GU), BF16),
            pltpu.VMEM((ROWS, EW - GU), BF16),
            pltpu.VMEM((2, 4, 4, 64, SLOTS * EXPERT), BF16),
            pltpu.VMEM((2, 2, 64, EW), BF16),
            pltpu.VMEM((2, 2, 64, EW), BF16),
            pltpu.VMEM((2, 4, 64, EXPERT), BF16),
            pltpu.VMEM((2, 4, 64, EXPERT), BF16),
            pltpu.VMEM((2, 2, 2, BLK, D), BF16),
            pltpu.VMEM((2, SEQ, 512), BF16),
            pltpu.VMEM((ROWS, 128), F32),
            pltpu.VMEM((2, 2, 2, BLK, 128), F32),
        ]
        + collect_scratch(D, BF16, False)
        + collect_scratch(128, F32, False)
        + [pltpu.VMEM((BLK, D), BF16)]
        + wire_scratch(88, 120),
        compiler_params=params(2, 62),
    )(mid, cot, w_exp, near_last, far_last, mask, small, state, cot_own, gains)


QKV_GROUP = (0, 0, 768)
SMALL_GROUP = (768, 768, 128)
OUT_GROUP = (896, 896, 256)


def backward_kernel(
    bg_in, w_att_in, normed_in, proj_in, qkv_in, attended_in, mixed, near_rows, far_rows, mid_all,
    logit_grad, mid_gain, state, state_grad, x_own, gains, head_gains, cos, sin, live,
    input_grad, output, exp_sum, att_sum, small_sum,
    bg, w_att, normed, proj, qkv, attended, mid_own, att_bg, proj_grad, in_part, in_gain,
    head_gain, small_rows, attg, near_half, far_half, near_main, far_main,
    got, half, arrived, across, mgot, mown, mhalf, marrived, macross,
    near_in, far_in, far_sum, att_near, att_far, att_near_end, att_far_end, att_far_sum,
    exp_got, att_got, small_all, small_in, send, recv, near,
):
    p = Place()
    w = Wires(send, recv, near)
    xl, y, z, t = p.xl, p.y, p.z, p.t
    greet(cell_peers(p) + plane_peers(p) + [p.at(dx=2, dc=1)])
    mixes = Collect(w, p, mixed, mgot, mown, mhalf, marrived, macross)
    mixes.begin()
    loads = [
        w.here(a, b)
        for a, b in (
            (bg_in, bg),
            (w_att_in, w_att),
            (attended_in, attended),
            (qkv_in, qkv),
            (proj_in, proj),
            (normed_in, normed),
            (mid_all.at[xl, p.xh, p.c], mid_own),
        )
    ]
    exps = []
    for k in (1, 3, 2):
        to_z, to_y = lax.rem(z + k, 4), lax.rem(y + k, 4)
        exps.append(w.to(p.at(dy=k), near_rows.at[to_y], near_in.at[k - 1]))
        exps.append(w.to(p.at(dz=k), far_rows.at[to_z], far_in.at[k - 1]))
    local = [
        w.here(near_rows.at[y], near_in.at[3]),
        w.here(far_rows.at[z], far_in.at[3]),
    ]
    along_z = Reduce(
        w, p.at(dz=1), p.at(dz=3), lambda k: attg.at[xl, :, k], z, near_half, near_main
    )
    along_y = Reduce(
        w, p.at(dy=1), p.at(dy=3), lambda k: attg.at[1 - xl, k], y, far_half, far_main
    )
    in_gain[...] = jnp.zeros_like(in_gain)
    head_gain[...] = jnp.zeros_like(head_gain)
    for copy in loads[:3]:
        copy.wait()
    for s in range(2):
        att_bg[s] = dot(bg[s], w_att[:, 768:1024]).astype(BF16)
    for copy in loads[3:]:
        copy.wait()

    def heads(s):
        for h in range(2):
            head = pl.ds(h * HD, HD)
            q, k, v = (qkv[s, :, pl.ds(c * 256 + h * HD, HD)] for c in range(3))
            scores = dot(q, k, ((1,), (1,)))
            weights = jnp.exp(scores - jnp.max(scores, axis=-1, keepdims=True))
            weights = weights * live[s, 0:1].astype(F32)
            probs = weights / jnp.sum(weights, axis=-1, keepdims=True)
            out_grad = att_bg[s, :, head]
            prob_grad = dot(out_grad, v, ((1,), (1,)))
            inner = jnp.sum(probs * prob_grad, axis=-1, keepdims=True)
            score_grad = (probs * (prob_grad - inner)).astype(BF16)
            value_grad = dot(probs.astype(BF16), out_grad, ((0,), (0,)))
            proj_grad[s, :, pl.ds(512 + h * HD, HD)] = value_grad.astype(BF16)
            both = (
                (0, dot(score_grad, k) * HD ** (-0.5)),
                (1, dot(score_grad, q, ((0,), (0,)))),
            )
            for c, grad in both:
                cols = pl.ds(c * 256 + h * HD, HD)
                grad = grad * cos[...] - turn_half(grad) * sin[...]
                gain = head_gains[c : c + 1, h * HD : (h + 1) * HD]
                change, gain_part = norm_back(proj[s, :, cols], gain, grad)
                proj_grad[s, :, cols] = change.astype(BF16)
                head_gain[c : c + 1, h * HD : (h + 1) * HD] += jnp.sum(
                    gain_part, axis=0, keepdims=True
                )

    def inputs(s):
        for b in range(4):
            rows = pl.ds(b * BLK, BLK)
            part = dot(proj_grad[s, rows], w_att[:, :768], ((1,), (1,)))
            in_part[s, b // 2, b % 2] = part.astype(BF16)
            in_gain[0:1] += jnp.sum(part * normed[s, rows].astype(F32), axis=0, keepdims=True)

    def weight_rows(left, right, at, width):
        for n in range(4):
            cols = pl.ds(n * 512, 512)
            grad = dot(left(0, cols), right(0), ((0,), (0,)))
            grad = grad + dot(left(1, cols), right(1), ((0,), (0,)))
            attg[n // 2, pl.ds(n % 2 * 2, 2), :, :, pl.ds(at, width)] = grad.astype(BF16).reshape(
                2, 4, 64, width
            )

    sums = Collect(w, p, in_part, got, None, half, arrived, across)
    first, second = xl, 1 - xl
    weight_rows(lambda s, cols: bg[s, :, cols], lambda s: attended[s], 896, 256)
    along_z.begin(OUT_GROUP)
    along_y.begin(OUT_GROUP)
    mixes.start()
    mixes.ahead()
    heads(first)
    mixes.pass_on()
    heads(second)
    along_z.relay(OUT_GROUP)
    along_y.relay(OUT_GROUP)
    weight_rows(lambda s, cols: normed[s, :, cols], lambda s: proj_grad[s], 0, 768)
    along_z.begin(QKV_GROUP)
    along_y.begin(QKV_GROUP)
    for copy in local:
        copy.wait()
    for copy in exps:
        copy.wait_recv()

    def exp_far(rows):
        total = far_in[3, rows].astype(F32)
        for k in range(3):
            total = total + far_in[k, rows].astype(F32)
        far_sum[rows] = total.astype(BF16)

    each_rows(64, 16, exp_far)
    exp_swap = w.to(p.partner(), far_sum, exp_got)
    inputs(first)
    sums.begin((2, 0))
    inputs(second)
    sums.begin((1, 3))
    sums.start()
    sums.ahead()

    small_rows[...] = jnp.zeros_like(small_rows)
    small_rows[0:1] = in_gain[0:1] / gains[0:1]
    small_rows[1:2] = mid_gain[0:1]
    start = pl.multiple_of(t * 512 + xl * 256, 256)
    small_rows[2:4, pl.ds(start, 256)] = head_gain[0:2]
    high = logit_grad[...].astype(BF16)
    low = (logit_grad[...] - high.astype(F32)).astype(BF16)
    for n in range(16):
        cols = pl.ds(n * 128, 128)
        strip = dot(mid_own[:, cols], high, ((0,), (0,))) + dot(mid_own[:, cols], low, ((0,), (0,)))
        strip = strip + jnp.transpose(small_rows[:, cols])
        attg[n // 8, n % 8 // 2, pl.ds(n % 2 * 2, 2), :, pl.ds(768, 128)] = strip.astype(
            BF16
        ).reshape(2, 64, 128)
    along_z.begin(SMALL_GROUP)
    along_y.begin(SMALL_GROUP)
    along_z.relay(QKV_GROUP)
    along_y.relay(QKV_GROUP)
    sums.pass_on()

    along_z.relay(SMALL_GROUP)
    along_y.relay(SMALL_GROUP)
    for group in (OUT_GROUP, QKV_GROUP, SMALL_GROUP):
        for along, rows_ref in ((along_z, att_near), (along_y, att_far)):

            def store(b, total, rows_ref=rows_ref, group=group):
                rows_ref[b, :, pl.ds(group[1], group[2])] = total.astype(BF16)

            along.fetch(group)
            along.total(group, store)
    ends = []
    for k in (1, 3, 2):
        to_z, to_y = lax.rem(z + k, 4), lax.rem(y + k, 4)
        ends.append(w.to(p.at(dz=k), att_far.at[to_z], att_far_end.at[k - 1]))
        ends.append(w.to(p.at(dy=k), att_near.at[to_y], att_near_end.at[k - 1]))
    mixes.arrive()

    def finish(rows):
        output[rows] = (state[rows] + mixes.total(rows)).astype(BF16)

    each_rows(BLK, 16, finish)

    def exp_near(rows):
        total = near_in[3, rows].astype(F32)
        for k in range(3):
            total = total + near_in[k, rows].astype(F32)
        exp_sum[xl, rows] = total

    each_rows(64, 16, exp_near)
    for copy in ends:
        copy.wait_recv()

    def att_far_add(rows):
        total = att_far[z, rows].astype(F32)
        for k in range(3):
            total = total + att_far_end[k, rows].astype(F32)
        att_far_sum[rows] = total.astype(BF16)

    each_rows(64, 16, att_far_add)
    att_swap = w.to(p.partner(), att_far_sum, att_got)

    sums.arrive()

    def back(rows):
        change, _ = norm_back(x_own[rows].astype(F32), gains[0:1], sums.total(rows))
        input_grad[rows] = state_grad[rows] + change

    each_rows(BLK, 16, back)
    exp_swap.wait_recv()
    exp_sum[1 - xl] = exp_got[...].astype(F32)

    def att_near_add(rows):
        total = att_near[y, rows].astype(F32)
        for k in range(3):
            total = total + att_near_end[k, rows].astype(F32)
        att_sum[xl, rows] = total

    each_rows(64, 16, att_near_add)
    att_swap.wait_recv()
    att_sum[1 - xl] = att_got[...].astype(F32)
    small_all[...] = att_sum[0, :, 768:896] + att_sum[1, :, 768:896]
    smalls = []
    for n, (a, b) in enumerate(((0, 1), (2, 0), (2, 1))):
        dest = lax.rem(p.xh + a // 2, 2) * 2 + lax.rem(p.c + b, 2)
        smalls.append(
            w.to(
                p.at(dx=a, dc=b),
                small_all.at[pl.ds(pl.multiple_of(dest * 16, 16), 16)],
                small_in.at[n],
            )
        )
    for copy in smalls:
        copy.wait_recv()
    total = small_all[pl.ds(pl.multiple_of(t * 16, 16), 16)]
    for n in range(3):
        total = total + small_in[n]
    small_sum[...] = total
    for group in (sums, mixes, along_z, along_y):
        group.finish()
    for copy in exps + ends + [exp_swap, att_swap] + smalls:
        copy.wait_send()


def backward(
    bg, w_att, normed, proj, qkv, attended, mixed, near_rows, far_rows, mid_all,
    logit_grad, mid_gain, state, state_grad, x_own, gains, head_gains, cos, sin, live,
):
    return pl.pallas_call(
        backward_kernel,
        name="backward",
        out_shape=[
            jax.ShapeDtypeStruct((BLK, D), F32),
            jax.ShapeDtypeStruct((BLK, D), BF16),
            jax.ShapeDtypeStruct((2, 64, EW), F32),
            jax.ShapeDtypeStruct((2, 64, AW), F32),
            jax.ShapeDtypeStruct((16, 128), F32),
        ],
        in_specs=[ANY] * 10 + [VMEM] * 10,
        out_specs=[VMEM] * 5,
        scratch_shapes=[
            pltpu.VMEM((2, SEQ, D), BF16),
            pltpu.VMEM((D, AW), BF16),
            pltpu.VMEM((2, SEQ, D), BF16),
            pltpu.VMEM((2, SEQ, 768), F32),
            pltpu.VMEM((2, SEQ, 768), BF16),
            pltpu.VMEM((2, SEQ, 256), BF16),
            pltpu.VMEM((BLK, D), BF16),
            pltpu.VMEM((2, SEQ, 256), BF16),
            pltpu.VMEM((2, SEQ, 768), BF16),
            pltpu.VMEM((2, 2, 2, BLK, D), BF16),
            pltpu.VMEM((8, D), F32),
            pltpu.VMEM((8, 256), F32),
            pltpu.VMEM((128, D), F32),
            pltpu.VMEM((2, 4, 4, 64, AW), BF16),
            pltpu.VMEM((2, 2, 64, AW), BF16),
            pltpu.VMEM((2, 2, 64, AW), BF16),
            pltpu.VMEM((2, 4, 64, AW), BF16),
            pltpu.VMEM((2, 4, 64, AW), BF16),
        ]
        + collect_scratch(D, BF16, False)
        + collect_scratch(D, BF16, True)
        + [
            pltpu.VMEM((4, 64, EW), BF16),
            pltpu.VMEM((4, 64, EW), BF16),
            pltpu.VMEM((64, EW), BF16),
            pltpu.VMEM((4, 64, AW), BF16),
            pltpu.VMEM((4, 64, AW), BF16),
            pltpu.VMEM((3, 64, AW), BF16),
            pltpu.VMEM((3, 64, AW), BF16),
            pltpu.VMEM((64, AW), BF16),
            pltpu.VMEM((64, EW), BF16),
            pltpu.VMEM((64, AW), BF16),
            pltpu.VMEM((64, 128), F32),
            pltpu.VMEM((3, 16, 128), F32),
        ]
        + wire_scratch(72, 20),
        compiler_params=params(3, 62),
    )(
        bg, w_att, normed, proj, qkv, attended, mixed, near_rows, far_rows, mid_all,
        logit_grad, mid_gain, state, state_grad, x_own, gains, head_gains, cos, sin, live,
    )


def finish_kernel(
    input_grad, output, exp_sum, att_sum, small_sum,
    output_out, input_out, gains_out, qkv_out, out_out, router_out, gate_up_out, down_out,
):
    output_out[...] = output[...]
    input_out[...] = input_grad[...]
    gains_out[...] = jnp.transpose(small_sum[...])[:4]
    router_out[...] = pltpu.roll(small_sum[...], 128 - ROUTER_AT, 1)[:, :E]
    for h in range(2):
        for c in range(3):
            qkv_out[c, :, h * 256 : (h + 1) * 256] = att_sum[h, :, c * 256 : (c + 1) * 256]
        out_out[:, h * 256 : (h + 1) * 256] = att_sum[h, :, 896:1152]
        for e in range(HALF_E):
            for g in range(2):
                at = (e * 3 + g) * FFS
                gate_up_out[h * HALF_E + e, g] = exp_sum[h, :, at : at + FFS]
            at = (e * 3 + 2) * FFS
            down_out[h * HALF_E + e] = exp_sum[h, :, at : at + FFS]


def finish(input_grad, output, exp_sum, att_sum, small_sum):
    return pl.pallas_call(
        finish_kernel,
        name="finish",
        out_shape=[
            jax.ShapeDtypeStruct((BLK, D), BF16),
            jax.ShapeDtypeStruct((BLK, D), F32),
            jax.ShapeDtypeStruct((4, 16), F32),
            jax.ShapeDtypeStruct((3, 64, 512), F32),
            jax.ShapeDtypeStruct((64, 512), F32),
            jax.ShapeDtypeStruct((16, E), F32),
            jax.ShapeDtypeStruct((E, 2, 64, FFS), F32),
            jax.ShapeDtypeStruct((E, 64, FFS), F32),
        ],
        in_specs=[VMEM] * 5,
        out_specs=[VMEM] * 8,
        compiler_params=params(),
    )(input_grad, output, exp_sum, att_sum, small_sum)


def rotary_tables():
    half = HD // 2
    freqs = np.float32(THETA) ** (-(np.arange(half, dtype=np.float32) * np.float32(2.0 / HD)))
    angles = np.arange(SEQ, dtype=np.float32)[:, None] * freqs[None, :].astype(np.float32)
    cos, sin = np.cos(angles), np.sin(angles)
    return (
        np.concatenate([cos, cos], axis=1).astype(np.float32),
        np.concatenate([-sin, sin], axis=1).astype(np.float32),
    )


def local(
    layer_input, cotangent, lengths, expert_ids, gains, w_qkv, w_out, w_router, w_gate_up, w_down
):
    cos, sin = (jnp.asarray(table) for table in rotary_tables())
    (
        cot_all, mid_all, w_exp, near_last, far_last, att_full, normed, proj, qkv, attended,
        state, gain_rows,
        head_gains, w_small, mask_both, live_both,
    ) = forward(
        lengths, layer_input, cotangent, w_qkv, w_out.T, w_gate_up, w_down.transpose(0, 2, 1),
        gains, w_router, expert_ids, cos, sin,
    )
    cot_all = cot_all.reshape(ROWS, D)
    w_att = att_full.reshape(D, AW)
    mid = mid_all.reshape(ROWS, D)
    branch_grad, _, mixed, near_sum, far_sum, _, _, state_grad, mid_gain, logit_grad = experts(
        mid, cot_all, w_exp, near_last, far_last, mask_both.reshape(ROWS, 128), w_small, state,
        cotangent, gain_rows,
    )
    input_grad, output, exp_sum, att_sum, small_sum = backward(
        branch_grad.reshape(2, SEQ, D),
        w_att,
        normed,
        proj,
        qkv,
        attended,
        mixed.reshape(2, 2, 2, BLK, D),
        near_sum,
        far_sum,
        mid_all,
        logit_grad,
        mid_gain,
        state,
        state_grad,
        layer_input,
        gain_rows,
        head_gains,
        cos,
        sin,
        live_both,
    )
    results = finish(input_grad, output, exp_sum, att_sum, small_sum)
    output, input_grad, gains_out, qkv_out, out_out, router_out, gate_up_out, down_out = results
    down_out = down_out.transpose(0, 2, 1)
    return (
        output, input_grad, gains_out, qkv_out, out_out.T, router_out, gate_up_out, down_out
    )


def solution(mesh):
    split = Mesh(mesh.devices.reshape(SIZES), AXES)
    rows, tensor = P(AXES, None), ("xh", "c")
    return jax.shard_map(
        local,
        mesh=split,
        in_specs=(
            rows,
            rows,
            P(DP),
            P(DP, None),
            P(None, AXES),
            P(None, DP, tensor),
            P(tensor, DP),
            rows,
            P(None, None, DP, tensor),
            P(None, tensor, DP),
        ),
        out_specs=(
            rows,
            rows,
            P(None, AXES),
            P(None, DP, tensor),
            P(tensor, DP),
            rows,
            P(None, None, DP, tensor),
            P(None, tensor, DP),
        ),
        check_vma=False,
    )
```

```python
import functools

import jax
import jax.numpy as jnp
import numpy as np
from jax import lax
from jax.experimental import pallas as pl
from jax.experimental.pallas import tpu as pltpu
from jax.sharding import Mesh
from jax.sharding import PartitionSpec as P

HD = 128
TOPK = 8
E = 10
D = 2048
SEQ = 512
ROWS = 1024
BLK = 128
HALF_E = 5
FFS = 256
GU = HALF_E * 2 * FFS
EW = HALF_E * 3 * FFS
AW = 1152
KEPT = 4 * 3 * FFS
ROUTER_AT = 4
AXES = ("xl", "y", "z", "xh", "c")
SIZES = (2, 4, 4, 2, 2)
DP = ("xl", "y", "z")
EPS = 1e-06
THETA = 10000.0
F32 = jnp.float32
BF16 = jnp.bfloat16
MIB = 1 << 20
LOGICAL = pl.DeviceIdType.MESH
VMEM = pl.BlockSpec(memory_space=pltpu.VMEM)
ANY = pl.BlockSpec(memory_space=pl.ANY)


class Place:
    def __init__(self):
        self.xl, self.y, self.z, self.xh, self.c = (lax.axis_index(a) for a in AXES)
        self.x = self.xh * 2 + self.xl
        self.t = self.xh * 2 + self.c

    def at(self, dx=0, dy=0, dz=0, dc=0):
        x = lax.rem(self.x + (dx + 4), 4)
        return (
            lax.rem(x, 2),
            lax.rem(self.y + (dy + 4), 4),
            lax.rem(self.z + (dz + 4), 4),
            lax.div(x, 2),
            lax.rem(self.c + (dc + 2), 2),
        )

    def chip(self, dx):
        x = lax.rem(self.x + (dx + 4), 4)
        return lax.rem(x, 2), lax.div(x, 2)

    def partner(self):
        return (1 - self.xl, self.y, self.z, self.xh, self.c)


class Wires:
    def __init__(self, send, recv, near):
        self.send, self.recv, self.near = send, recv, near
        self.count, self.near_count = 0, 0

    def to(self, device, src, dst):
        k, self.count = self.count, self.count + 1
        copy = pltpu.make_async_remote_copy(
            src_ref=src,
            dst_ref=dst,
            send_sem=self.send.at[k],
            recv_sem=self.recv.at[k],
            device_id=device,
            device_id_type=LOGICAL,
        )
        copy.start()
        return copy

    def here(self, src, dst):
        k, self.near_count = self.near_count, self.near_count + 1
        copy = pltpu.make_async_copy(src, dst, self.near.at[k])
        copy.start()
        return copy


def wire_scratch(copies, local):
    return [
        pltpu.SemaphoreType.DMA((copies,)),
        pltpu.SemaphoreType.DMA((copies,)),
        pltpu.SemaphoreType.DMA((local,)),
    ]


def greet(devices, meanwhile=None):
    barrier = pltpu.get_barrier_semaphore()
    for device in devices:
        pl.semaphore_signal(barrier, inc=1, device_id=device, device_id_type=LOGICAL)
    if meanwhile is not None:
        meanwhile()
    pl.semaphore_wait(barrier, len(devices))


def params(collective_id=None, vmem=56):
    if collective_id is None:
        return pltpu.CompilerParams(vmem_limit_bytes=vmem * MIB)
    return pltpu.CompilerParams(
        collective_id=collective_id, has_side_effects=True, vmem_limit_bytes=vmem * MIB
    )


def each_rows(total, step, body):
    def run(i, carry):
        body(pl.ds(pl.multiple_of(i * step, step), step))
        return carry

    lax.fori_loop(0, total // step, run, 0)


class Spread:
    def __init__(self, wires, place, block, out):
        self.wires, self.place, self.out = wires, place, out
        mine = out.at[place.xl, place.xh, place.c]
        self.up = wires.to(place.at(dx=1), block, mine)
        self.down = wires.to(place.at(dx=3), block, mine)
        self.rest = [wires.to(place.at(dc=1), block, mine)]
        self.local = wires.here(block, mine)

    def of(self, dx):
        xl, xh = self.place.chip(dx)
        return self.out.at[xl, xh, self.place.c]

    def across(self, part):
        self.rest.append(self.wires.to(self.place.at(dc=1), part, part))

    def relay(self):
        self.up.wait_recv()
        low = self.of(-1).at[pl.ds(0, BLK // 2)]
        self.up_relay = self.wires.to(self.place.at(dx=1), low, low)
        self.across(self.of(-1))
        self.down.wait_recv()
        high = self.of(1).at[pl.ds(BLK // 2, BLK // 2)]
        self.down_relay = self.wires.to(self.place.at(dx=3), high, high)
        self.across(self.of(1))

    def forward(self):
        self.up_relay.wait_recv()
        self.across(self.of(2).at[pl.ds(0, BLK // 2)])
        self.down_relay.wait_recv()
        self.across(self.of(2).at[pl.ds(BLK // 2, BLK // 2)])

    def arrived(self):
        self.local.wait()
        for copy in self.rest:
            copy.wait_recv()

    def finish(self):
        for copy in self.rest + [self.up, self.down, self.up_relay, self.down_relay]:
            copy.wait_send()


class Collect:
    def __init__(self, wires, place, parts, got, own, half, arrived, across):
        self.wires, self.place, self.parts = wires, place, parts
        self.got, self.own, self.half, self.arrived = got, own, half, arrived
        self.across = across
        self.swap, self.load, self.sent = {}, {}, []
        self.low, self.high = pl.ds(0, BLK // 2), pl.ds(BLK // 2, BLK // 2)

    def begin(self, steps=(2, 1, 3, 0)):
        for k in steps:
            xl, xh = self.place.chip(k)
            self.swap[k] = self.wires.to(
                self.place.at(dc=1), self.parts.at[xl, xh, 1 - self.place.c], self.got.at[k]
            )
            if self.own is not None:
                self.load[k] = self.wires.here(
                    self.parts.at[xl, xh, self.place.c], self.own.at[k]
                )

    def ready(self, k):
        self.swap[k].wait_recv()
        if self.own is not None:
            self.load[k].wait()

    def mine(self, k, rows):
        if self.own is not None:
            return self.own[k, rows]
        xl, xh = self.place.chip(k)
        return self.parts[xl, xh, self.place.c, rows]

    def add(self, k, start, size, also=None):
        def run(rows):
            rows = pl.ds(pl.multiple_of(start + rows.start, 16), 16)
            both = self.mine(k, rows).astype(F32) + self.got[k, rows].astype(F32)
            if also is not None:
                beside = pl.ds(pl.multiple_of(rows.start - start, 16), 16)
                both = both + self.across[also, beside].astype(F32)
            self.half[k - 1, rows] = both.astype(self.half.dtype)

        each_rows(size, 16, run)

    def start(self):
        self.ready(2)
        self.add(2, 0, BLK)
        self.via = [
            self.wires.to(self.place.at(dx=1), self.half.at[1, self.low], self.across.at[0]),
            self.wires.to(self.place.at(dx=3), self.half.at[1, self.high], self.across.at[1]),
        ]

    def ahead(self):
        for k, side, rows in ((1, 0, self.high), (3, 1, self.low)):
            self.ready(k)
            self.add(k, rows.start, BLK // 2)
            self.send(k, side, rows)

    def pass_on(self):
        for k, side, rows in ((1, 0, self.low), (3, 1, self.high)):
            self.via[side].wait_recv()
            self.add(k, rows.start, BLK // 2, side)
            self.send(k, side, rows)

    def send(self, k, side, rows):
        self.sent.append(
            self.wires.to(
                self.place.at(dx=k), self.half.at[k - 1, rows], self.arrived.at[side, rows]
            )
        )

    def arrive(self):
        self.ready(0)
        for copy in self.sent:
            copy.wait_recv()

    def total(self, rows):
        total = self.mine(0, rows).astype(F32) + self.got[0, rows].astype(F32)
        for side in range(2):
            total = total + self.arrived[side, rows].astype(F32)
        return total

    def finish(self):
        for copy in list(self.swap.values()) + self.via + self.sent:
            copy.wait_send()


def collect_scratch(width, dtype, own):
    block = pltpu.VMEM((4, BLK, width), dtype)
    return [block] * (2 if own else 1) + [
        pltpu.VMEM((3, BLK, width), dtype),
        pltpu.VMEM((2, BLK, width), dtype),
        pltpu.VMEM((2, BLK // 2, width), dtype),
    ]


def dot(a, b, dims=((1,), (0,))):
    return lax.dot_general(a, b, (dims, ((), ())), preferred_element_type=F32)


def turn_half(v):
    return pltpu.roll(v, HD // 2, 1)


def cell_peers(place):
    return [place.at(dx=1), place.at(dx=2), place.at(dx=3), place.at(dc=1)]


def plane_peers(place):
    return [place.at(dy=k) for k in (1, 2, 3)] + [place.at(dz=k) for k in (1, 2, 3)]


def forward_kernel(
    lengths, x_own, cot_own, w_qkv, w_out, w_gate_up, w_down, gains_own, router_own, ids, cos, sin,
    cot_all, mid_all, exp_full, near_last, far_last, att_out, normed_out, proj_out, qkv, attended, state, gains,
    head_gains, w_small, mask_both, live_out,
    x_all, att_full, live_both, near_rows, far_rows, normed, proj, branch,
    got, half, arrived, across, block, att, exp, square, small, mask, live, send, recv, near,
):
    p = Place()
    w = Wires(send, recv, near)

    def arrange():
        square[...] = jnp.zeros_like(square)
        square[0:4, 0:16] = gains_own[...].astype(F32)
        left = jnp.transpose(square[...])[0:16]
        square[0:4] = jnp.zeros((4, 128), F32)
        square[0:16, 0:E] = router_own[...].astype(F32)
        small[...] = (left + pltpu.roll(square[0:16], ROUTER_AT, 1)).astype(BF16)
        for h in range(2):
            for c in range(3):
                att[h, :, c * 256 : (c + 1) * 256] = w_qkv[c, :, h * 256 : (h + 1) * 256]
            att[h, :, 768:1024] = w_out[:, h * 256 : (h + 1) * 256]

    greet(cell_peers(p) + plane_peers(p) + [p.at(dx=2, dc=1)], arrange)
    xl, y, z, t = p.xl, p.y, p.z, p.t

    rows_t = pl.ds(pl.multiple_of(t * 16, 16), 16)
    mine = att_full.at[xl, y, z]
    small_mine = mine.at[rows_t, pl.ds(1024, 128)]
    smalls = [w.to(p.at(dx=a, dc=b), small, small_mine) for a, b in ((0, 1), (2, 0), (2, 1))]
    att_swap = w.to(p.partner(), att.at[1 - xl], mine.at[:, pl.ds(0, 1024)])
    mine[:, 0:1024] = att[xl]
    mine[rows_t, 1024:1152] = small[...]
    body, side = pl.ds(0, 1024), pl.ds(1024, 128)
    att_near = [w.to(p.at(dy=k), mine.at[:, body], mine.at[:, body]) for k in (1, 3, 2)]
    length = lengths[0]
    live[...] = (lax.broadcasted_iota(jnp.int32, (16, SEQ), 1) < length).astype(F32).astype(BF16)
    live_both[xl] = live[...]
    theirs = att_full.at[1 - xl, y, z]
    att_swap.wait_recv()
    att_far = [w.to(p.at(dz=k), theirs.at[:, body], theirs.at[:, body]) for k in (1, 3, 2)]
    for copy in smalls:
        copy.wait_recv()
    strip = mine.at[:, side]
    small_swap = w.to(p.partner(), strip, strip)
    att_near += [w.to(p.at(dy=k), strip, strip) for k in (1, 3, 2)]
    number = lax.broadcasted_iota(jnp.int32, (128, SEQ), 0) - ROUTER_AT
    named = jnp.zeros((128, SEQ), F32)
    for k in range(TOPK):
        named = jnp.where(ids[k : k + 1] == number, 1.0, named)
    on = lax.broadcasted_iota(jnp.int32, (128, SEQ), 1) < length
    mask[...] = jnp.transpose(jnp.where(on, named, 0.0)).astype(BF16)
    small_swap.wait_recv()
    strip = theirs.at[:, side]
    att_far += [w.to(p.at(dz=k), strip, strip) for k in (1, 3, 2)]
    tokens = Spread(w, p, x_own, x_all)
    masks = [
        w.to(p.partner(), live, live_both.at[xl]),
        w.to(p.partner(), mask, mask_both.at[xl]),
    ]
    local = [w.here(mask, mask_both.at[xl])]
    for h in range(2):
        for e in range(HALF_E):
            for g in range(2):
                at = (e * 3 + g) * FFS
                exp[h, :, at : at + FFS] = w_gate_up[h * HALF_E + e, g]
            at = (e * 3 + 2) * FFS
            exp[h, :, at : at + FFS] = w_down[h * HALF_E + e]
    near_rows[y] = exp[xl]
    for copy in att_near + att_far:
        copy.wait_recv()
    whole = att_full.at[xl, :, z]
    att_up = [w.to(p.at(dz=k), whole, whole) for k in (1, 3)]
    whole = att_full.at[1 - xl, y]
    att_up += [w.to(p.at(dy=k), whole, whole) for k in (1, 3)]
    below, above = lax.rem(z + 3, 4), lax.rem(z + 1, 4)
    left, right = lax.rem(y + 3, 4), lax.rem(y + 1, 4)

    def pass_along(copies, full, cols):
        steps = (
            (p.at(dz=1), full.at[xl, pl.ds(0, 2), below, :, cols]),
            (p.at(dz=3), full.at[xl, pl.ds(2, 2), above, :, cols]),
            (p.at(dy=1), full.at[1 - xl, left, pl.ds(0, 2), :, cols]),
            (p.at(dy=3), full.at[1 - xl, right, pl.ds(2, 2), :, cols]),
        )
        sent = []
        for copy, (device, part) in zip(copies, steps):
            copy.wait_recv()
            sent.append(w.to(device, part, part))
        return sent

    tokens.relay()
    exp_swap = w.to(p.partner(), exp.at[1 - xl], far_rows.at[z])
    att_end = pass_along(att_up, att_full, pl.ds(0, AW))
    tokens.forward()
    exp_swap.wait_recv()
    cots = Spread(w, p, cot_own, cot_all)
    for copy in att_end:
        copy.wait_recv()
    exp_near = [w.to(p.at(dy=k), exp.at[xl], near_rows.at[y]) for k in (1, 3)]
    exp_far = [w.to(p.at(dz=k), far_rows.at[z], far_rows.at[z]) for k in (1, 3)]
    tokens.arrived()

    for n in range(16):
        column = att_full[n // 8, n % 8 // 2, pl.ds(n % 2 * 2, 2), :, 1024:1152]
        column = jnp.transpose(column.astype(F32).reshape(128, 128))
        gains[:, n * 128 : (n + 1) * 128] = column[:8]
    start = pl.multiple_of(t * 512 + xl * 256, 256)
    head_gains[...] = jnp.zeros_like(head_gains)
    head_gains[0:2] = gains[2:4, pl.ds(start, 256)]
    w_small[...] = att_full[:, :, :, :, 1024:1152].reshape(D, 128)
    masks[0].wait_recv()
    local.append(w.here(att_full, att_out))
    local.append(w.here(live_both, live_out))

    sums = Collect(w, p, branch, got, None, half, arrived, across)

    def project(s):
        for b in range(4):

            def norm(rows, b=b):
                v = x_all[s, b // 2, b % 2, rows].astype(F32)
                scale = lax.rsqrt(jnp.mean(v * v, axis=-1, keepdims=True) + EPS)
                value = (v * scale * gains[0:1]).astype(BF16)
                normed[s, pl.ds(pl.multiple_of(b * BLK + rows.start, 16), 16)] = value

            each_rows(BLK, 16, norm)
        for c in range(3):
            cols = pl.ds(c * 256, 256)
            weight = att_full[:, :, :, :, cols].reshape(D, 256)
            proj[s, :, cols] = dot(normed[s], weight)

    def attend(s):
        for h in range(2):
            for c, factor in ((0, HD ** (-0.5)), (1, 1.0)):
                cols = pl.ds(c * 256 + h * HD, HD)
                v = proj[s, :, cols]
                scale = lax.rsqrt(jnp.mean(v * v, axis=-1, keepdims=True) + EPS)
                v = v * scale * head_gains[c : c + 1, h * HD : (h + 1) * HD]
                v = (v * cos[...] + turn_half(v) * sin[...]) * factor
                qkv[s, :, cols] = v.astype(BF16)
        qkv[s, :, 512:768] = proj[s, :, 512:768].astype(BF16)
        for h in range(2):
            q, k, v = (qkv[s, :, pl.ds(c * 256 + h * HD, HD)] for c in range(3))
            scores = dot(q, k, ((1,), (1,)))
            weights = jnp.exp(scores - jnp.max(scores, axis=-1, keepdims=True))
            weights = weights * live_both[s, 0:1].astype(F32)
            probs = (weights / jnp.sum(weights, axis=-1, keepdims=True)).astype(BF16)
            attended[s, :, pl.ds(h * HD, HD)] = dot(probs, v).astype(BF16)
        for n in range(4):
            weight = att_full[n // 2, pl.ds(n % 2 * 2, 2), :, :, 768:1024].reshape(512, 256)
            part = dot(attended[s], weight, ((1,), (1,))).astype(BF16)
            branch[s, :, :, :, pl.ds(n * 512, 512)] = part.reshape(2, 2, BLK, 512)

    first, second = xl, 1 - xl
    project(first)
    attend(first)
    low, high = pl.ds(0, 32), pl.ds(32, 32)
    exp_relay = []
    for copy, device, part in (
        (exp_near[0], p.at(dy=1), near_rows.at[left, low]),
        (exp_near[1], p.at(dy=3), near_rows.at[right, high]),
        (exp_far[0], p.at(dz=1), far_rows.at[below, low]),
        (exp_far[1], p.at(dz=3), far_rows.at[above, high]),
    ):
        copy.wait_recv()
        exp_relay.append(w.to(device, part, part))
    sums.begin((2, 0))
    project(second)
    cots.relay()
    sums.start()
    for copy in exp_relay:
        copy.wait_recv()
    mine_z = exp_full.at[xl, :, z]
    mine_y = exp_full.at[1 - xl, y]
    kept, last = pl.ds(0, KEPT), pl.ds(KEPT, EW - KEPT)
    near_kept, far_kept = near_rows.at[:, :, kept], far_rows.at[:, :, kept]
    exp_up = [w.to(p.at(dz=k), near_kept, mine_z) for k in (1, 3)]
    exp_up += [w.to(p.at(dy=k), far_kept, mine_y) for k in (1, 3)]
    local += [w.here(near_kept, mine_z), w.here(far_kept, mine_y)]
    local += [
        w.here(near_rows.at[:, :, last], near_last),
        w.here(far_rows.at[:, :, last], far_last),
    ]
    attend(second)
    sums.begin((1, 3))
    cots.forward()
    local += [w.here(normed, normed_out), w.here(proj, proj_out)]
    sums.ahead()
    sums.pass_on()
    sums.arrive()

    def norm(rows):
        now = x_own[rows].astype(F32) + sums.total(rows)
        state[rows] = now
        scale = lax.rsqrt(jnp.mean(now * now, axis=-1, keepdims=True) + EPS)
        block[rows] = (now * scale * gains[1:2]).astype(BF16)

    each_rows(BLK, 16, norm)
    mids = Spread(w, p, block, mid_all)
    mids.relay()
    exp_end = pass_along(exp_up, exp_full, kept)
    mids.forward()
    mids.arrived()
    cots.arrived()
    for copy in masks[1:]:
        copy.wait_recv()
    for copy in exp_end:
        copy.wait_recv()
    for copy in local:
        copy.wait()
    for group in (tokens, cots, mids, sums):
        group.finish()
    for copy in (
        smalls + [att_swap, small_swap, exp_swap] + masks + att_near + att_far + att_up
        + att_end + exp_near + exp_far + exp_relay + exp_up + exp_end
    ):
        copy.wait_send()


def forward(
    lengths, x_own, cot_own, w_qkv, w_out, w_gate_up, w_down, gains, router, ids, cos, sin
):
    cell = jax.ShapeDtypeStruct((2, 2, 2, BLK, D), BF16)
    return pl.pallas_call(
        forward_kernel,
        name="forward",
        out_shape=[
            cell,
            cell,
            jax.ShapeDtypeStruct((2, 4, 4, 64, KEPT), BF16),
            jax.ShapeDtypeStruct((4, 64, EW - KEPT), BF16),
            jax.ShapeDtypeStruct((4, 64, EW - KEPT), BF16),
            jax.ShapeDtypeStruct((2, 4, 4, 64, AW), BF16),
            jax.ShapeDtypeStruct((2, SEQ, D), BF16),
            jax.ShapeDtypeStruct((2, SEQ, 768), F32),
            jax.ShapeDtypeStruct((2, SEQ, 768), BF16),
            jax.ShapeDtypeStruct((2, SEQ, 256), BF16),
            jax.ShapeDtypeStruct((BLK, D), F32),
            jax.ShapeDtypeStruct((8, D), F32),
            jax.ShapeDtypeStruct((8, 256), F32),
            jax.ShapeDtypeStruct((D, 128), BF16),
            jax.ShapeDtypeStruct((2, SEQ, 128), BF16),
            jax.ShapeDtypeStruct((2, 16, SEQ), BF16),
        ],
        in_specs=[pl.BlockSpec(memory_space=pltpu.SMEM)] + [VMEM] * 11,
        out_specs=[ANY] * 8 + [VMEM] * 6 + [ANY] * 2,
        scratch_shapes=[
            pltpu.VMEM((2, 2, 2, BLK, D), BF16),
            pltpu.VMEM((2, 4, 4, 64, AW), BF16),
            pltpu.VMEM((2, 16, SEQ), BF16),
            pltpu.VMEM((4, 64, EW), BF16),
            pltpu.VMEM((4, 64, EW), BF16),
            pltpu.VMEM((2, SEQ, D), BF16),
            pltpu.VMEM((2, SEQ, 768), F32),
            pltpu.VMEM((2, 2, 2, BLK, D), BF16),
        ]
        + collect_scratch(D, BF16, False)
        + [
            pltpu.VMEM((BLK, D), BF16),
            pltpu.VMEM((2, 64, 1024), BF16),
            pltpu.VMEM((2, 64, EW), BF16),
            pltpu.VMEM((128, 128), F32),
            pltpu.VMEM((16, 128), BF16),
            pltpu.VMEM((SEQ, 128), BF16),
            pltpu.VMEM((16, SEQ), BF16),
        ]
        + wire_scratch(96, 20),
        compiler_params=params(0, 60),
    )(lengths, x_own, cot_own, w_qkv, w_out, w_gate_up, w_down, gains, router, ids, cos, sin)


def split_dot(value, other, dims):
    high = value.astype(BF16)
    low = (value - high.astype(F32)).astype(BF16)
    dot = functools.partial(
        lax.dot_general, dimension_numbers=(dims, ((), ())), preferred_element_type=F32
    )
    return dot(high, other) + dot(low, other)


def norm_back(value, gain, grad):
    scale = lax.rsqrt(jnp.mean(value * value, axis=-1, keepdims=True) + EPS)
    shaped = grad * gain
    along = jnp.mean(shaped * value, axis=-1, keepdims=True)
    return scale * shaped - value * (scale * scale * scale * along), grad * value * scale


class Reduce:
    def __init__(self, wires, up, down, blocks, here, halves, mains, stage=None):
        self.wires, self.up, self.down = wires, up, down
        self.blocks, self.here, self.halves, self.mains = blocks, here, halves, mains
        self.stage = stage
        self.first, self.second, self.loading = {}, {}, {}

    def begin(self, group):
        at, to, width = group
        opposite = self.blocks(lax.rem(self.here + 2, 4))
        span = pl.ds(at, width)
        self.first[group] = [
            self.wires.to(
                device,
                opposite.at[pl.ds(side * 2, 2), :, span],
                self.halves.at[side, :, :, pl.ds(to, width)],
            )
            for side, device in ((0, self.up), (1, self.down))
        ]

    def relay(self, group):
        at, to, width = group
        span, wide = pl.ds(at, width), pl.ds(to, width)
        self.second[group] = []
        for side, device in ((0, self.up), (1, self.down)):
            self.first[group][side].wait_recv()
            block = self.blocks(lax.rem(self.here + (1 if side == 0 else 3), 4))
            for b in range(2):
                cell = (side * 2 + b, slice(None), span)
                total = block[cell].astype(F32) + self.halves[side, b, :, wide].astype(F32)
                block[cell] = total.astype(BF16)
            self.second[group].append(
                self.wires.to(device, block.at[:, :, span], self.mains.at[side, :, :, wide])
            )

    def fetch(self, group):
        _, to, width = group
        for copy in self.second[group]:
            copy.wait_recv()
        if self.stage is not None:
            self.loading[group] = self.wires.here(
                self.mains.at[:, :, :, pl.ds(to, width)], self.stage
            )

    def total(self, group, store):
        at, to, width = group
        span, wide = pl.ds(at, width), pl.ds(to, width)
        if self.stage is not None:
            self.loading[group].wait()
        own = self.blocks(self.here)
        for b in range(4):
            total = own[b, :, span].astype(F32)
            for side in range(2):
                if self.stage is not None:
                    total = total + self.stage[side, b].astype(F32)
                else:
                    total = total + self.mains[side, b, :, wide].astype(F32)
            store(b, total)

    def sent(self, group):
        for copy in self.first.pop(group) + self.second.pop(group):
            copy.wait_send()

    def finish(self):
        for group in list(self.first):
            self.sent(group)


TILE = 256
EXPERT = 3 * FFS
SLOTS = 3


def expert_kernel(
    mid, cot, w_exp, near_last, far_last, mask, small, state, cot_own, gains,
    branch_grad, w_last, mixed, near_rows, far_rows, near_main, far_main,
    state_grad, gain_grad, logit_grad,
    mid_here, cot_here, weight, pre_grad, gated, dw, near_half, far_half, near_stage, far_stage,
    mid_part, mix_out, soft, route, got, half, arrived, across,
    rgot, rhalf, rarrived, racross, block,
    send, recv, near,
):
    p = Place()
    w = Wires(send, recv, near)
    xl, y, z, t = p.xl, p.y, p.z, p.t

    def source(e, cols=(0, EXPERT)):
        if e == HALF_E - 1:
            return w_last, pl.ds(*cols)
        return w_exp, pl.ds(e * EXPERT + cols[0], cols[1])

    def fetch(e):
        full, cols = source(e)
        return w.here(full.at[:, :, :, :, cols], weight.at[e % 2])

    stage_in = [w.here(near_last, near_stage.at[0]), w.here(far_last, far_stage.at[0])]
    loads = [w.here(mid, mid_here), fetch(0), w.here(cot, cot_here)]
    ready = {0: loads[1], 1: fetch(1)}
    greet(cell_peers(p) + [p.at(dy=1), p.at(dy=3), p.at(dz=1), p.at(dz=3)])
    for copy in stage_in:
        copy.wait()
    mine_z, mine_y = w_last.at[xl, :, z], w_last.at[1 - xl, y]
    last_up = [w.to(p.at(dz=k), near_stage.at[0], mine_z) for k in (1, 3)]
    last_up += [w.to(p.at(dy=k), far_stage.at[0], mine_y) for k in (1, 3)]
    last_local = [w.here(near_stage.at[0], mine_z), w.here(far_stage.at[0], mine_y)]

    def pass_last():
        steps = (
            (p.at(dz=1), w_last.at[xl, pl.ds(0, 2), lax.rem(z + 3, 4)]),
            (p.at(dz=3), w_last.at[xl, pl.ds(2, 2), lax.rem(z + 1, 4)]),
            (p.at(dy=1), w_last.at[1 - xl, lax.rem(y + 3, 4), pl.ds(0, 2)]),
            (p.at(dy=3), w_last.at[1 - xl, lax.rem(y + 1, 4), pl.ds(2, 2)]),
        )
        sent = []
        for copy, (device, part) in zip(last_up, steps):
            copy.wait_recv()
            sent.append(w.to(device, part, part))
        return sent

    along_z = Reduce(
        w, p.at(dz=1), p.at(dz=3), lambda k: dw.at[xl, :, k], z,
        near_half, near_main, near_stage,
    )
    along_y = Reduce(
        w, p.at(dy=1), p.at(dy=3), lambda k: dw.at[1 - xl, k], y,
        far_half, far_main, far_stage,
    )
    groups = [(e % SLOTS * EXPERT, e * EXPERT, EXPERT) for e in range(HALF_E)]
    loads[0].wait()
    for n in range(ROWS // TILE):
        rows = pl.ds(n * TILE, TILE)
        logits = dot(mid_here[rows], small[...])
        on = mask[rows] > 0
        peak = jnp.max(jnp.where(on, logits, -1e30), axis=-1, keepdims=True)
        chance = jnp.where(on, jnp.exp(jnp.where(on, logits - peak, 0.0)), 0.0)
        soft[rows] = chance / jnp.maximum(jnp.sum(chance, axis=-1, keepdims=True), 1.0)
    route[...] = jnp.zeros_like(route)
    lane = lax.broadcasted_iota(jnp.int32, (TILE, 128), 1)
    loads[2].wait()

    def expert(e):
        ready[e].wait()
        here = lane == ROUTER_AT + xl * HALF_E + e
        for n in range(ROWS // TILE):
            rows = pl.ds(n * TILE, TILE)
            gate = jnp.sum(jnp.where(here, soft[rows], 0.0), axis=-1, keepdims=True)
            pre = dot(
                mid_here[rows], weight[e % 2, :, :, :, :, : 2 * FFS].reshape(D, 2 * FFS)
            )
            hidden = dot(cot_here[rows], weight[e % 2, :, :, :, :, 2 * FFS :].reshape(D, FFS))
            gate_pre, up_pre = pre[:, :FFS], pre[:, FFS:]
            sig = 1.0 / (1.0 + jnp.exp(-gate_pre))
            silu = gate_pre * sig
            inner = (silu * up_pre).astype(BF16).astype(F32)
            routed = jnp.where(here, jnp.sum(inner * hidden, axis=-1, keepdims=True), 0.0)
            route[n // 2, n % 2] += routed.reshape(2, BLK, 128)
            gated[rows, pl.ds(e * FFS, FFS)] = (gate * inner).astype(BF16)
            hidden = gate * hidden
            pre_grad[rows, pl.ds(e * 512, FFS)] = (
                hidden * up_pre * (sig + silu * (1.0 - sig))
            ).astype(BF16)
            pre_grad[rows, pl.ds(e * 512 + FFS, FFS)] = (hidden * silu).astype(BF16)

    def weight_grads(e):
        at = groups[e][0]
        for n in range(4):
            cols = pl.ds(n * 512, 512)
            to = (n // 2, pl.ds(n % 2 * 2, 2), slice(None), slice(None))
            grad = dot(mid_here[:, cols], pre_grad[:, pl.ds(e * 512, 512)], ((0,), (0,)))
            dw[(*to, pl.ds(at, 512))] = grad.astype(BF16).reshape(2, 4, 64, 512)
            grad = dot(cot_here[:, cols], gated[:, pl.ds(e * FFS, FFS)], ((0,), (0,)))
            dw[(*to, pl.ds(at + 512, FFS))] = grad.astype(BF16).reshape(2, 4, 64, FFS)
        along_z.begin(groups[e])
        along_y.begin(groups[e])

    def relay(e):
        along_z.relay(groups[e])
        along_y.relay(groups[e])

    def retire(e):
        along_z.fetch(groups[e])
        along_y.fetch(groups[e])
        out = []
        for along, own, rows_out in (
            (along_z, dw.at[xl, :, z], near_rows),
            (along_y, dw.at[1 - xl, y], far_rows),
        ):
            at, to, width = groups[e]
            span = pl.ds(at, width)

            def store(b, total, own=own, span=span):
                own[b, :, span] = total.astype(BF16)

            along.total(groups[e], store)
            out.append(w.here(own.at[:, :, span], rows_out.at[:, :, pl.ds(to, width)]))
            along.sent(groups[e])
        return out

    def rows_fetch(n):
        copies = []
        for e in range(HALF_E):
            full, cols = source(e)
            copies.append(
                w.here(
                    full.at[n // 4, n % 4, :, :, cols], weight.at[(n + 1) % 2, e // 4, e % 4]
                )
            )
        return copies

    expert(0)
    last_end = pass_last()
    ready[2] = fetch(2)
    weight_grads(0)
    expert(1)
    ready[3] = fetch(3)
    relay(0)
    weight_grads(1)
    expert(2)
    for copy in last_end:
        copy.wait_recv()
    for copy in last_local:
        copy.wait()
    for copy in last_up:
        copy.wait_send()
    ready[4] = fetch(4)
    relay(1)
    weight_grads(2)
    expert(3)
    chunk = {0: rows_fetch(0)}
    expert(4)
    relay(2)
    chunk[1] = rows_fetch(1)
    routes = Collect(w, p, route, rgot, None, rhalf, rarrived, racross)
    routes.begin()
    sums = Collect(w, p, mid_part, got, None, half, arrived, across)
    chunks = D // TILE
    for n in range(chunks):
        for copy in chunk[n]:
            copy.wait()
        slot = (n + 1) % 2
        for r in range(2):
            total = None
            for e in range(HALF_E):
                part = dot(
                    pre_grad[r * SEQ : (r + 1) * SEQ, e * 512 : (e + 1) * 512],
                    weight[slot, e // 4, e % 4, :, :, :512].reshape(TILE, 512),
                    ((1,), (1,)),
                )
                total = part if e == 0 else total + part
            mid_part[r, :, :, :, pl.ds(n * TILE, TILE)] = total.astype(BF16).reshape(
                2, 2, BLK, TILE
            )
        if n + 2 < chunks:
            chunk[n + 2] = rows_fetch(n + 2)

    def down_fetch(n):
        copies = []
        for e in range(HALF_E):
            full, cols = source(e, (512, FFS))
            copies.append(
                w.here(
                    full.at[n // 2, pl.ds(n % 2 * 2, 2), :, :, cols],
                    weight.at[
                        (n + 1) % 2, 0, pl.ds(e // 3 * 2, 2), :, :, pl.ds(e % 3 * FFS, FFS)
                    ],
                )
            )
        return copies

    sums.begin()
    downs = {0: down_fetch(0), 1: down_fetch(1)}
    routes.start()
    routes.ahead()
    out = retire(0)
    for copy in out:
        copy.wait()
    weight_grads(3)
    sums.start()
    sums.ahead()
    routes.pass_on()
    out = retire(1)
    for copy in out:
        copy.wait()
    weight_grads(4)
    sums.pass_on()
    relay(3)
    mixing = {}
    for n in range(4):
        for copy in downs[n]:
            copy.wait()
        for r in range(2):
            if n > 0:
                mixing[n - 1, r].wait()
            total = None
            for e in range(HALF_E):
                at, cols = e // 3 * 2, pl.ds(e % 3 * FFS, FFS)
                part = dot(
                    gated[r * SEQ : (r + 1) * SEQ, e * FFS : (e + 1) * FFS],
                    weight[(n + 1) % 2, 0, at : at + 2, :, :, cols].reshape(512, FFS),
                    ((1,), (1,)),
                )
                total = part if e == 0 else total + part
            mix_out[r] = total.astype(BF16)
            mixing[n, r] = w.here(
                mix_out.at[r], mixed.at[pl.ds(r * SEQ, SEQ), pl.ds(n * 512, 512)]
            )
        if n + 2 < 4:
            downs[n + 2] = down_fetch(n + 2)
    routes.arrive()

    def router(rows):
        chance = soft[pl.ds(pl.multiple_of((xl * 4 + t) * BLK + rows.start, 16), 16)]
        grad = routes.total(rows)
        grad = chance * (grad - jnp.sum(chance * grad, axis=-1, keepdims=True))
        logit_grad[rows] = grad

    each_rows(BLK, 16, router)
    state_grad[...] = split_dot(logit_grad[...], small[...], ((1,), (1,)))
    sums.arrive()
    gain_grad[...] = jnp.zeros_like(gain_grad)

    def back(rows):
        grad = sums.total(rows) + state_grad[rows]
        change, gain_part = norm_back(state[rows], gains[1:2], grad)
        total = cot_own[rows].astype(F32) + change
        state_grad[rows] = total
        block[rows] = total.astype(BF16)
        gain_grad[0:1] += jnp.sum(gain_part, axis=0, keepdims=True)

    each_rows(BLK, 16, back)
    tokens = Spread(w, p, block, branch_grad)
    relay(4)
    out = retire(2)
    tokens.relay()
    out += retire(3)
    tokens.forward()
    out += retire(4)
    tokens.arrived()
    for copy in out + [mixing[3, 0], mixing[3, 1]]:
        copy.wait()
    for group in (tokens, sums, routes, along_z, along_y):
        group.finish()
    for copy in last_end:
        copy.wait_send()


def experts(mid, cot, w_exp, near_last, far_last, mask, small, state, cot_own, gains):
    part = jax.ShapeDtypeStruct((4, 64, EW), BF16)
    landing = jax.ShapeDtypeStruct((2, 4, 64, EW), BF16)
    return pl.pallas_call(
        expert_kernel,
        name="experts",
        out_shape=[
            jax.ShapeDtypeStruct((2, 2, 2, BLK, D), BF16),
            jax.ShapeDtypeStruct((2, 4, 4, 64, EW - KEPT), BF16),
            jax.ShapeDtypeStruct((ROWS, D), BF16),
            part,
            part,
            landing,
            landing,
            jax.ShapeDtypeStruct((BLK, D), F32),
            jax.ShapeDtypeStruct((8, D), F32),
            jax.ShapeDtypeStruct((BLK, 128), F32),
        ],
        in_specs=[ANY] * 5 + [VMEM] * 5,
        out_specs=[ANY] * 7 + [VMEM] * 3,
        scratch_shapes=[
            pltpu.VMEM((ROWS, D), BF16),
            pltpu.VMEM((ROWS, D), BF16),
            pltpu.VMEM((2, 2, 4, 4, 64, EXPERT), BF16),
            pltpu.VMEM((ROWS, GU), BF16),
            pltpu.VMEM((ROWS, EW - GU), BF16),
            pltpu.VMEM((2, 4, 4, 64, SLOTS * EXPERT), BF16),
            pltpu.VMEM((2, 2, 64, EW), BF16),
            pltpu.VMEM((2, 2, 64, EW), BF16),
            pltpu.VMEM((2, 4, 64, EXPERT), BF16),
            pltpu.VMEM((2, 4, 64, EXPERT), BF16),
            pltpu.VMEM((2, 2, 2, BLK, D), BF16),
            pltpu.VMEM((2, SEQ, 512), BF16),
            pltpu.VMEM((ROWS, 128), F32),
            pltpu.VMEM((2, 2, 2, BLK, 128), F32),
        ]
        + collect_scratch(D, BF16, False)
        + collect_scratch(128, F32, False)
        + [pltpu.VMEM((BLK, D), BF16)]
        + wire_scratch(88, 120),
        compiler_params=params(2, 62),
    )(mid, cot, w_exp, near_last, far_last, mask, small, state, cot_own, gains)


QKV_GROUP = (0, 0, 768)
SMALL_GROUP = (768, 768, 128)
OUT_GROUP = (896, 896, 256)


def backward_kernel(
    bg_in, w_att_in, normed_in, proj_in, qkv_in, attended_in, mixed, near_rows, far_rows, mid_all,
    logit_grad, mid_gain, state, state_grad, x_own, gains, head_gains, cos, sin, live,
    input_grad, output, exp_sum, att_sum, small_sum,
    bg, w_att, normed, proj, qkv, attended, mid_own, att_bg, proj_grad, in_part, in_gain,
    head_gain, small_rows, attg, near_half, far_half, near_main, far_main,
    got, half, arrived, across, mgot, mown, mhalf, marrived, macross,
    near_in, far_in, far_sum, att_near, att_far, att_near_end, att_far_end, att_far_sum,
    exp_got, att_got, small_all, small_in, send, recv, near,
):
    p = Place()
    w = Wires(send, recv, near)
    xl, y, z, t = p.xl, p.y, p.z, p.t
    greet(cell_peers(p) + plane_peers(p) + [p.at(dx=2, dc=1)])
    mixes = Collect(w, p, mixed, mgot, mown, mhalf, marrived, macross)
    mixes.begin()
    loads = [
        w.here(a, b)
        for a, b in (
            (bg_in, bg),
            (w_att_in, w_att),
            (attended_in, attended),
            (qkv_in, qkv),
            (proj_in, proj),
            (normed_in, normed),
            (mid_all.at[xl, p.xh, p.c], mid_own),
        )
    ]
    exps = []
    for k in (1, 3, 2):
        to_z, to_y = lax.rem(z + k, 4), lax.rem(y + k, 4)
        exps.append(w.to(p.at(dy=k), near_rows.at[to_y], near_in.at[k - 1]))
        exps.append(w.to(p.at(dz=k), far_rows.at[to_z], far_in.at[k - 1]))
    local = [
        w.here(near_rows.at[y], near_in.at[3]),
        w.here(far_rows.at[z], far_in.at[3]),
    ]
    along_z = Reduce(
        w, p.at(dz=1), p.at(dz=3), lambda k: attg.at[xl, :, k], z, near_half, near_main
    )
    along_y = Reduce(
        w, p.at(dy=1), p.at(dy=3), lambda k: attg.at[1 - xl, k], y, far_half, far_main
    )
    in_gain[...] = jnp.zeros_like(in_gain)
    head_gain[...] = jnp.zeros_like(head_gain)
    for copy in loads[:3]:
        copy.wait()
    mixes.start()
    mixes.ahead()
    for s in range(2):
        att_bg[s] = dot(bg[s], w_att[:, 768:1024]).astype(BF16)
    for copy in loads[3:]:
        copy.wait()

    def heads(s):
        for h in range(2):
            head = pl.ds(h * HD, HD)
            q, k, v = (qkv[s, :, pl.ds(c * 256 + h * HD, HD)] for c in range(3))
            scores = dot(q, k, ((1,), (1,)))
            weights = jnp.exp(scores - jnp.max(scores, axis=-1, keepdims=True))
            weights = weights * live[s, 0:1].astype(F32)
            probs = weights / jnp.sum(weights, axis=-1, keepdims=True)
            out_grad = att_bg[s, :, head]
            prob_grad = dot(out_grad, v, ((1,), (1,)))
            inner = jnp.sum(probs * prob_grad, axis=-1, keepdims=True)
            score_grad = (probs * (prob_grad - inner)).astype(BF16)
            value_grad = dot(probs.astype(BF16), out_grad, ((0,), (0,)))
            proj_grad[s, :, pl.ds(512 + h * HD, HD)] = value_grad.astype(BF16)
            both = (
                (0, dot(score_grad, k) * HD ** (-0.5)),
                (1, dot(score_grad, q, ((0,), (0,)))),
            )
            for c, grad in both:
                cols = pl.ds(c * 256 + h * HD, HD)
                grad = grad * cos[...] - turn_half(grad) * sin[...]
                gain = head_gains[c : c + 1, h * HD : (h + 1) * HD]
                change, gain_part = norm_back(proj[s, :, cols], gain, grad)
                proj_grad[s, :, cols] = change.astype(BF16)
                head_gain[c : c + 1, h * HD : (h + 1) * HD] += jnp.sum(
                    gain_part, axis=0, keepdims=True
                )

    def inputs(s):
        for b in range(4):
            rows = pl.ds(b * BLK, BLK)
            part = dot(proj_grad[s, rows], w_att[:, :768], ((1,), (1,)))
            in_part[s, b // 2, b % 2] = part.astype(BF16)
            in_gain[0:1] += jnp.sum(part * normed[s, rows].astype(F32), axis=0, keepdims=True)

    def weight_rows(left, right, at, width):
        for n in range(4):
            cols = pl.ds(n * 512, 512)
            grad = dot(left(0, cols), right(0), ((0,), (0,)))
            grad = grad + dot(left(1, cols), right(1), ((0,), (0,)))
            attg[n // 2, pl.ds(n % 2 * 2, 2), :, :, pl.ds(at, width)] = grad.astype(BF16).reshape(
                2, 4, 64, width
            )

    sums = Collect(w, p, in_part, got, None, half, arrived, across)
    first, second = xl, 1 - xl
    weight_rows(lambda s, cols: bg[s, :, cols], lambda s: attended[s], 896, 256)
    along_z.begin(OUT_GROUP)
    along_y.begin(OUT_GROUP)
    heads(first)
    mixes.pass_on()
    heads(second)
    along_z.relay(OUT_GROUP)
    along_y.relay(OUT_GROUP)
    weight_rows(lambda s, cols: normed[s, :, cols], lambda s: proj_grad[s], 0, 768)
    along_z.begin(QKV_GROUP)
    along_y.begin(QKV_GROUP)
    for copy in local:
        copy.wait()
    for copy in exps:
        copy.wait_recv()

    def exp_far(rows):
        total = far_in[3, rows].astype(F32)
        for k in range(3):
            total = total + far_in[k, rows].astype(F32)
        far_sum[rows] = total.astype(BF16)

    each_rows(64, 16, exp_far)
    exp_swap = w.to(p.partner(), far_sum, exp_got)
    inputs(first)
    sums.begin((2, 0))
    inputs(second)
    sums.begin((1, 3))
    sums.start()
    sums.ahead()

    small_rows[...] = jnp.zeros_like(small_rows)
    small_rows[0:1] = in_gain[0:1] / gains[0:1]
    small_rows[1:2] = mid_gain[0:1]
    start = pl.multiple_of(t * 512 + xl * 256, 256)
    small_rows[2:4, pl.ds(start, 256)] = head_gain[0:2]
    high = logit_grad[...].astype(BF16)
    low = (logit_grad[...] - high.astype(F32)).astype(BF16)
    for n in range(16):
        cols = pl.ds(n * 128, 128)
        strip = dot(mid_own[:, cols], high, ((0,), (0,))) + dot(mid_own[:, cols], low, ((0,), (0,)))
        strip = strip + jnp.transpose(small_rows[:, cols])
        attg[n // 8, n % 8 // 2, pl.ds(n % 2 * 2, 2), :, pl.ds(768, 128)] = strip.astype(
            BF16
        ).reshape(2, 64, 128)
    along_z.begin(SMALL_GROUP)
    along_y.begin(SMALL_GROUP)
    along_z.relay(QKV_GROUP)
    along_y.relay(QKV_GROUP)
    sums.pass_on()

    along_z.relay(SMALL_GROUP)
    along_y.relay(SMALL_GROUP)
    for group in (OUT_GROUP, QKV_GROUP, SMALL_GROUP):
        for along, rows_ref in ((along_z, att_near), (along_y, att_far)):

            def store(b, total, rows_ref=rows_ref, group=group):
                rows_ref[b, :, pl.ds(group[1], group[2])] = total.astype(BF16)

            along.fetch(group)
            along.total(group, store)
    ends = []
    for k in (1, 3, 2):
        to_z, to_y = lax.rem(z + k, 4), lax.rem(y + k, 4)
        ends.append(w.to(p.at(dz=k), att_far.at[to_z], att_far_end.at[k - 1]))
        ends.append(w.to(p.at(dy=k), att_near.at[to_y], att_near_end.at[k - 1]))
    mixes.arrive()

    def finish(rows):
        output[rows] = (state[rows] + mixes.total(rows)).astype(BF16)

    each_rows(BLK, 16, finish)

    def exp_near(rows):
        total = near_in[3, rows].astype(F32)
        for k in range(3):
            total = total + near_in[k, rows].astype(F32)
        exp_sum[xl, rows] = total

    each_rows(64, 16, exp_near)
    for copy in ends:
        copy.wait_recv()

    def att_far_add(rows):
        total = att_far[z, rows].astype(F32)
        for k in range(3):
            total = total + att_far_end[k, rows].astype(F32)
        att_far_sum[rows] = total.astype(BF16)

    each_rows(64, 16, att_far_add)
    att_swap = w.to(p.partner(), att_far_sum, att_got)

    sums.arrive()

    def back(rows):
        change, _ = norm_back(x_own[rows].astype(F32), gains[0:1], sums.total(rows))
        input_grad[rows] = state_grad[rows] + change

    each_rows(BLK, 16, back)
    exp_swap.wait_recv()
    exp_sum[1 - xl] = exp_got[...].astype(F32)

    def att_near_add(rows):
        total = att_near[y, rows].astype(F32)
        for k in range(3):
            total = total + att_near_end[k, rows].astype(F32)
        att_sum[xl, rows] = total

    each_rows(64, 16, att_near_add)
    att_swap.wait_recv()
    att_sum[1 - xl] = att_got[...].astype(F32)
    small_all[...] = att_sum[0, :, 768:896] + att_sum[1, :, 768:896]
    smalls = []
    for n, (a, b) in enumerate(((0, 1), (2, 0), (2, 1))):
        dest = lax.rem(p.xh + a // 2, 2) * 2 + lax.rem(p.c + b, 2)
        smalls.append(
            w.to(
                p.at(dx=a, dc=b),
                small_all.at[pl.ds(pl.multiple_of(dest * 16, 16), 16)],
                small_in.at[n],
            )
        )
    for copy in smalls:
        copy.wait_recv()
    total = small_all[pl.ds(pl.multiple_of(t * 16, 16), 16)]
    for n in range(3):
        total = total + small_in[n]
    small_sum[...] = total
    for group in (sums, mixes, along_z, along_y):
        group.finish()
    for copy in exps + ends + [exp_swap, att_swap] + smalls:
        copy.wait_send()


def backward(
    bg, w_att, normed, proj, qkv, attended, mixed, near_rows, far_rows, mid_all,
    logit_grad, mid_gain, state, state_grad, x_own, gains, head_gains, cos, sin, live,
):
    return pl.pallas_call(
        backward_kernel,
        name="backward",
        out_shape=[
            jax.ShapeDtypeStruct((BLK, D), F32),
            jax.ShapeDtypeStruct((BLK, D), BF16),
            jax.ShapeDtypeStruct((2, 64, EW), F32),
            jax.ShapeDtypeStruct((2, 64, AW), F32),
            jax.ShapeDtypeStruct((16, 128), F32),
        ],
        in_specs=[ANY] * 10 + [VMEM] * 10,
        out_specs=[VMEM] * 5,
        scratch_shapes=[
            pltpu.VMEM((2, SEQ, D), BF16),
            pltpu.VMEM((D, AW), BF16),
            pltpu.VMEM((2, SEQ, D), BF16),
            pltpu.VMEM((2, SEQ, 768), F32),
            pltpu.VMEM((2, SEQ, 768), BF16),
            pltpu.VMEM((2, SEQ, 256), BF16),
            pltpu.VMEM((BLK, D), BF16),
            pltpu.VMEM((2, SEQ, 256), BF16),
            pltpu.VMEM((2, SEQ, 768), BF16),
            pltpu.VMEM((2, 2, 2, BLK, D), BF16),
            pltpu.VMEM((8, D), F32),
            pltpu.VMEM((8, 256), F32),
            pltpu.VMEM((128, D), F32),
            pltpu.VMEM((2, 4, 4, 64, AW), BF16),
            pltpu.VMEM((2, 2, 64, AW), BF16),
            pltpu.VMEM((2, 2, 64, AW), BF16),
            pltpu.VMEM((2, 4, 64, AW), BF16),
            pltpu.VMEM((2, 4, 64, AW), BF16),
        ]
        + collect_scratch(D, BF16, False)
        + collect_scratch(D, BF16, True)
        + [
            pltpu.VMEM((4, 64, EW), BF16),
            pltpu.VMEM((4, 64, EW), BF16),
            pltpu.VMEM((64, EW), BF16),
            pltpu.VMEM((4, 64, AW), BF16),
            pltpu.VMEM((4, 64, AW), BF16),
            pltpu.VMEM((3, 64, AW), BF16),
            pltpu.VMEM((3, 64, AW), BF16),
            pltpu.VMEM((64, AW), BF16),
            pltpu.VMEM((64, EW), BF16),
            pltpu.VMEM((64, AW), BF16),
            pltpu.VMEM((64, 128), F32),
            pltpu.VMEM((3, 16, 128), F32),
        ]
        + wire_scratch(72, 20),
        compiler_params=params(3, 62),
    )(
        bg, w_att, normed, proj, qkv, attended, mixed, near_rows, far_rows, mid_all,
        logit_grad, mid_gain, state, state_grad, x_own, gains, head_gains, cos, sin, live,
    )


def finish_kernel(
    input_grad, output, exp_sum, att_sum, small_sum,
    output_out, input_out, gains_out, qkv_out, out_out, router_out, gate_up_out, down_out,
):
    output_out[...] = output[...]
    input_out[...] = input_grad[...]
    gains_out[...] = jnp.transpose(small_sum[...])[:4]
    router_out[...] = pltpu.roll(small_sum[...], 128 - ROUTER_AT, 1)[:, :E]
    for h in range(2):
        for c in range(3):
            qkv_out[c, :, h * 256 : (h + 1) * 256] = att_sum[h, :, c * 256 : (c + 1) * 256]
        out_out[:, h * 256 : (h + 1) * 256] = att_sum[h, :, 896:1152]
        for e in range(HALF_E):
            for g in range(2):
                at = (e * 3 + g) * FFS
                gate_up_out[h * HALF_E + e, g] = exp_sum[h, :, at : at + FFS]
            at = (e * 3 + 2) * FFS
            down_out[h * HALF_E + e] = exp_sum[h, :, at : at + FFS]


def finish(input_grad, output, exp_sum, att_sum, small_sum):
    return pl.pallas_call(
        finish_kernel,
        name="finish",
        out_shape=[
            jax.ShapeDtypeStruct((BLK, D), BF16),
            jax.ShapeDtypeStruct((BLK, D), F32),
            jax.ShapeDtypeStruct((4, 16), F32),
            jax.ShapeDtypeStruct((3, 64, 512), F32),
            jax.ShapeDtypeStruct((64, 512), F32),
            jax.ShapeDtypeStruct((16, E), F32),
            jax.ShapeDtypeStruct((E, 2, 64, FFS), F32),
            jax.ShapeDtypeStruct((E, 64, FFS), F32),
        ],
        in_specs=[VMEM] * 5,
        out_specs=[VMEM] * 8,
        compiler_params=params(),
    )(input_grad, output, exp_sum, att_sum, small_sum)


def rotary_tables():
    half = HD // 2
    freqs = np.float32(THETA) ** (-(np.arange(half, dtype=np.float32) * np.float32(2.0 / HD)))
    angles = np.arange(SEQ, dtype=np.float32)[:, None] * freqs[None, :].astype(np.float32)
    cos, sin = np.cos(angles), np.sin(angles)
    return (
        np.concatenate([cos, cos], axis=1).astype(np.float32),
        np.concatenate([-sin, sin], axis=1).astype(np.float32),
    )


def local(
    layer_input, cotangent, lengths, expert_ids, gains, w_qkv, w_out, w_router, w_gate_up, w_down
):
    cos, sin = (jnp.asarray(table) for table in rotary_tables())
    (
        cot_all, mid_all, w_exp, near_last, far_last, att_full, normed, proj, qkv, attended,
        state, gain_rows,
        head_gains, w_small, mask_both, live_both,
    ) = forward(
        lengths, layer_input, cotangent, w_qkv, w_out.T, w_gate_up, w_down.transpose(0, 2, 1),
        gains, w_router, expert_ids.T, cos, sin,
    )
    cot_all = cot_all.reshape(ROWS, D)
    w_att = att_full.reshape(D, AW)
    mid = mid_all.reshape(ROWS, D)
    branch_grad, _, mixed, near_sum, far_sum, _, _, state_grad, mid_gain, logit_grad = experts(
        mid, cot_all, w_exp, near_last, far_last, mask_both.reshape(ROWS, 128), w_small, state,
        cotangent, gain_rows,
    )
    input_grad, output, exp_sum, att_sum, small_sum = backward(
        branch_grad.reshape(2, SEQ, D),
        w_att,
        normed,
        proj,
        qkv,
        attended,
        mixed.reshape(2, 2, 2, BLK, D),
        near_sum,
        far_sum,
        mid_all,
        logit_grad,
        mid_gain,
        state,
        state_grad,
        layer_input,
        gain_rows,
        head_gains,
        cos,
        sin,
        live_both,
    )
    results = finish(input_grad, output, exp_sum, att_sum, small_sum)
    output, input_grad, gains_out, qkv_out, out_out, router_out, gate_up_out, down_out = results
    down_out = down_out.transpose(0, 2, 1)
    return (
        output, input_grad, gains_out, qkv_out, out_out.T, router_out, gate_up_out, down_out
    )


def solution(mesh):
    split = Mesh(mesh.devices.reshape(SIZES), AXES)
    rows, tensor = P(AXES, None), ("xh", "c")
    return jax.shard_map(
        local,
        mesh=split,
        in_specs=(
            rows,
            rows,
            P(DP),
            P(DP, None),
            P(None, AXES),
            P(None, DP, tensor),
            P(tensor, DP),
            rows,
            P(None, None, DP, tensor),
            P(None, tensor, DP),
        ),
        out_specs=(
            rows,
            rows,
            P(None, AXES),
            P(None, DP, tensor),
            P(tensor, DP),
            rows,
            P(None, None, DP, tensor),
            P(None, tensor, DP),
        ),
        check_vma=False,
    )
```
